32 devices in a mesh: dp: 2 (over y), expert: 16 (over z, x, core).
Axes of the slice: x: 2, y: 2, z: 4, core: 2. Of those that a mesh axis runs over, the one named last changes fastest.
Arguments:
- tokens: bfloat16 [2, 32, 64, 768], P(None, ('dp', 'expert')), may hold values from -6 to 6
- attn_weight: bfloat16 [768, 3072], P(None, ('dp', 'expert'))
- gain_attn: bfloat16 [768], replicated, may hold values from 0.5 to 1.5
- gain_expert: bfloat16 [768], replicated, may hold values from 0.5 to 1.5
- bias_table: bfloat16 [32, 12], replicated, may hold values from -5 to 5
- router_weight: bfloat16 [768, 16], replicated, may hold values from -0.15625 to 0.15625
- expert_in: bfloat16 [16, 768, 3072], P('expert', 'dp'), may hold values from -0.21875 to 0.21875
- expert_out: bfloat16 [16, 3072, 768], P('expert', None, 'dp'), may hold values from -2 to 2
- routes: int32 [2, 32, 64], P(None, ('dp', 'expert')), may hold values from 0 to 15, as said below
- slots: int32 [2, 32, 64], P(None, ('dp', 'expert')), may hold values from 0 to 5, as said below
- buckets: int32 [64, 64], replicated, may hold values from 0 to 31, as said below
- cotangent: bfloat16 [2, 32, 64, 768], P(None, ('dp', 'expert')), may hold values from -6 to 6
Outputs:
- output: bfloat16 [2, 32, 64, 768], P(None, ('dp', 'expert'))
- token_grad: float32 [2, 32, 64, 768], P(None, ('dp', 'expert'))
- attn_weight_grad: float32 [768, 3072], P(None, ('dp', 'expert'))
- gain_attn_grad: float32 [768], replicated
- gain_expert_grad: float32 [768], replicated
- bias_grad: float32 [32, 12], replicated
- router_grad: float32 [768, 16], replicated
- expert_in_grad: float32 [16, 768, 3072], P('expert', 'dp')
- expert_out_grad: float32 [16, 3072, 768], P('expert', None, 'dp')
The draws below stay inside these ranges and needn't reach their ends.
Inputs may be any that keep to these rules, and one draw needn't show every extreme that they name: `routes`: an expert index for each token; in each micro-batch one expert is named by at least 6 tokens of every sequence, so some of its tokens are dropped. `slots`: the number of earlier tokens of the same sequence with the same route, or 5 where that number is 5 or more (the token is dropped). buckets[a, b] depends only on b - a.
All inputs are finite; a program needn't handle non-finite values.
Results may differ from the reference program's by a relative error of at most 0.012.
The reference program's roundings to bfloat16 on the way count: a program that leaves them out, or rounds other values in their place, can miss the bound.
Values may be sent and summed in bfloat16 or wider, within the bound.
No kernel may reach another device: no remote copies, remote signals or barrier semaphores. Data moves between devices by JAX's collectives and lax.ppermute only.
A program may use at most 128 MiB of HBM per device.

```python
import math
import jax
import jax.numpy as jnp
from jax import lax

D = 768
H = 12
HD = 64
FF = 3072
NB = 32
SEQ = 64
MICRO = 2
EXPERTS = 16
SEQS = 32
CAP = 5


def route_pair(key):
    key_base, key_pick, key_order = jax.random.split(key, 3)
    base = jax.random.randint(key_base, (MICRO, SEQS, SEQ), 0, EXPERTS)
    full_expert = jax.random.randint(key_pick, (MICRO, 1, 1), 0, EXPERTS)
    order_keys = jax.random.split(key_order, MICRO * SEQS)
    order = jax.vmap(lambda one_key: jax.random.permutation(one_key, SEQ))(order_keys).reshape(MICRO, SEQS, SEQ)
    route_ids = jnp.where(order <= CAP, full_expert, base).astype(jnp.int32)
    hot = (route_ids[..., None] == jnp.arange(EXPERTS)).astype(jnp.int32)
    before = jnp.cumsum(hot, axis=2) - hot
    slot_ids = jnp.minimum(jnp.sum(before * hot, axis=-1), CAP).astype(jnp.int32)
    return (route_ids, slot_ids)


def draw_routes(key, part):
    route_ids, slot_ids = route_pair(key)
    return route_ids


def draw_slots(key, part):
    route_ids, slot_ids = route_pair(key)
    return slot_ids


def draw_buckets(key, part):
    key = jax.random.fold_in(key, 5)
    table = jax.random.randint(key, (2 * SEQ - 1,), 0, NB)
    offset = jnp.arange(SEQ)[None, :] - jnp.arange(SEQ)[:, None] + SEQ - 1
    return table[offset].astype(jnp.int32)


def draw_attn_weight(key, part):
    key = jax.random.fold_in(key, 11)
    base = jnp.clip(jax.random.normal(key, (D, 4 * D), jnp.float32), -5.0, 5.0)
    column = jnp.arange(4 * D) // D
    qk_scale = math.sqrt(1.2 / math.sqrt(HD)) / math.sqrt(D)
    scale = jnp.where(column < 2, qk_scale, jnp.where(column == 2, 1.0 / math.sqrt(D), 4.0 / math.sqrt(D)))
    return (base * scale[None, :]).astype(jnp.bfloat16)


def level_of(stream_key, dims, pieces, least, top_value):
    level = 1.0
    for axis_at, shards_of in pieces:
        heights = jax.random.uniform(jax.random.fold_in(jax.random.fold_in(stream_key, 6), axis_at), (shards_of,), jnp.float32, least / len(pieces), top_value / len(pieces))
        level = level * jnp.repeat(jnp.exp(heights), dims[axis_at] // shards_of).reshape((-1,) + (1,) * (len(dims) - 1 - axis_at))
    return level


def scatter_about(rng, shape, width, reach, cuts=(), held_as=jnp.bfloat16):
    values = jax.random.normal(rng, shape, jnp.float32) * width
    if len(cuts) > 0:
        values = level_of(rng, shape, cuts, -0.22, 0.18) * values
    return jnp.clip(values, min=-reach, max=reach).astype(held_as)


def setup_inputs(seed: int = 0) -> dict:
    keys = jax.random.split(jax.random.key(seed), 13)
    tokens = scatter_about(keys[0], (MICRO, SEQS, SEQ, D), 1.0, 6.0, ((1, 32),))
    attn_weight = draw_attn_weight(jax.random.fold_in(keys[12], 71), 0)
    gain_attn = jnp.clip(1.0 + 0.1 * jax.random.normal(keys[2], (D,), jnp.float32), 0.5, 1.5).astype(jnp.bfloat16)
    gain_expert = jnp.clip(1.0 + 0.1 * jax.random.normal(keys[3], (D,), jnp.float32), 0.5, 1.5).astype(jnp.bfloat16)
    bias_table = scatter_about(keys[4], (NB, H), 1.0, 5.0)
    router_weight = scatter_about(keys[5], (D, EXPERTS), (0.7 / (D ** 0.5)), 0.15625)
    expert_in = scatter_about(keys[6], (EXPERTS, D, FF), D ** -0.5, 0.21875, ((0, 16), (1, 2)))
    expert_out = scatter_about(keys[7], (EXPERTS, FF, D), (1.25 * EXPERTS / (FF ** 0.5)), 2.0, ((0, 16), (2, 2)))
    routes = draw_routes(jax.random.fold_in(keys[12], 71), 0)
    slots = draw_slots(jax.random.fold_in(keys[12], 71), 0)
    buckets = draw_buckets(jax.random.fold_in(keys[12], 71), 0)
    cotangent = scatter_about(keys[11], (MICRO, SEQS, SEQ, D), 1.0, 6.0, ((1, 32),))
    return {"tokens": tokens, "attn_weight": attn_weight, "gain_attn": gain_attn, "gain_expert": gain_expert, "bias_table": bias_table, "router_weight": router_weight, "expert_in": expert_in, "expert_out": expert_out, "routes": routes, "slots": slots, "buckets": buckets, "cotangent": cotangent}


EPSILON = 1e-06
HIGH = lax.Precision.HIGHEST

@jax.custom_vjp
def low(v):
    return lax.optimization_barrier(v.astype(jnp.bfloat16)).astype(jnp.float32)

@jax.custom_vjp
def low_back(v):
    return v

def low_keep(v):
    return (low(v), None)

def low_pass(kept, grad):
    return (grad,)

def back_keep(v):
    return (v, None)

def back_low(kept, grad):
    return (low(grad),)
low.defvjp(low_keep, low_pass)
low_back.defvjp(back_keep, back_low)

def smooth_gate(values):
    return jax.nn.gelu(values, approximate=True)

def rms_scale(values):
    return lax.rsqrt(lax.optimization_barrier(jnp.mean(values * values, axis=-1, keepdims=True)) + EPSILON)

def layer_forward(inputs, attn_w, gain_one, gain_two, bias_t, router_w, in_w, out_w, route_ids, slot_ids, bucket_ids):
    groups = inputs.shape[0]
    normed = low(inputs * rms_scale(inputs) * gain_one)
    project = jnp.einsum('gsd,de->gse', normed, attn_w[:, :3 * D], precision=HIGH)
    query = low(low_back(project[..., :D])).reshape(groups, SEQ, H, HD)
    key_part = low(low_back(project[..., D:2 * D])).reshape(groups, SEQ, H, HD)
    value_part = low(low_back(project[..., 2 * D:])).reshape(groups, SEQ, H, HD)
    bias_term = jnp.transpose(bias_t[bucket_ids], (2, 0, 1))
    scores = low_back(jnp.einsum('gihd,gjhd->ghij', query, key_part, precision=HIGH)) + bias_term[None]
    probs = jax.nn.softmax(scores, axis=-1)
    mixed = jnp.einsum('ghij,gjhd->gihd', low(probs), value_part, precision=HIGH).reshape(groups, SEQ, D)
    mixed = low(low_back(mixed))
    resid = inputs + low_back(jnp.einsum('gsd,de->gse', mixed, attn_w[:, 3 * D:], precision=HIGH))
    normed_two = low(resid * rms_scale(resid) * gain_two)
    logits = jnp.einsum('gsd,de->gse', normed_two, router_w, precision=HIGH)
    router_probs = jax.nn.softmax(logits, axis=-1)
    picked = (route_ids[..., None] == jnp.arange(EXPERTS)).astype(jnp.float32)
    gate = lax.optimization_barrier(jnp.sum(router_probs * picked, axis=-1))
    flat = route_ids * CAP + slot_ids
    dispatch = ((flat[..., None] == jnp.arange(EXPERTS * CAP)) & (slot_ids[..., None] < CAP)).astype(jnp.float32)
    rows = jnp.einsum('gsk,gsd->kgd', dispatch, low_back(normed_two), precision=HIGH).reshape(EXPERTS, CAP * groups, D)
    hidden_pre = low_back(jnp.einsum('erd,edf->erf', rows, in_w, precision=HIGH))
    hidden = low(smooth_gate(hidden_pre))
    made = low(low_back(jnp.einsum('erf,efd->erd', hidden, out_w, precision=HIGH)))
    returned = jnp.einsum('gsk,kgd->gsd', dispatch, made.reshape(EXPERTS * CAP, groups, D), precision=HIGH)
    return resid + gate[..., None] * returned

def reference(tokens, attn_weight, gain_attn, gain_expert, bias_table, router_weight, expert_in, expert_out, routes, slots, buckets, cotangent):
    group = math.gcd(MICRO * SEQS, max(1, 4096 // SEQ))
    count = MICRO * SEQS // group
    inputs = tokens.astype(jnp.float32).reshape(count, group, SEQ, D)
    upstream = cotangent.astype(jnp.float32).reshape(count, group, SEQ, D)
    route_blocks = routes.reshape(count, group, SEQ)
    slot_blocks = slots.reshape(count, group, SEQ)
    params = tuple((w.astype(jnp.float32) for w in (attn_weight, gain_attn, gain_expert, bias_table, router_weight, expert_in, expert_out)))

    def one_block(totals, block):
        block_in, block_up, block_routes, block_slots = block

        def forward(values, *weights):
            return layer_forward(values, *weights, block_routes, block_slots, buckets)
        result, pullback = jax.vjp(forward, block_in, *params)
        grads = pullback(block_up)
        totals = tuple((total + grad for total, grad in zip(totals, grads[1:])))
        return (totals, (result.astype(jnp.bfloat16), grads[0]))
    start = tuple((jnp.zeros_like(w) for w in params))
    totals, (outputs, input_grads) = lax.scan(one_block, start, (inputs, upstream, route_blocks, slot_blocks))
    whole = (MICRO, SEQS, SEQ, D)
    return (outputs.reshape(whole), input_grads.reshape(whole), totals[0], totals[1], totals[2], totals[3], totals[4], totals[5], totals[6])
```

```python
import jax
import jax.numpy as jnp
from jax import lax
from jax.sharding import PartitionSpec as P

EPSILON = 1e-06
HIGH = lax.Precision.HIGHEST


def smooth_gate(values):
    return jax.nn.gelu(values, approximate=True)


def rms_scale(values):
    return lax.rsqrt(jnp.mean(values * values, axis=-1, keepdims=True) + EPSILON)


def body(
    tokens,
    attn_weight,
    gain_attn,
    gain_expert,
    bias_table,
    router_weight,
    expert_in,
    expert_out,
    routes,
    slots,
    buckets,
    cotangent,
):
    micro = tokens.shape[0]
    seq_len = tokens.shape[2]
    width = tokens.shape[3]
    heads = bias_table.shape[1]
    head_size = width // heads
    bucket_count = bias_table.shape[0]
    local_experts = expert_in.shape[0]
    expert_devices = lax.axis_size("expert")
    total_experts = local_experts * expert_devices
    capacity = (5 * seq_len + 4 * total_experts - 1) // (4 * total_experts)
    slot_total = total_experts * capacity
    gain_one = gain_attn.astype(jnp.float32)
    gain_two = gain_expert.astype(jnp.float32)
    router_full = router_weight.astype(jnp.float32)
    bucket_hot = (buckets[:, :, None] == jnp.arange(bucket_count)).astype(jnp.float32)
    bias_term = jnp.einsum(
        "ijb,bh->hij", bucket_hot, bias_table.astype(jnp.float32), precision=HIGH
    )

    def to_experts(tensor):
        tensor = tensor.reshape(expert_devices, local_experts, capacity, width)
        return jnp.transpose(tensor, (1, 0, 2, 3)).reshape(
            local_experts, expert_devices * capacity, width
        )

    def from_experts(tensor):
        tensor = tensor.reshape(local_experts, expert_devices, capacity, width)
        return jnp.transpose(tensor, (1, 0, 2, 3)).reshape(total_experts, capacity, width)

    gain_one_total = jnp.zeros((width,), jnp.float32)
    gain_two_total = jnp.zeros((width,), jnp.float32)
    bias_total = jnp.zeros((bucket_count, heads), jnp.float32)
    router_total = jnp.zeros((width, total_experts), jnp.float32)
    results = []
    token_grads = []
    kept_rows = []
    kept_hidden = []
    kept_dmade = []
    kept_dpre = []
    kept_mixed = []
    kept_dattn = []
    kept_normed = []
    kept_dqkv = []
    for micro_index in range(micro):
        inputs = tokens[micro_index, 0].astype(jnp.float32)
        full_attn = lax.all_gather(attn_weight, ("dp", "expert"), axis=1, tiled=True)
        scale_one = rms_scale(inputs)
        n1hat = inputs * scale_one
        n1b = (n1hat * gain_one).astype(jnp.bfloat16)
        qkv = jnp.dot(n1b, full_attn[:, : 3 * width], preferred_element_type=jnp.float32).astype(
            jnp.bfloat16
        )
        query = qkv[:, :width].reshape(seq_len, heads, head_size)
        key_part = qkv[:, width : 2 * width].reshape(seq_len, heads, head_size)
        value_part = qkv[:, 2 * width :].reshape(seq_len, heads, head_size)
        scores = (
            jnp.einsum("ihd,jhd->hij", query, key_part, preferred_element_type=jnp.float32)
            + bias_term
        )
        log_total = jax.nn.logsumexp(scores, axis=-1, keepdims=True)
        probs_b = jnp.exp(scores - log_total).astype(jnp.bfloat16)
        mixed = jnp.einsum("hij,jhd->ihd", probs_b, value_part, preferred_element_type=jnp.float32)
        mixed_b = mixed.reshape(seq_len, width).astype(jnp.bfloat16)
        resid = inputs + jnp.dot(
            mixed_b, full_attn[:, 3 * width :], preferred_element_type=jnp.float32
        )
        scale_two = rms_scale(resid)
        n2hat = resid * scale_two
        n2b = (n2hat * gain_two).astype(jnp.bfloat16)
        logits = jnp.dot(n2b, router_weight, preferred_element_type=jnp.float32)
        router_probs = jax.nn.softmax(logits, axis=-1)
        route_ids = routes[micro_index, 0]
        slot_ids = slots[micro_index, 0]
        picked = (route_ids[:, None] == jnp.arange(total_experts)).astype(jnp.float32)
        gate = jnp.sum(router_probs * picked, axis=-1)
        flat = route_ids * capacity + slot_ids
        dispatch = (
            (flat[:, None] == jnp.arange(slot_total)) & (slot_ids[:, None] < capacity)
        ).astype(jnp.bfloat16)
        outgoing = jnp.einsum(
            "sk,sd->kd", dispatch, n2b, preferred_element_type=jnp.float32
        ).astype(jnp.bfloat16)
        arrived = lax.all_to_all(
            outgoing.reshape(total_experts, capacity, width),
            "expert",
            split_axis=0,
            concat_axis=0,
            tiled=True,
        )
        expert_rows = to_experts(arrived)
        full_in, full_out = (
            lax.all_gather(expert_in, "dp", axis=1, tiled=True),
            lax.all_gather(expert_out, "dp", axis=2, tiled=True),
        )
        hidden_pre = jnp.einsum(
            "erd,edf->erf", expert_rows, full_in, preferred_element_type=jnp.float32
        )
        hidden = smooth_gate(hidden_pre).astype(jnp.bfloat16)
        made = jnp.einsum(
            "erf,efd->erd", hidden, full_out, preferred_element_type=jnp.float32
        ).astype(jnp.bfloat16)
        kept_rows.append(expert_rows)
        kept_hidden.append(hidden)
        came_back = lax.all_to_all(
            from_experts(made), "expert", split_axis=0, concat_axis=0, tiled=True
        )
        returned = jnp.einsum(
            "sk,kd->sd",
            dispatch,
            came_back.reshape(slot_total, width),
            preferred_element_type=jnp.float32,
        )
        results.append((resid + gate[:, None] * returned).astype(jnp.bfloat16))
        upstream = cotangent[micro_index, 0].astype(jnp.float32)
        dgate = jnp.sum(upstream * returned, axis=-1)
        dreturned = (gate[:, None] * upstream).astype(jnp.bfloat16)
        dslots = jnp.einsum(
            "sk,sd->kd", dispatch, dreturned, preferred_element_type=jnp.float32
        ).astype(jnp.bfloat16)
        dmade = to_experts(
            lax.all_to_all(
                dslots.reshape(total_experts, capacity, width),
                "expert",
                split_axis=0,
                concat_axis=0,
                tiled=True,
            )
        )
        back_attn = lax.all_gather(attn_weight, ("dp", "expert"), axis=1, tiled=True)
        back_in, back_out = (
            lax.all_gather(expert_in, "dp", axis=1, tiled=True),
            lax.all_gather(expert_out, "dp", axis=2, tiled=True),
        )
        dhidden = jnp.einsum("erd,efd->erf", dmade, back_out, preferred_element_type=jnp.float32)
        dpre = jax.vjp(smooth_gate, hidden_pre)[1](dhidden)[0].astype(jnp.bfloat16)
        kept_dmade.append(dmade)
        kept_dpre.append(dpre)
        drows = jnp.einsum(
            "erf,edf->erd", dpre, back_in, preferred_element_type=jnp.float32
        ).astype(jnp.bfloat16)
        drows_home = lax.all_to_all(
            from_experts(drows), "expert", split_axis=0, concat_axis=0, tiled=True
        )
        dnormed = jnp.einsum(
            "sk,kd->sd",
            dispatch,
            drows_home.reshape(slot_total, width),
            preferred_element_type=jnp.float32,
        )
        dpick = picked * dgate[:, None]
        dlogits = router_probs * (dpick - jnp.sum(router_probs * dpick, axis=-1, keepdims=True))
        router_total = router_total + jnp.dot(n2b.astype(jnp.float32).T, dlogits, precision=HIGH)
        dnormed = dnormed + jnp.dot(dlogits, router_full.T, precision=HIGH)
        gain_two_total = gain_two_total + jnp.sum(dnormed * n2hat, axis=0)
        dhat_two = dnormed * gain_two
        dresid = upstream + scale_two * (
            dhat_two - n2hat * jnp.mean(dhat_two * n2hat, axis=-1, keepdims=True)
        )
        dattn = dresid.astype(jnp.bfloat16)
        dmixed = jnp.einsum(
            "se,de->sd", dattn, back_attn[:, 3 * width :], preferred_element_type=jnp.float32
        )
        dmixed = dmixed.astype(jnp.bfloat16).reshape(seq_len, heads, head_size)
        again_scores = (
            jnp.einsum("ihd,jhd->hij", query, key_part, preferred_element_type=jnp.float32)
            + bias_term
        )
        probs = jnp.exp(again_scores - log_total)
        again_b = probs.astype(jnp.bfloat16)
        dvalue = jnp.einsum("hij,ihd->jhd", again_b, dmixed, preferred_element_type=jnp.float32)
        dprobs = jnp.einsum("ihd,jhd->hij", dmixed, value_part, preferred_element_type=jnp.float32)
        dscores = probs * (dprobs - jnp.sum(probs * dprobs, axis=-1, keepdims=True))
        bias_total = bias_total + jnp.einsum("hij,ijb->bh", dscores, bucket_hot, precision=HIGH)
        dscores_b = dscores.astype(jnp.bfloat16)
        dquery = jnp.einsum("hij,jhd->ihd", dscores_b, key_part, preferred_element_type=jnp.float32)
        dkey = jnp.einsum("hij,ihd->jhd", dscores_b, query, preferred_element_type=jnp.float32)
        dqkv = jnp.concatenate(
            [
                dquery.reshape(seq_len, width),
                dkey.reshape(seq_len, width),
                dvalue.reshape(seq_len, width),
            ],
            axis=1,
        ).astype(jnp.bfloat16)
        kept_mixed.append(mixed_b)
        kept_dattn.append(dattn)
        kept_normed.append(n1b)
        kept_dqkv.append(dqkv)
        dnormed_one = jnp.einsum(
            "se,de->sd", dqkv, back_attn[:, : 3 * width], preferred_element_type=jnp.float32
        )
        gain_one_total = gain_one_total + jnp.sum(dnormed_one * n1hat, axis=0)
        dhat_one = dnormed_one * gain_one
        token_grads.append(
            dresid
            + scale_one * (dhat_one - n1hat * jnp.mean(dhat_one * n1hat, axis=-1, keepdims=True))
        )
    normed_all = jnp.concatenate(kept_normed, axis=0)
    dqkv_all = jnp.concatenate(kept_dqkv, axis=0)
    mixed_all = jnp.concatenate(kept_mixed, axis=0)
    dattn_all = jnp.concatenate(kept_dattn, axis=0)
    dqkv_proj = jnp.einsum("sd,se->de", normed_all, dqkv_all, preferred_element_type=jnp.float32)
    dout_proj = jnp.einsum("sd,se->de", mixed_all, dattn_all, preferred_element_type=jnp.float32)
    attn_total = jnp.concatenate([dqkv_proj, dout_proj], axis=1)
    attn_share = lax.psum_scatter(attn_total, ("dp", "expert"), scatter_dimension=1, tiled=True)
    rows_all = jnp.concatenate(kept_rows, axis=1)
    hidden_all = jnp.concatenate(kept_hidden, axis=1)
    dmade_cat = jnp.concatenate(kept_dmade, axis=1)
    dpre_all = jnp.concatenate(kept_dpre, axis=1)
    in_total = jnp.einsum("erd,erf->edf", rows_all, dpre_all, preferred_element_type=jnp.float32)
    out_turned_total = jnp.einsum(
        "erd,erf->edf", dmade_cat, hidden_all, preferred_element_type=jnp.float32
    )
    in_share, out_turned_share = (
        lax.psum_scatter(
            in_total.astype(jnp.bfloat16), "dp", scatter_dimension=1, tiled=True
        ).astype(jnp.float32),
        lax.psum_scatter(
            out_turned_total.astype(jnp.bfloat16), "dp", scatter_dimension=1, tiled=True
        ).astype(jnp.float32),
    )
    out_share = jnp.transpose(out_turned_share, (0, 2, 1))
    gain_one_sum, gain_two_sum, bias_sum, router_sum = lax.psum(
        (gain_one_total, gain_two_total, bias_total, router_total), ("dp", "expert")
    )
    output = jnp.stack(results)[:, None]
    token_grad = jnp.stack(token_grads)[:, None]
    return (
        output,
        token_grad,
        attn_share,
        gain_one_sum,
        gain_two_sum,
        bias_sum,
        router_sum,
        in_share,
        out_share,
    )


BOTH = ("dp", "expert")


def flip(tensor, bit):
    if bit == "y":
        return lax.ppermute(tensor, "dp", [(0, 1), (1, 0)])
    count = lax.axis_size("expert")
    return lax.ppermute(tensor, "expert", [(i, i ^ bit) for i in range(count)])


def own_bit(bit):
    if bit == "y":
        return lax.axis_index("dp")
    return (lax.axis_index("expert") // bit) % 2


ORDERS = ((8, 4, "y", 2), (2, 8, 4, "y"), ("y", 2, 8, 4))
RS_ORDERS = ((2, "y", 8, 4), ("y", 8, 4, 2), (8, 4, 2, "y"))
PLACE = {"y": 0, 8: 1, 4: 2, 2: 3, 1: 4}


def gather_rows(shard):
    rows, width = shard.shape
    third = width // 3
    pieces = [
        shard[:, i * third : (i + 1) * third].reshape(1, 1, 1, 1, 1, rows, third) for i in range(3)
    ]

    def grow(piece, bit):
        got = flip(piece, bit)
        low = own_bit(bit) == 0
        return jnp.concatenate(
            [jnp.where(low, piece, got), jnp.where(low, got, piece)], axis=PLACE[bit]
        )

    for step in range(5):
        pieces = [
            grow(piece, (ORDERS[i] + (1,))[step]) for i, piece in enumerate(pieces)
        ]
    return jnp.concatenate(pieces, axis=-1).reshape(32 * rows, width)


def reduce_step(total, bit):
    mine = own_bit(bit)
    axis = PLACE[bit]
    send = lax.dynamic_index_in_dim(total, 1 - mine, axis, keepdims=True).astype(jnp.bfloat16)
    keep = lax.dynamic_index_in_dim(total, mine, axis, keepdims=True)
    return keep + flip(send, bit).astype(jnp.float32)


def scatter_rows(total):
    third = total.shape[-1] // 3
    pieces = [total[..., i * third : (i + 1) * third] for i in range(3)]
    for step in range(4):
        pieces = [reduce_step(piece, RS_ORDERS[i][step]) for i, piece in enumerate(pieces)]
    whole = jnp.concatenate(pieces, axis=-1)
    return whole.reshape(whole.shape[-2], whole.shape[-1])


def sum_all(tensor):
    for bit in (1, 2, "y", 4, 8):
        tensor = tensor + flip(tensor, bit)
    return tensor


def dot(left, right, dims, **more):
    return lax.dot_general(
        left, right, (dims, ((), ())), preferred_element_type=jnp.float32, **more
    )


def paired_body(
    tokens,
    attn_weight,
    gain_attn,
    gain_expert,
    bias_table,
    router_weight,
    expert_in,
    expert_out,
    routes,
    slots,
    buckets,
    cotangent,
):
    f32, bf16 = jnp.float32, jnp.bfloat16
    micro, _, seq_len, width = tokens.shape
    count = micro * seq_len
    heads = bias_table.shape[1]
    head_size = width // heads
    bucket_count = bias_table.shape[0]
    experts = lax.axis_size("expert")
    capacity = (5 * seq_len + 4 * experts - 1) // (4 * experts)
    places = micro * capacity
    hidden_half = expert_in.shape[2] // 2
    width_half = width // 2
    dp_at, expert_at = lax.axis_index("dp"), lax.axis_index("expert")
    core = expert_at % 2
    home = core == dp_at
    host = expert_at - core + dp_at
    gain_one, gain_two = gain_attn.astype(f32), gain_expert.astype(f32)

    away = [
        (dp * experts + e, (1 - dp) * experts + (e ^ 1))
        for dp in range(2)
        for e in range(experts)
        if e % 2 != dp
    ]
    groups = [
        [dp * experts + 2 * pair + side for dp in range(2) for pair in range(experts // 2)]
        for side in range(2)
    ]

    def to_chips(tensor):
        return lax.all_to_all(
            tensor, BOTH, split_axis=0, concat_axis=0, tiled=True, axis_index_groups=groups
        )

    wt = gather_rows(attn_weight.T)

    route_ids, slot_ids = routes[:, 0], slots[:, 0]
    chip = (route_ids % 2) * (experts // 2) + route_ids // 2
    flat = chip * places + jnp.arange(micro)[:, None] * capacity + slot_ids
    dispatch = (
        (flat[..., None] == jnp.arange(experts * places)) & (slot_ids[..., None] < capacity)
    ).astype(bf16).reshape(count, experts * places)
    upstream_b = cotangent.reshape(count, width)
    upstream = upstream_b.astype(f32)
    dy_rows = to_chips(dot(dispatch, upstream_b, ((0,), (0,))).astype(bf16))
    dy_rows = jnp.concatenate([dy_rows, flip(dy_rows, 1)], axis=0)

    def settle(local):
        return jnp.where(home, local, lax.ppermute(local, BOTH, away))

    in_rows = settle(expert_in[0])
    out_columns = settle(expert_out[0])
    in_keep = lax.dynamic_slice_in_dim(in_rows, core * hidden_half, hidden_half, 1)
    in_got = flip(lax.dynamic_slice_in_dim(in_rows, (1 - core) * hidden_half, hidden_half, 1), 1)
    out_keep = lax.dynamic_slice_in_dim(out_columns, core * hidden_half, hidden_half, 0)
    out_got = flip(
        lax.dynamic_slice_in_dim(out_columns, (1 - core) * hidden_half, hidden_half, 0), 1
    )

    def halves(tensor):
        return (
            lax.dynamic_slice_in_dim(tensor, core * width_half, width_half, 1),
            lax.dynamic_slice_in_dim(tensor, (1 - core) * width_half, width_half, 1),
        )

    def whole(keep, got, axis):
        low = core == 0
        return jnp.concatenate(
            [jnp.where(low, keep, got), jnp.where(low, got, keep)], axis=axis
        )

    bucket_hot = (buckets[:, :, None] == jnp.arange(bucket_count)).astype(f32)
    bias_term = jnp.einsum("ijb,bh->hij", bucket_hot, bias_table.astype(f32), precision=HIGH)

    inputs = tokens.reshape(count, width).astype(f32)
    scale_one = rms_scale(inputs)
    n1hat = inputs * scale_one
    n1b = (n1hat * gain_one).astype(bf16)
    qkv = dot(n1b, wt[: 3 * width], ((1,), (1,))).astype(bf16)
    qkv = qkv.reshape(micro, seq_len, 3, heads, head_size)
    query, key_part, value_part = qkv[:, :, 0], qkv[:, :, 1], qkv[:, :, 2]
    scores = (
        jnp.einsum("mihd,mjhd->mhij", query, key_part, preferred_element_type=f32) + bias_term
    )
    probs = jax.nn.softmax(scores, axis=-1)
    probs_b = probs.astype(bf16)
    mixed_b = (
        jnp.einsum("mhij,mjhd->mihd", probs_b, value_part, preferred_element_type=f32)
        .reshape(count, width)
        .astype(bf16)
    )
    resid = inputs + dot(mixed_b, wt[3 * width :], ((1,), (1,)))
    scale_two = rms_scale(resid)
    n2hat = resid * scale_two
    n2b = (n2hat * gain_two).astype(bf16)

    own_rows = to_chips(dot(dispatch, n2b, ((0,), (0,))).astype(bf16))
    rows = jnp.concatenate([own_rows, flip(own_rows, 1)], axis=0)
    row_count = own_rows.shape[0]

    row_probs = jax.nn.softmax(dot(rows, router_weight, ((1,), (0,))), axis=-1)
    chosen = (jnp.arange(experts) == host).astype(f32)
    row_gate = jnp.sum(row_probs * chosen, axis=-1, keepdims=True)
    dmade = (row_gate * dy_rows.astype(f32)).astype(bf16)

    rows_keep, rows_got = halves(rows)
    dmade_keep, dmade_got = halves(dmade)
    upre = dot(rows_keep, in_keep, ((1,), (0,))) + dot(rows_got, in_got, ((1,), (0,)))
    hidden = smooth_gate(upre).astype(bf16)
    dhidden = dot(dmade_keep, out_keep, ((1,), (1,))) + dot(dmade_got, out_got, ((1,), (1,)))
    du = jax.vjp(smooth_gate, upre)[1](dhidden)[0].astype(bf16)
    made_part = whole(
        dot(hidden, out_keep, ((1,), (0,))), dot(hidden, out_got, ((1,), (0,))), 1
    )
    drows_part = whole(dot(du, in_keep, ((1,), (1,))), dot(du, in_got, ((1,), (1,))), 1)
    parts = jnp.stack([made_part, drows_part])
    parts = parts[:, :row_count] + flip(parts[:, row_count:], 1)
    made = parts[0].astype(bf16)
    drows = parts[1].astype(bf16)
    dgate = jnp.sum(dy_rows[:row_count].astype(f32) * made.astype(f32), axis=-1, keepdims=True)
    dlogits = row_probs[:row_count] * dgate * (chosen - row_gate[:row_count])
    router_part = dot(own_rows.astype(f32), dlogits, ((0,), (0,)), precision=HIGH)
    dn2_rows = drows.astype(f32) + dot(
        dlogits, router_weight.astype(f32), ((1,), (1,)), precision=HIGH
    )
    dn2_home = to_chips(dn2_rows.astype(bf16))
    made_home = to_chips(made)

    in_mine = dot(rows_keep, du, ((0,), (0,)))
    in_other = flip(dot(rows_got, du, ((0,), (0,))).astype(bf16), 1).astype(f32)
    out_mine = dot(hidden, dmade_keep, ((0,), (0,)))
    out_other = flip(dot(hidden, dmade_got, ((0,), (0,))).astype(bf16), 1).astype(f32)
    in_total = whole(in_mine, in_other, 1)
    out_total = whole(out_mine, out_other, 0)
    in_share = jnp.where(
        home, in_total, lax.ppermute(in_total.astype(bf16), BOTH, away).astype(f32)
    )
    out_share = jnp.where(
        home, out_total, lax.ppermute(out_total.astype(bf16), BOTH, away).astype(f32)
    )

    dn2 = dot(dispatch, dn2_home, ((1,), (0,)))
    gain_two_part = jnp.sum(dn2 * n2hat, axis=0)
    dhat_two = dn2 * gain_two
    dresid = upstream + scale_two * (
        dhat_two - n2hat * jnp.mean(dhat_two * n2hat, axis=-1, keepdims=True)
    )
    dattn = dresid.astype(bf16)
    dmixed = dot(dattn, wt[3 * width :], ((1,), (0,))).astype(bf16)
    dmixed = dmixed.reshape(micro, seq_len, heads, head_size)
    dvalue = jnp.einsum("mhij,mihd->mjhd", probs_b, dmixed, preferred_element_type=f32)
    dprobs = jnp.einsum("mihd,mjhd->mhij", dmixed, value_part, preferred_element_type=f32)
    dscores = probs * (dprobs - jnp.sum(probs * dprobs, axis=-1, keepdims=True))
    bias_part = jnp.einsum("hij,ijb->bh", jnp.sum(dscores, axis=0), bucket_hot, precision=HIGH)
    dscores_b = dscores.astype(bf16)
    dquery = jnp.einsum("mhij,mjhd->mihd", dscores_b, key_part, preferred_element_type=f32)
    dkey = jnp.einsum("mhij,mihd->mjhd", dscores_b, query, preferred_element_type=f32)
    dqkv = jnp.concatenate(
        [part.reshape(count, width).astype(bf16) for part in (dquery, dkey, dvalue)], axis=1
    )

    def core_step(gradient, values):
        block = width * 4 // 32
        columns = gradient.T.reshape(-1, 2, block, count)

        def product(side):
            picked = lax.dynamic_index_in_dim(columns, side, 1, keepdims=False)
            return dot(picked.reshape(-1, count), values, ((1,), (0,)))

        got = flip(product(1 - core).astype(bf16), 1)
        return product(core) + got.astype(f32)

    o_total = core_step(dattn, mixed_b)
    qkv_total = core_step(dqkv, n1b)
    total = jnp.concatenate([qkv_total, o_total], axis=0)
    attn_share = scatter_rows(total.reshape(2, 2, 2, 2, 1, -1, width)).T

    dn1 = dot(dqkv, wt[: 3 * width], ((1,), (0,)))
    gain_one_part = jnp.sum(dn1 * n1hat, axis=0)
    dhat_one = dn1 * gain_one
    token_grad = dresid + scale_one * (
        dhat_one - n1hat * jnp.mean(dhat_one * n1hat, axis=-1, keepdims=True)
    )

    router_probs = jax.nn.softmax(dot(n2b, router_weight, ((1,), (0,))), axis=-1)
    picked = (route_ids.reshape(count, 1) == jnp.arange(experts)).astype(f32)
    gate = jnp.sum(router_probs * picked, axis=-1, keepdims=True)
    returned = dot(dispatch, made_home, ((1,), (0,)))
    output = (resid + gate * returned).astype(bf16)

    early = sum_all(
        jnp.concatenate([gain_two_part[None], router_part.T], axis=0)
    )
    late = sum_all(
        jnp.concatenate([gain_one_part, bias_part.reshape(-1)]).reshape(1, -1)
    )[0]
    return (
        output.reshape(tokens.shape),
        token_grad.reshape(tokens.shape),
        attn_share,
        late[:width],
        early[0],
        late[width:].reshape(bucket_count, heads),
        early[1:].T,
        in_share[None],
        out_share[None],
    )


def solution(mesh):
    paired = mesh.shape["dp"] == 2 and mesh.shape["expert"] == 16
    chosen = paired_body if paired else body
    placed = (
        P(None, ("dp", "expert"), None, None),
        P(None, ("dp", "expert")),
        P(),
        P(),
        P(),
        P(),
        P("expert", "dp", None),
        P("expert", None, "dp"),
        P(None, ("dp", "expert"), None),
        P(None, ("dp", "expert"), None),
        P(),
        P(None, ("dp", "expert"), None, None),
    )
    return jax.shard_map(
        chosen,
        mesh=mesh,
        in_specs=placed,
        out_specs=(
            P(None, ("dp", "expert"), None, None),
            P(None, ("dp", "expert"), None, None),
            P(None, ("dp", "expert")),
            P(),
            P(),
            P(),
            P(),
            P("expert", "dp", None),
            P("expert", None, "dp"),
        ),
        check_vma=False,
    )
```

```python
import functools
import jax
import jax.numpy as jnp
from jax import lax
from jax.experimental import pallas as pl
from jax.experimental.pallas import tpu as pltpu
from jax.sharding import PartitionSpec as P

EPSILON = 1e-06
HIGH = lax.Precision.HIGHEST


def smooth_gate(values):
    return jax.nn.gelu(values, approximate=True)


def rms_scale(values):
    return lax.rsqrt(jnp.mean(values * values, axis=-1, keepdims=True) + EPSILON)


def body(
    tokens,
    attn_weight,
    gain_attn,
    gain_expert,
    bias_table,
    router_weight,
    expert_in,
    expert_out,
    routes,
    slots,
    buckets,
    cotangent,
):
    micro = tokens.shape[0]
    seq_len = tokens.shape[2]
    width = tokens.shape[3]
    heads = bias_table.shape[1]
    head_size = width // heads
    bucket_count = bias_table.shape[0]
    local_experts = expert_in.shape[0]
    expert_devices = lax.axis_size("expert")
    total_experts = local_experts * expert_devices
    capacity = (5 * seq_len + 4 * total_experts - 1) // (4 * total_experts)
    slot_total = total_experts * capacity
    gain_one = gain_attn.astype(jnp.float32)
    gain_two = gain_expert.astype(jnp.float32)
    router_full = router_weight.astype(jnp.float32)
    bucket_hot = (buckets[:, :, None] == jnp.arange(bucket_count)).astype(jnp.float32)
    bias_term = jnp.einsum(
        "ijb,bh->hij", bucket_hot, bias_table.astype(jnp.float32), precision=HIGH
    )

    def to_experts(tensor):
        tensor = tensor.reshape(expert_devices, local_experts, capacity, width)
        return jnp.transpose(tensor, (1, 0, 2, 3)).reshape(
            local_experts, expert_devices * capacity, width
        )

    def from_experts(tensor):
        tensor = tensor.reshape(local_experts, expert_devices, capacity, width)
        return jnp.transpose(tensor, (1, 0, 2, 3)).reshape(total_experts, capacity, width)

    gain_one_total = jnp.zeros((width,), jnp.float32)
    gain_two_total = jnp.zeros((width,), jnp.float32)
    bias_total = jnp.zeros((bucket_count, heads), jnp.float32)
    router_total = jnp.zeros((width, total_experts), jnp.float32)
    results = []
    token_grads = []
    kept_rows = []
    kept_hidden = []
    kept_dmade = []
    kept_dpre = []
    kept_mixed = []
    kept_dattn = []
    kept_normed = []
    kept_dqkv = []
    for micro_index in range(micro):
        inputs = tokens[micro_index, 0].astype(jnp.float32)
        full_attn = lax.all_gather(attn_weight, ("dp", "expert"), axis=1, tiled=True)
        scale_one = rms_scale(inputs)
        n1hat = inputs * scale_one
        n1b = (n1hat * gain_one).astype(jnp.bfloat16)
        qkv = jnp.dot(n1b, full_attn[:, : 3 * width], preferred_element_type=jnp.float32).astype(
            jnp.bfloat16
        )
        query = qkv[:, :width].reshape(seq_len, heads, head_size)
        key_part = qkv[:, width : 2 * width].reshape(seq_len, heads, head_size)
        value_part = qkv[:, 2 * width :].reshape(seq_len, heads, head_size)
        scores = (
            jnp.einsum("ihd,jhd->hij", query, key_part, preferred_element_type=jnp.float32)
            + bias_term
        )
        log_total = jax.nn.logsumexp(scores, axis=-1, keepdims=True)
        probs_b = jnp.exp(scores - log_total).astype(jnp.bfloat16)
        mixed = jnp.einsum("hij,jhd->ihd", probs_b, value_part, preferred_element_type=jnp.float32)
        mixed_b = mixed.reshape(seq_len, width).astype(jnp.bfloat16)
        resid = inputs + jnp.dot(
            mixed_b, full_attn[:, 3 * width :], preferred_element_type=jnp.float32
        )
        scale_two = rms_scale(resid)
        n2hat = resid * scale_two
        n2b = (n2hat * gain_two).astype(jnp.bfloat16)
        logits = jnp.dot(n2b, router_weight, preferred_element_type=jnp.float32)
        router_probs = jax.nn.softmax(logits, axis=-1)
        route_ids = routes[micro_index, 0]
        slot_ids = slots[micro_index, 0]
        picked = (route_ids[:, None] == jnp.arange(total_experts)).astype(jnp.float32)
        gate = jnp.sum(router_probs * picked, axis=-1)
        flat = route_ids * capacity + slot_ids
        dispatch = (
            (flat[:, None] == jnp.arange(slot_total)) & (slot_ids[:, None] < capacity)
        ).astype(jnp.bfloat16)
        outgoing = jnp.einsum(
            "sk,sd->kd", dispatch, n2b, preferred_element_type=jnp.float32
        ).astype(jnp.bfloat16)
        arrived = lax.all_to_all(
            outgoing.reshape(total_experts, capacity, width),
            "expert",
            split_axis=0,
            concat_axis=0,
            tiled=True,
        )
        expert_rows = to_experts(arrived)
        full_in, full_out = (
            lax.all_gather(expert_in, "dp", axis=1, tiled=True),
            lax.all_gather(expert_out, "dp", axis=2, tiled=True),
        )
        hidden_pre = jnp.einsum(
            "erd,edf->erf", expert_rows, full_in, preferred_element_type=jnp.float32
        )
        hidden = smooth_gate(hidden_pre).astype(jnp.bfloat16)
        made = jnp.einsum(
            "erf,efd->erd", hidden, full_out, preferred_element_type=jnp.float32
        ).astype(jnp.bfloat16)
        kept_rows.append(expert_rows)
        kept_hidden.append(hidden)
        came_back = lax.all_to_all(
            from_experts(made), "expert", split_axis=0, concat_axis=0, tiled=True
        )
        returned = jnp.einsum(
            "sk,kd->sd",
            dispatch,
            came_back.reshape(slot_total, width),
            preferred_element_type=jnp.float32,
        )
        results.append((resid + gate[:, None] * returned).astype(jnp.bfloat16))
        upstream = cotangent[micro_index, 0].astype(jnp.float32)
        dgate = jnp.sum(upstream * returned, axis=-1)
        dreturned = (gate[:, None] * upstream).astype(jnp.bfloat16)
        dslots = jnp.einsum(
            "sk,sd->kd", dispatch, dreturned, preferred_element_type=jnp.float32
        ).astype(jnp.bfloat16)
        dmade = to_experts(
            lax.all_to_all(
                dslots.reshape(total_experts, capacity, width),
                "expert",
                split_axis=0,
                concat_axis=0,
                tiled=True,
            )
        )
        back_attn = lax.all_gather(attn_weight, ("dp", "expert"), axis=1, tiled=True)
        back_in, back_out = (
            lax.all_gather(expert_in, "dp", axis=1, tiled=True),
            lax.all_gather(expert_out, "dp", axis=2, tiled=True),
        )
        dhidden = jnp.einsum("erd,efd->erf", dmade, back_out, preferred_element_type=jnp.float32)
        dpre = jax.vjp(smooth_gate, hidden_pre)[1](dhidden)[0].astype(jnp.bfloat16)
        kept_dmade.append(dmade)
        kept_dpre.append(dpre)
        drows = jnp.einsum(
            "erf,edf->erd", dpre, back_in, preferred_element_type=jnp.float32
        ).astype(jnp.bfloat16)
        drows_home = lax.all_to_all(
            from_experts(drows), "expert", split_axis=0, concat_axis=0, tiled=True
        )
        dnormed = jnp.einsum(
            "sk,kd->sd",
            dispatch,
            drows_home.reshape(slot_total, width),
            preferred_element_type=jnp.float32,
        )
        dpick = picked * dgate[:, None]
        dlogits = router_probs * (dpick - jnp.sum(router_probs * dpick, axis=-1, keepdims=True))
        router_total = router_total + jnp.dot(n2b.astype(jnp.float32).T, dlogits, precision=HIGH)
        dnormed = dnormed + jnp.dot(dlogits, router_full.T, precision=HIGH)
        gain_two_total = gain_two_total + jnp.sum(dnormed * n2hat, axis=0)
        dhat_two = dnormed * gain_two
        dresid = upstream + scale_two * (
            dhat_two - n2hat * jnp.mean(dhat_two * n2hat, axis=-1, keepdims=True)
        )
        dattn = dresid.astype(jnp.bfloat16)
        dmixed = jnp.einsum(
            "se,de->sd", dattn, back_attn[:, 3 * width :], preferred_element_type=jnp.float32
        )
        dmixed = dmixed.astype(jnp.bfloat16).reshape(seq_len, heads, head_size)
        again_scores = (
            jnp.einsum("ihd,jhd->hij", query, key_part, preferred_element_type=jnp.float32)
            + bias_term
        )
        probs = jnp.exp(again_scores - log_total)
        again_b = probs.astype(jnp.bfloat16)
        dvalue = jnp.einsum("hij,ihd->jhd", again_b, dmixed, preferred_element_type=jnp.float32)
        dprobs = jnp.einsum("ihd,jhd->hij", dmixed, value_part, preferred_element_type=jnp.float32)
        dscores = probs * (dprobs - jnp.sum(probs * dprobs, axis=-1, keepdims=True))
        bias_total = bias_total + jnp.einsum("hij,ijb->bh", dscores, bucket_hot, precision=HIGH)
        dscores_b = dscores.astype(jnp.bfloat16)
        dquery = jnp.einsum("hij,jhd->ihd", dscores_b, key_part, preferred_element_type=jnp.float32)
        dkey = jnp.einsum("hij,ihd->jhd", dscores_b, query, preferred_element_type=jnp.float32)
        dqkv = jnp.concatenate(
            [
                dquery.reshape(seq_len, width),
                dkey.reshape(seq_len, width),
                dvalue.reshape(seq_len, width),
            ],
            axis=1,
        ).astype(jnp.bfloat16)
        kept_mixed.append(mixed_b)
        kept_dattn.append(dattn)
        kept_normed.append(n1b)
        kept_dqkv.append(dqkv)
        dnormed_one = jnp.einsum(
            "se,de->sd", dqkv, back_attn[:, : 3 * width], preferred_element_type=jnp.float32
        )
        gain_one_total = gain_one_total + jnp.sum(dnormed_one * n1hat, axis=0)
        dhat_one = dnormed_one * gain_one
        token_grads.append(
            dresid
            + scale_one * (dhat_one - n1hat * jnp.mean(dhat_one * n1hat, axis=-1, keepdims=True))
        )
    normed_all = jnp.concatenate(kept_normed, axis=0)
    dqkv_all = jnp.concatenate(kept_dqkv, axis=0)
    mixed_all = jnp.concatenate(kept_mixed, axis=0)
    dattn_all = jnp.concatenate(kept_dattn, axis=0)
    dqkv_proj = jnp.einsum("sd,se->de", normed_all, dqkv_all, preferred_element_type=jnp.float32)
    dout_proj = jnp.einsum("sd,se->de", mixed_all, dattn_all, preferred_element_type=jnp.float32)
    attn_total = jnp.concatenate([dqkv_proj, dout_proj], axis=1)
    attn_share = lax.psum_scatter(attn_total, ("dp", "expert"), scatter_dimension=1, tiled=True)
    rows_all = jnp.concatenate(kept_rows, axis=1)
    hidden_all = jnp.concatenate(kept_hidden, axis=1)
    dmade_cat = jnp.concatenate(kept_dmade, axis=1)
    dpre_all = jnp.concatenate(kept_dpre, axis=1)
    in_total = jnp.einsum("erd,erf->edf", rows_all, dpre_all, preferred_element_type=jnp.float32)
    out_turned_total = jnp.einsum(
        "erd,erf->edf", dmade_cat, hidden_all, preferred_element_type=jnp.float32
    )
    in_share, out_turned_share = (
        lax.psum_scatter(
            in_total.astype(jnp.bfloat16), "dp", scatter_dimension=1, tiled=True
        ).astype(jnp.float32),
        lax.psum_scatter(
            out_turned_total.astype(jnp.bfloat16), "dp", scatter_dimension=1, tiled=True
        ).astype(jnp.float32),
    )
    out_share = jnp.transpose(out_turned_share, (0, 2, 1))
    gain_one_sum, gain_two_sum, bias_sum, router_sum = lax.psum(
        (gain_one_total, gain_two_total, bias_total, router_total), ("dp", "expert")
    )
    output = jnp.stack(results)[:, None]
    token_grad = jnp.stack(token_grads)[:, None]
    return (
        output,
        token_grad,
        attn_share,
        gain_one_sum,
        gain_two_sum,
        bias_sum,
        router_sum,
        in_share,
        out_share,
    )


BOTH = ("dp", "expert")


def flip(tensor, bit):
    if bit == "y":
        return lax.ppermute(tensor, "dp", [(0, 1), (1, 0)])
    count = lax.axis_size("expert")
    return lax.ppermute(tensor, "expert", [(i, i ^ bit) for i in range(count)])


def own_bit(bit):
    if bit == "y":
        return lax.axis_index("dp")
    return (lax.axis_index("expert") // bit) % 2


ORDERS = ((8, 4, "y", 2), (2, 8, 4, "y"), ("y", 2, 8, 4))
RS_ORDERS = ((2, "y", 8, 4), ("y", 8, 4, 2), (8, 4, 2, "y"))
PLACE = {"y": 0, 8: 1, 4: 2, 2: 3, 1: 4}


def gather_rows(shard, soon, later, prepare, waiting):
    rows, width = shard.shape
    third = width // 3
    pieces = [
        shard[:, i * third : (i + 1) * third].reshape(1, 1, 1, 1, rows, third) for i in range(3)
    ]

    def grow(piece, bit):
        got = flip(piece, bit)
        low = own_bit(bit) == 0
        return jnp.concatenate(
            [jnp.where(low, piece, got), jnp.where(low, got, piece)], axis=PLACE[bit]
        )

    for step in range(4):
        if step == 1:
            pieces, waiting = lax.optimization_barrier((pieces, waiting))
            ready = prepare(*waiting)
        if step == 2:
            pieces, soon = lax.optimization_barrier((pieces, soon))
        pieces = [grow(piece, ORDERS[i][step]) for i, piece in enumerate(pieces)]
    pieces, later, ready = lax.optimization_barrier((pieces, later, ready))
    pieces = [piece.reshape(-1, rows, third) for piece in pieces]
    return pieces + [flip(piece, 1) for piece in pieces], soon, later, ready


def reduce_step(total, bit):
    mine = own_bit(bit)
    axis = PLACE[bit]
    send = lax.dynamic_index_in_dim(total, 1 - mine, axis, keepdims=True).astype(jnp.bfloat16)
    keep = lax.dynamic_index_in_dim(total, mine, axis, keepdims=True)
    return keep + flip(send, bit).astype(jnp.float32)


def scatter_rows(leaves, stays, small, late):
    late = list(late)
    pieces = []
    for index, (leave, stay) in enumerate(zip(leaves, stays)):
        bit = RS_ORDERS[index][0]
        shape = [2, 2, 2, 2, 1] + list(stay.shape[1:])
        shape[PLACE[bit]] = 1
        pieces.append((stay + flip(leave, bit).astype(jnp.float32)).reshape(shape))
    for bit in (1, 2):
        small = small + flip(small, bit)
    for step in range(1, 4):
        pieces, late[step], small = lax.optimization_barrier((pieces, late[step], small))
        pieces = [reduce_step(piece, RS_ORDERS[i][step]) for i, piece in enumerate(pieces)]
        small = small + flip(small, ("y", 8, 4)[step - 1])
    whole = jnp.concatenate(pieces, axis=-1)
    return whole.reshape(whole.shape[-2], whole.shape[-1]), small, late


def dot(left, right, dims, **more):
    return lax.dot_general(
        left, right, (dims, ((), ())), preferred_element_type=jnp.float32, **more
    )


def call(kernel, mib, outs, scratch, *operands, plain_in=(), plain_out=()):
    def spec(shape):
        return pl.BlockSpec(
            shape, lambda i: (0,) * len(shape), pipeline_mode=pl.Buffered(1)
        )

    left = pl.BlockSpec(memory_space=pl.ANY)
    operands = operands[:1] + tuple(
        pltpu.with_memory_space_constraint(operand, pltpu.HBM) for operand in operands[1:]
    )
    return pl.pallas_call(
        kernel,
        grid=(1,),
        out_shape=tuple(pltpu.HBM(*out) for out in outs),
        in_specs=[pl.BlockSpec(memory_space=pltpu.SMEM)]
        + [left if i in plain_in else spec(operand.shape) for i, operand in enumerate(operands) if i],
        out_specs=tuple(left if i in plain_out else spec(out[0]) for i, out in enumerate(outs)),
        scratch_shapes=scratch,
        compiler_params=pltpu.CompilerParams(vmem_limit_bytes=mib * 2**20),
    )(*operands)


def bias_kernel(table_ref, buckets_ref, square_ref):
    heads, count, _ = square_ref.shape
    row = lax.broadcasted_iota(jnp.int32, (count, count), 0)
    column = lax.broadcasted_iota(jnp.int32, (count, count), 1)
    half = count // 2
    same = (row < half) == (column < half)
    buckets = buckets_ref[...]
    for head in range(heads):
        total = jnp.where(same, 0.0, -jnp.inf)
        for bucket in range(table_ref.shape[0]):
            total = jnp.where(same & (buckets == bucket), table_ref[bucket, head], total)
        square_ref[head] = total


def attend_kernel(
    place_ref, x_ref, *rest,
):
    pieces, rest = rest[:6], rest[6:]
    (
        gain_one_ref, gain_two_ref, bias_ref, dispatch_ref, dy_ref,
        wt_qkv_ref, wt_o_ref, n1b_ref, qkv_ref, probs_ref, mixed_ref, resid_ref, n2b_ref, rows_ref,
        mixed_t, wt_ref, come, go_qkv, go_o,
    ) = rest
    core = place_ref[0]
    pairs, block, third = pieces[0].shape
    for side, part in ((core, pieces[:3]), (1 - core, pieces[3:])):
        for index in range(3):
            pltpu.make_async_copy(
                part[index], wt_ref.at[:, side, :, pl.ds(index * third, third)], come
            ).start()
    heads = probs_ref.shape[0]
    width = x_ref.shape[1]
    size = width // heads
    x = x_ref[...].astype(jnp.float32)
    n1b_ref[...] = (x * rms_scale(x) * gain_one_ref[...]).astype(jnp.bfloat16)
    pltpu.make_async_copy(wt_ref, wt_ref, come).wait()
    most = pairs * 3 // 4
    leave_qkv = pltpu.make_async_copy(wt_ref.at[pl.ds(0, most)], wt_qkv_ref, go_qkv)
    leave_o = pltpu.make_async_copy(wt_ref.at[pl.ds(most, pairs - most)], wt_o_ref, go_o)
    leave_qkv.start()
    leave_o.start()
    qkv_ref[...] = dot(wt_ref[:most].reshape(3 * width, width), n1b_ref[...], ((1,), (1,))).astype(jnp.bfloat16)
    for head in range(heads):
        query = qkv_ref[head * size : (head + 1) * size]
        keys = qkv_ref[width + head * size : width + (head + 1) * size]
        values = qkv_ref[2 * width + head * size : 2 * width + (head + 1) * size]
        scores = dot(keys, query, ((0,), (0,))) + bias_ref[head]
        raised = jnp.exp(scores - jnp.max(scores, axis=0, keepdims=True))
        probs = raised / jnp.sum(raised, axis=0, keepdims=True)
        probs_ref[head] = probs
        mixed_t[head * size : (head + 1) * size] = dot(
            values, probs.astype(jnp.bfloat16), ((1,), (0,))
        )
    mixed_ref[...] = mixed_t[...].T.astype(jnp.bfloat16)
    resid = x + dot(
        mixed_ref[...], wt_ref[most:].reshape(width, width), ((1,), (1,))
    )
    resid_ref[...] = resid
    n2b_ref[...] = (resid * rms_scale(resid) * gain_two_ref[...]).astype(jnp.bfloat16)
    rows = dot(dispatch_ref[...], n2b_ref[...], ((1,), (0,)))
    rows_ref[:, :width] = rows.astype(jnp.bfloat16)
    dy_rows = dot(dispatch_ref[...], dy_ref[...], ((1,), (0,)))
    rows_ref[:, width:] = dy_rows.astype(jnp.bfloat16)
    leave_qkv.wait()
    leave_o.wait()


def attend_back_kernel(
    core_ref, dn2_ref, dispatch_ref, resid_ref, dy_ref, gain_two_ref, wt_ref, qkv_ref, probs_ref,
    n1b_ref, mixed_ref, dresid_ref, gain_ref, dqkv_ref, fold_ref, send_ref, keep_ref, columns,
):
    heads = probs_ref.shape[0]
    count, width = resid_ref.shape
    size = width // heads
    core = core_ref[0]
    resid = resid_ref[...]
    scale = rms_scale(resid)
    n2hat = resid * scale
    dn2 = dot(dispatch_ref[...], dn2_ref[:, :width], ((0,), (0,)))
    gain_ref[...] = jnp.sum(dn2 * n2hat, axis=0, keepdims=True)
    dhat = dn2 * gain_two_ref[...]
    dresid = dy_ref[...].astype(jnp.float32) + scale * (
        dhat - n2hat * jnp.mean(dhat * n2hat, axis=-1, keepdims=True)
    )
    dresid_ref[...] = dresid
    dattn = dresid.astype(jnp.bfloat16)
    dab = dot(dattn, wt_ref[...], ((1,), (0,)))
    dab_t = dab.T.astype(jnp.bfloat16)
    columns[3 * width :] = dresid.T.astype(jnp.bfloat16)
    for head in range(heads):
        at = slice(head * size, (head + 1) * size)
        query = qkv_ref[head * size : (head + 1) * size]
        keys = qkv_ref[width + head * size : width + (head + 1) * size]
        values = qkv_ref[2 * width + head * size : 2 * width + (head + 1) * size]
        dab_head = dab_t[at]
        probs = probs_ref[head]
        dvalue = dot(dab_head, probs.astype(jnp.bfloat16), ((1,), (1,)))
        dprobs = dot(values, dab_head, ((0,), (0,)))
        dscores = probs * (dprobs - jnp.sum(probs * dprobs, axis=0, keepdims=True))
        half = count // 2
        fold_ref[head] = dscores[:half] + dscores[half:]
        dscores_b = dscores.astype(jnp.bfloat16)
        dquery = dot(keys, dscores_b, ((1,), (0,)))
        dkey = dot(query, dscores_b, ((1,), (1,)))
        columns[head * size : (head + 1) * size] = dquery.astype(jnp.bfloat16)
        columns[width + head * size : width + (head + 1) * size] = dkey.astype(jnp.bfloat16)
        columns[2 * width + head * size : 2 * width + (head + 1) * size] = dvalue.astype(
            jnp.bfloat16
        )
    dqkv_ref[...] = columns[: 3 * width]
    block = width // 8
    sent = []
    for pair in range(16):
        theirs = pl.multiple_of((2 * pair + 1 - core) * block, block)
        mine = pl.multiple_of((2 * pair + core) * block, block)
        keep_ref[pair * block : (pair + 1) * block] = columns[pl.ds(mine, block), :]
        sent.append(columns[pl.ds(theirs, block), :])
    sent = jnp.concatenate(sent, axis=0)
    split = 12 * block
    send_ref[:split] = dot(sent[:split], n1b_ref[...], ((1,), (0,))).astype(jnp.bfloat16)
    send_ref[split:] = dot(sent[split:], mixed_ref[...], ((1,), (0,))).astype(jnp.bfloat16)


def token_back_kernel(
    bucket_count, _, x_ref, dqkv_ref, wt_ref, gain_one_ref, dresid_ref, fold_ref, buckets_ref, gain_part_ref,
    router_part_ref, grad_ref, small_ref,
):
    x = x_ref[...].astype(jnp.float32)
    scale = rms_scale(x)
    n1hat = x * scale
    width = x.shape[1]
    dn1 = dot(dqkv_ref[...], wt_ref[...], ((0,), (0,)))
    gain_part = jnp.sum(dn1 * n1hat, axis=0, keepdims=True)
    dhat = dn1 * gain_one_ref[...]
    grad_ref[...] = dresid_ref[...] + scale * (
        dhat - n1hat * jnp.mean(dhat * n1hat, axis=-1, keepdims=True)
    )
    experts = router_part_ref.shape[0]
    tiles = width // 128
    small_ref[...] = jnp.zeros(small_ref.shape, jnp.float32)
    for tile in range(tiles):
        at = slice(tile * 128, (tile + 1) * 128)
        small_ref[tile * experts : (tile + 1) * experts] = router_part_ref[:, at]
        base = tiles * experts + tile
        small_ref[base : base + 1] = gain_part[:, at]
        small_ref[base + 8 : base + 9] = gain_part_ref[:, at]
    heads = fold_ref.shape[0]
    lane = lax.broadcasted_iota(jnp.int32, (1, 128), 1)
    table = jnp.zeros((heads, 128), jnp.float32)
    buckets = buckets_ref[: fold_ref.shape[1]]
    fold = fold_ref[...]
    for bucket in range(bucket_count):
        column = jnp.sum(jnp.where((buckets == bucket)[None], fold, 0.0), axis=1)
        column = jnp.sum(column, axis=-1, keepdims=True)
        table = table + jnp.where(lane == bucket, column, 0.0)
    start = tiles * experts + 16
    small_ref[start : start + heads] = table


def split_kernel(
    place_ref, keep_ref, n1b_ref, mixed_ref, got_ref,
    send_a, send_b, send_c, keep_a, keep_b, keep_c, total,
):
    split = keep_ref.shape[0] * 3 // 4
    blocks, block, width = total.shape
    first = dot(keep_ref[:split], n1b_ref[...], ((1,), (0,)))
    first = first + got_ref[:split].astype(jnp.float32)
    total[: blocks * 3 // 4] = first.reshape(blocks * 3 // 4, block, width)
    last = dot(keep_ref[split:], mixed_ref[...], ((1,), (0,)))
    last = last + got_ref[split:].astype(jnp.float32)
    total[blocks * 3 // 4 :] = last.reshape(blocks // 4, block, width)
    begin = 0
    for index, (send, keep) in enumerate(((send_a, keep_a), (send_b, keep_b), (send_c, keep_c))):
        mine = place_ref[3 + index]
        stride = {2: 1, 4: 2, 8: 4, "y": 8}[RS_ORDERS[index][0]]
        columns = slice(begin, begin + send.shape[2])
        begin += send.shape[2]
        for j in range(blocks // 2):
            low = j // stride * 2 * stride + j % stride
            send[j] = total[low + (1 - mine) * stride, :, columns].astype(jnp.bfloat16)
            keep[j] = total[low + mine * stride, :, columns]


def expert_kernel(
    place_ref, own_ref, got_ref, router_ref,
    in_near_ref, in_arrived_ref, in_far_ref, out_near_ref, out_arrived_ref, out_far_ref,
    rows_ref, hidden_ref, du_ref, dmade_ref, mine_ref, theirs_ref, probs_ref, in_full, out_full,
):
    core, host = place_ref[0], place_ref[1]
    half, units = in_far_ref.shape
    own, width = got_ref.shape[0], got_ref.shape[1] // 2
    for side in range(2):

        at, other = slice(side * half, (side + 1) * half), slice((1 - side) * half, (2 - side) * half)

        @pl.when(core == side)
        def _():
            in_full[other] = in_far_ref[...]
            out_full[:, other] = out_far_ref[...]

        @pl.when((core == side) & (place_ref[2] == 1))
        def _():
            in_full[at] = in_near_ref[...]
            out_full[:, at] = out_near_ref[...]

        @pl.when((core == side) & (place_ref[2] == 0))
        def _():
            in_full[at] = in_arrived_ref[...]
            out_full[:, at] = out_arrived_ref[...]

    rows = jnp.concatenate([own_ref[:, :width], got_ref[:, :width]], axis=0)
    dy = jnp.concatenate([own_ref[:, width:], got_ref[:, width:]], axis=0)
    rows_ref[...] = rows
    logits = dot(rows, router_ref[...], ((1,), (0,)))
    raised = jnp.exp(logits - jnp.max(logits, axis=-1, keepdims=True))
    probs = raised / jnp.sum(raised, axis=-1, keepdims=True)
    probs_ref[...] = probs[:own]
    chosen = lax.broadcasted_iota(jnp.int32, probs.shape, 1) == host
    gate = jnp.sum(jnp.where(chosen, probs, 0.0), axis=-1, keepdims=True)
    dmade_ref[...] = (gate * dy.astype(jnp.float32)).astype(jnp.bfloat16)
    dmade = dmade_ref[...]
    made = jnp.zeros(rows.shape, jnp.float32)
    drows = jnp.zeros(rows.shape, jnp.float32)
    step = units // 3
    for begin in range(0, units, step):
        at = slice(begin, begin + step)
        upre = dot(rows, in_full[:, at], ((1,), (0,)))
        square = upre * upre
        bent = jnp.tanh(0.7978845608028654 * (upre + 0.044715 * upre * square))
        hidden = (0.5 * upre * (1.0 + bent)).astype(jnp.bfloat16)
        slope = 0.5 * (1.0 + bent) + 0.5 * upre * (1.0 - bent * bent) * (
            0.7978845608028654 * (1.0 + 3.0 * 0.044715 * square)
        )
        dhidden = dot(dmade, out_full[at, :], ((1,), (1,)))
        du = (dhidden * slope).astype(jnp.bfloat16)
        hidden_ref[:, at] = hidden
        du_ref[:, at] = du
        made = made + dot(hidden, out_full[at, :], ((1,), (0,)))
        drows = drows + dot(du, in_full[:, at], ((1,), (1,)))
    mine_ref[0] = made[:own]
    mine_ref[1] = drows[:own]
    theirs_ref[0] = made[own:]
    theirs_ref[1] = drows[own:]


def settle_kernel(
    place_ref, mine_ref, got_ref, own_ref, probs_ref, router_ref, back_ref, router_part_ref
):
    width = own_ref.shape[1] // 2
    made = (mine_ref[0] + got_ref[0]).astype(jnp.bfloat16)
    back_ref[:, width:] = made
    drows = (mine_ref[1] + got_ref[1]).astype(jnp.bfloat16).astype(jnp.float32)
    probs = probs_ref[...]
    chosen = (lax.broadcasted_iota(jnp.int32, probs.shape, 1) == place_ref[1]).astype(jnp.float32)
    gate = jnp.sum(probs * chosen, axis=-1, keepdims=True)
    dgate = jnp.sum(
        own_ref[:, width:].astype(jnp.float32) * made.astype(jnp.float32),
        axis=-1,
        keepdims=True,
    )
    dlogits = probs * dgate * (chosen - gate)
    router_part_ref[...] = dot(
        dlogits, own_ref[:, :width].astype(jnp.float32), ((0,), (0,)), precision=HIGH
    )
    dn2 = drows + dot(dlogits, router_ref[...].astype(jnp.float32), ((1,), (1,)), precision=HIGH)
    back_ref[:, :width] = dn2.astype(jnp.bfloat16)


def paired_body(
    tokens,
    attn_weight,
    gain_attn,
    gain_expert,
    bias_table,
    router_weight,
    expert_in,
    expert_out,
    routes,
    slots,
    buckets,
    cotangent,
):
    f32, bf16 = jnp.float32, jnp.bfloat16
    micro, _, seq_len, width = tokens.shape
    count = micro * seq_len
    heads = bias_table.shape[1]
    head_size = width // heads
    bucket_count = bias_table.shape[0]
    experts = lax.axis_size("expert")
    capacity = (5 * seq_len + 4 * experts - 1) // (4 * experts)
    places = micro * capacity
    hidden_half = expert_in.shape[2] // 2
    width_half = width // 2
    dp_at, expert_at = lax.axis_index("dp"), lax.axis_index("expert")
    core = expert_at % 2
    home = core == dp_at
    host = expert_at - core + dp_at
    gain_one, gain_two = gain_attn.astype(f32), gain_expert.astype(f32)

    across, first = [], []
    for dp in range(2):
        for e in range(experts):
            here = dp * experts + e
            if e % 2 == dp:
                first.append((here, dp * experts + (e ^ 1), (1 - dp) * experts + e))
            else:
                across.append((here, (1 - dp) * experts + (e ^ 1)))
                first.append((here, (1 - dp) * experts + e, dp * experts + (e ^ 1)))
    outward = [(here, there) for here, there, _ in first]
    homeward = [(here, there) for here, _, there in first]

    groups = [
        [dp * experts + 2 * pair + side for dp in range(2) for pair in range(experts // 2)]
        for side in range(2)
    ]

    def to_chips(tensor):
        return lax.all_to_all(
            tensor, BOTH, split_axis=0, concat_axis=0, tiled=True, axis_index_groups=groups
        )

    route_ids, slot_ids = routes[:, 0], slots[:, 0]
    chip = (route_ids % 2) * (experts // 2) + route_ids // 2
    flat = chip * places + jnp.arange(micro)[:, None] * capacity + slot_ids
    flat = jnp.where(slot_ids < capacity, flat, -1).reshape(1, count)
    dispatch = (flat == jnp.arange(experts * places)[:, None]).astype(bf16)
    upstream_b = cotangent.reshape(count, width)
    def parts_of(local, axis):
        near = lax.dynamic_slice_in_dim(local, dp_at * hidden_half, hidden_half, axis)
        far = lax.dynamic_slice_in_dim(local, (1 - dp_at) * hidden_half, hidden_half, axis)
        return near, far

    in_near, in_far = parts_of(expert_in[0], 1)
    in_arrived = lax.ppermute(in_near, BOTH, across)

    def halves(tensor):
        return (
            lax.dynamic_slice_in_dim(tensor, core * width_half, width_half, 1),
            lax.dynamic_slice_in_dim(tensor, (1 - core) * width_half, width_half, 1),
        )

    def whole(keep, got, axis):
        low = core == 0
        return jnp.concatenate(
            [jnp.where(low, keep, got), jnp.where(low, got, keep)], axis=axis
        )

    def prepare(table, ids, out_local):
        tiled = jnp.tile(ids.T, (micro, micro))
        (square,) = call(bias_kernel, 10, (((heads, count, count), f32),), [], table, tiled)
        return (square, tiled, in_far) + parts_of(out_local, 0)

    pieces, in_arrived, dispatch, ready = gather_rows(
        attn_weight.T,
        in_arrived,
        dispatch,
        prepare,
        (bias_table.astype(f32), buckets, expert_out[0]),
    )
    square, tiled, in_far, out_near, out_far = ready
    out_arrived = lax.ppermute(out_near, BOTH, across)
    place = jnp.stack(
        [core, host, home.astype(jnp.int32)] + [own_bit(order[0]) for order in RS_ORDERS]
    ).astype(jnp.int32)
    gain_one, gain_two = gain_one[None], gain_two[None]
    local = tokens.reshape(count, width)
    row_count = dispatch.shape[0]
    wt_qkv, wt_o, n1b, qkv, probs, mixed_b, resid, n2b, outgoing = call(
        attend_kernel,
        26,
        (
            ((12, 2, width // 8, width), bf16),
            ((4, 2, width // 8, width), bf16),
            ((count, width), bf16),
            ((3 * width, count), bf16),
            ((heads, count, count), f32),
            ((count, width), bf16),
            ((count, width), f32),
            ((count, width), bf16),
            ((row_count, 2 * width), bf16),
        ),
        [
            pltpu.VMEM((width, count), f32),
            pltpu.VMEM((16, 2, width // 8, width), bf16),
            pltpu.SemaphoreType.DMA,
            pltpu.SemaphoreType.DMA,
            pltpu.SemaphoreType.DMA,
        ],
        place, local, *pieces, gain_one, gain_two, square, dispatch, upstream_b,
        plain_in=range(2, 8),
        plain_out=(0, 1),
    )
    wt_qkv, wt_o = wt_qkv.reshape(3 * width, width), wt_o.reshape(width, width)
    outgoing, out_arrived, in_far, out_far = lax.optimization_barrier(
        (outgoing, out_arrived, lax.ppermute(in_far, BOTH, outward), out_far)
    )
    own_rows = to_chips(outgoing)
    in_parts = (in_near, in_arrived, in_far)
    out_parts = (out_near, out_arrived, lax.ppermute(out_far, BOTH, outward))
    rows, hidden, du, dmade, mine, theirs, row_probs = call(
        expert_kernel,
        34,
        (
            ((2 * row_count, width), bf16),
            ((2 * row_count, hidden_half), bf16),
            ((2 * row_count, hidden_half), bf16),
            ((2 * row_count, width), bf16),
            ((2, row_count, width), f32),
            ((2, row_count, width), f32),
            ((row_count, experts), f32),
        ),
        [pltpu.VMEM((width, hidden_half), bf16), pltpu.VMEM((hidden_half, width), bf16)],
        place, own_rows, flip(own_rows, 1), router_weight, *in_parts, *out_parts,
    )
    back_rows, router_part = call(
        settle_kernel,
        10,
        (
            ((row_count, 2 * width), bf16),
            ((experts, width), f32),
        ),
        [],
        place, mine, flip(theirs, 1), own_rows, row_probs, router_weight,
    )
    in_other = dot(halves(rows)[1], du, ((0,), (0,))).astype(bf16)
    back_rows, rows, hidden, du, dmade = lax.optimization_barrier(
        (back_rows, rows, hidden, du, dmade)
    )
    home_rows = to_chips(back_rows)
    rows_keep, _ = halves(rows)
    dmade_keep, dmade_got = halves(dmade)

    in_homely = lax.ppermute(in_other, BOTH, homeward)
    in_mine = dot(rows_keep, du, ((0,), (0,)))
    out_other = dot(hidden, dmade_got, ((0,), (0,))).astype(bf16)
    out_homely = lax.ppermute(out_other, BOTH, homeward)
    out_mine = dot(hidden, dmade_keep, ((0,), (0,)))
    home_rows, in_homely, out_homely, in_leave, out_leave = lax.optimization_barrier(
        (home_rows, in_homely, out_homely, in_mine.astype(bf16), out_mine.astype(bf16))
    )
    in_arrived = lax.ppermute(in_leave, BOTH, across)
    out_arrived = lax.ppermute(out_leave, BOTH, across)

    dresid, gain_two_part, dqkv, fold, send, keep = call(
        attend_back_kernel,
        26,
        (
            ((count, width), f32),
            ((1, width), f32),
            ((3 * width, count), bf16),
            ((heads, count // 2, count), f32),
            ((2 * width, width), bf16),
            ((2 * width, count), bf16),
        ),
        [pltpu.VMEM((4 * width, count), bf16)],
        place, home_rows, dispatch, resid, upstream_b, gain_two, wt_o, qkv, probs, n1b, mixed_b,
    )
    got = flip(send, 1)
    small_rows = (width // 128) * experts + 16 + (heads + 7) // 8 * 8
    token_grad, small = call(
        functools.partial(token_back_kernel, bucket_count),
        26,
        (
            ((count, width), f32),
            ((small_rows, 128), f32),
        ),
        [],
        place, local, dqkv, wt_qkv, gain_one, dresid, fold, tiled, gain_two_part,
        router_part,
    )
    block = width // 8
    pieces = (width // 2, width // 3, width // 6)
    cut = call(
        split_kernel,
        30,
        tuple(((8, block, piece), bf16) for piece in pieces)
        + tuple(((8, block, piece), f32) for piece in pieces),
        [pltpu.VMEM((16, block, width), f32)],
        place, keep, n1b, mixed_b, got,
    )
    attn_share, small, late = scatter_rows(
        cut[:3],
        cut[3:],
        small,
        (
            (),
            (in_arrived, in_mine, in_homely),
            (out_arrived, out_mine, out_homely),
            home_rows,
        ),
    )
    _, (in_arrived, in_mine, in_homely), (out_arrived, out_mine, out_homely), home_rows = late
    in_back = (in_mine, in_homely, in_arrived)
    out_back = (out_mine, out_homely, out_arrived)

    def settled(parts, axis):
        near, homely, arrived = parts
        mine = jnp.where(home, near, homely.astype(f32))
        other = jnp.where(home, homely.astype(f32), arrived.astype(f32))
        return whole(mine, other, axis)

    in_share, out_share = settled(in_back, 1), settled(out_back, 0)
    router_probs = jax.nn.softmax(dot(n2b, router_weight, ((1,), (0,))), axis=-1)
    picked = (route_ids.reshape(count, 1) == jnp.arange(experts)).astype(f32)
    gate = jnp.sum(router_probs * picked, axis=-1, keepdims=True)
    returned = dot(dispatch, home_rows[:, width:], ((0,), (0,)))
    output = (resid + gate * returned).astype(bf16)

    attn_share = attn_share.T
    routed = (width // 128) * experts
    return (
        output.reshape(tokens.shape),
        token_grad.reshape(tokens.shape),
        attn_share,
        small[routed : routed + width // 128].reshape(width),
        small[routed + 8 : routed + 8 + width // 128].reshape(width),
        small[routed + 16 : routed + 16 + heads, :bucket_count].T,
        jnp.transpose(small[:routed].reshape(-1, experts, 128), (0, 2, 1)).reshape(width, experts),
        in_share[None],
        out_share[None],
    )


def solution(mesh):
    paired = mesh.shape["dp"] == 2 and mesh.shape["expert"] == 16
    chosen = paired_body if paired else body
    placed = (
        P(None, ("dp", "expert"), None, None),
        P(None, ("dp", "expert")),
        P(),
        P(),
        P(),
        P(),
        P("expert", "dp", None),
        P("expert", None, "dp"),
        P(None, ("dp", "expert"), None),
        P(None, ("dp", "expert"), None),
        P(),
        P(None, ("dp", "expert"), None, None),
    )
    return jax.shard_map(
        chosen,
        mesh=mesh,
        in_specs=placed,
        out_specs=(
            P(None, ("dp", "expert"), None, None),
            P(None, ("dp", "expert"), None, None),
            P(None, ("dp", "expert")),
            P(),
            P(),
            P(),
            P(),
            P("expert", "dp", None),
            P("expert", None, "dp"),
        ),
        check_vma=False,
    )
```

```python
import functools
import jax
import jax.numpy as jnp
from jax import lax
from jax.experimental import pallas as pl
from jax.experimental.pallas import tpu as pltpu
from jax.sharding import PartitionSpec as P

EPSILON = 1e-06
HIGH = lax.Precision.HIGHEST


def smooth_gate(values):
    return jax.nn.gelu(values, approximate=True)


def rms_scale(values):
    return lax.rsqrt(jnp.mean(values * values, axis=-1, keepdims=True) + EPSILON)


def body(
    tokens,
    attn_weight,
    gain_attn,
    gain_expert,
    bias_table,
    router_weight,
    expert_in,
    expert_out,
    routes,
    slots,
    buckets,
    cotangent,
):
    micro = tokens.shape[0]
    seq_len = tokens.shape[2]
    width = tokens.shape[3]
    heads = bias_table.shape[1]
    head_size = width // heads
    bucket_count = bias_table.shape[0]
    local_experts = expert_in.shape[0]
    expert_devices = lax.axis_size("expert")
    total_experts = local_experts * expert_devices
    capacity = (5 * seq_len + 4 * total_experts - 1) // (4 * total_experts)
    slot_total = total_experts * capacity
    gain_one = gain_attn.astype(jnp.float32)
    gain_two = gain_expert.astype(jnp.float32)
    router_full = router_weight.astype(jnp.float32)
    bucket_hot = (buckets[:, :, None] == jnp.arange(bucket_count)).astype(jnp.float32)
    bias_term = jnp.einsum(
        "ijb,bh->hij", bucket_hot, bias_table.astype(jnp.float32), precision=HIGH
    )

    def to_experts(tensor):
        tensor = tensor.reshape(expert_devices, local_experts, capacity, width)
        return jnp.transpose(tensor, (1, 0, 2, 3)).reshape(
            local_experts, expert_devices * capacity, width
        )

    def from_experts(tensor):
        tensor = tensor.reshape(local_experts, expert_devices, capacity, width)
        return jnp.transpose(tensor, (1, 0, 2, 3)).reshape(total_experts, capacity, width)

    gain_one_total = jnp.zeros((width,), jnp.float32)
    gain_two_total = jnp.zeros((width,), jnp.float32)
    bias_total = jnp.zeros((bucket_count, heads), jnp.float32)
    router_total = jnp.zeros((width, total_experts), jnp.float32)
    results = []
    token_grads = []
    kept_rows = []
    kept_hidden = []
    kept_dmade = []
    kept_dpre = []
    kept_mixed = []
    kept_dattn = []
    kept_normed = []
    kept_dqkv = []
    for micro_index in range(micro):
        inputs = tokens[micro_index, 0].astype(jnp.float32)
        full_attn = lax.all_gather(attn_weight, ("dp", "expert"), axis=1, tiled=True)
        scale_one = rms_scale(inputs)
        n1hat = inputs * scale_one
        n1b = (n1hat * gain_one).astype(jnp.bfloat16)
        qkv = jnp.dot(n1b, full_attn[:, : 3 * width], preferred_element_type=jnp.float32).astype(
            jnp.bfloat16
        )
        query = qkv[:, :width].reshape(seq_len, heads, head_size)
        key_part = qkv[:, width : 2 * width].reshape(seq_len, heads, head_size)
        value_part = qkv[:, 2 * width :].reshape(seq_len, heads, head_size)
        scores = (
            jnp.einsum("ihd,jhd->hij", query, key_part, preferred_element_type=jnp.float32)
            + bias_term
        )
        log_total = jax.nn.logsumexp(scores, axis=-1, keepdims=True)
        probs_b = jnp.exp(scores - log_total).astype(jnp.bfloat16)
        mixed = jnp.einsum("hij,jhd->ihd", probs_b, value_part, preferred_element_type=jnp.float32)
        mixed_b = mixed.reshape(seq_len, width).astype(jnp.bfloat16)
        resid = inputs + jnp.dot(
            mixed_b, full_attn[:, 3 * width :], preferred_element_type=jnp.float32
        )
        scale_two = rms_scale(resid)
        n2hat = resid * scale_two
        n2b = (n2hat * gain_two).astype(jnp.bfloat16)
        logits = jnp.dot(n2b, router_weight, preferred_element_type=jnp.float32)
        router_probs = jax.nn.softmax(logits, axis=-1)
        route_ids = routes[micro_index, 0]
        slot_ids = slots[micro_index, 0]
        picked = (route_ids[:, None] == jnp.arange(total_experts)).astype(jnp.float32)
        gate = jnp.sum(router_probs * picked, axis=-1)
        flat = route_ids * capacity + slot_ids
        dispatch = (
            (flat[:, None] == jnp.arange(slot_total)) & (slot_ids[:, None] < capacity)
        ).astype(jnp.bfloat16)
        outgoing = jnp.einsum(
            "sk,sd->kd", dispatch, n2b, preferred_element_type=jnp.float32
        ).astype(jnp.bfloat16)
        arrived = lax.all_to_all(
            outgoing.reshape(total_experts, capacity, width),
            "expert",
            split_axis=0,
            concat_axis=0,
            tiled=True,
        )
        expert_rows = to_experts(arrived)
        full_in, full_out = (
            lax.all_gather(expert_in, "dp", axis=1, tiled=True),
            lax.all_gather(expert_out, "dp", axis=2, tiled=True),
        )
        hidden_pre = jnp.einsum(
            "erd,edf->erf", expert_rows, full_in, preferred_element_type=jnp.float32
        )
        hidden = smooth_gate(hidden_pre).astype(jnp.bfloat16)
        made = jnp.einsum(
            "erf,efd->erd", hidden, full_out, preferred_element_type=jnp.float32
        ).astype(jnp.bfloat16)
        kept_rows.append(expert_rows)
        kept_hidden.append(hidden)
        came_back = lax.all_to_all(
            from_experts(made), "expert", split_axis=0, concat_axis=0, tiled=True
        )
        returned = jnp.einsum(
            "sk,kd->sd",
            dispatch,
            came_back.reshape(slot_total, width),
            preferred_element_type=jnp.float32,
        )
        results.append((resid + gate[:, None] * returned).astype(jnp.bfloat16))
        upstream = cotangent[micro_index, 0].astype(jnp.float32)
        dgate = jnp.sum(upstream * returned, axis=-1)
        dreturned = (gate[:, None] * upstream).astype(jnp.bfloat16)
        dslots = jnp.einsum(
            "sk,sd->kd", dispatch, dreturned, preferred_element_type=jnp.float32
        ).astype(jnp.bfloat16)
        dmade = to_experts(
            lax.all_to_all(
                dslots.reshape(total_experts, capacity, width),
                "expert",
                split_axis=0,
                concat_axis=0,
                tiled=True,
            )
        )
        back_attn = lax.all_gather(attn_weight, ("dp", "expert"), axis=1, tiled=True)
        back_in, back_out = (
            lax.all_gather(expert_in, "dp", axis=1, tiled=True),
            lax.all_gather(expert_out, "dp", axis=2, tiled=True),
        )
        dhidden = jnp.einsum("erd,efd->erf", dmade, back_out, preferred_element_type=jnp.float32)
        dpre = jax.vjp(smooth_gate, hidden_pre)[1](dhidden)[0].astype(jnp.bfloat16)
        kept_dmade.append(dmade)
        kept_dpre.append(dpre)
        drows = jnp.einsum(
            "erf,edf->erd", dpre, back_in, preferred_element_type=jnp.float32
        ).astype(jnp.bfloat16)
        drows_home = lax.all_to_all(
            from_experts(drows), "expert", split_axis=0, concat_axis=0, tiled=True
        )
        dnormed = jnp.einsum(
            "sk,kd->sd",
            dispatch,
            drows_home.reshape(slot_total, width),
            preferred_element_type=jnp.float32,
        )
        dpick = picked * dgate[:, None]
        dlogits = router_probs * (dpick - jnp.sum(router_probs * dpick, axis=-1, keepdims=True))
        router_total = router_total + jnp.dot(n2b.astype(jnp.float32).T, dlogits, precision=HIGH)
        dnormed = dnormed + jnp.dot(dlogits, router_full.T, precision=HIGH)
        gain_two_total = gain_two_total + jnp.sum(dnormed * n2hat, axis=0)
        dhat_two = dnormed * gain_two
        dresid = upstream + scale_two * (
            dhat_two - n2hat * jnp.mean(dhat_two * n2hat, axis=-1, keepdims=True)
        )
        dattn = dresid.astype(jnp.bfloat16)
        dmixed = jnp.einsum(
            "se,de->sd", dattn, back_attn[:, 3 * width :], preferred_element_type=jnp.float32
        )
        dmixed = dmixed.astype(jnp.bfloat16).reshape(seq_len, heads, head_size)
        again_scores = (
            jnp.einsum("ihd,jhd->hij", query, key_part, preferred_element_type=jnp.float32)
            + bias_term
        )
        probs = jnp.exp(again_scores - log_total)
        again_b = probs.astype(jnp.bfloat16)
        dvalue = jnp.einsum("hij,ihd->jhd", again_b, dmixed, preferred_element_type=jnp.float32)
        dprobs = jnp.einsum("ihd,jhd->hij", dmixed, value_part, preferred_element_type=jnp.float32)
        dscores = probs * (dprobs - jnp.sum(probs * dprobs, axis=-1, keepdims=True))
        bias_total = bias_total + jnp.einsum("hij,ijb->bh", dscores, bucket_hot, precision=HIGH)
        dscores_b = dscores.astype(jnp.bfloat16)
        dquery = jnp.einsum("hij,jhd->ihd", dscores_b, key_part, preferred_element_type=jnp.float32)
        dkey = jnp.einsum("hij,ihd->jhd", dscores_b, query, preferred_element_type=jnp.float32)
        dqkv = jnp.concatenate(
            [
                dquery.reshape(seq_len, width),
                dkey.reshape(seq_len, width),
                dvalue.reshape(seq_len, width),
            ],
            axis=1,
        ).astype(jnp.bfloat16)
        kept_mixed.append(mixed_b)
        kept_dattn.append(dattn)
        kept_normed.append(n1b)
        kept_dqkv.append(dqkv)
        dnormed_one = jnp.einsum(
            "se,de->sd", dqkv, back_attn[:, : 3 * width], preferred_element_type=jnp.float32
        )
        gain_one_total = gain_one_total + jnp.sum(dnormed_one * n1hat, axis=0)
        dhat_one = dnormed_one * gain_one
        token_grads.append(
            dresid
            + scale_one * (dhat_one - n1hat * jnp.mean(dhat_one * n1hat, axis=-1, keepdims=True))
        )
    normed_all = jnp.concatenate(kept_normed, axis=0)
    dqkv_all = jnp.concatenate(kept_dqkv, axis=0)
    mixed_all = jnp.concatenate(kept_mixed, axis=0)
    dattn_all = jnp.concatenate(kept_dattn, axis=0)
    dqkv_proj = jnp.einsum("sd,se->de", normed_all, dqkv_all, preferred_element_type=jnp.float32)
    dout_proj = jnp.einsum("sd,se->de", mixed_all, dattn_all, preferred_element_type=jnp.float32)
    attn_total = jnp.concatenate([dqkv_proj, dout_proj], axis=1)
    attn_share = lax.psum_scatter(attn_total, ("dp", "expert"), scatter_dimension=1, tiled=True)
    rows_all = jnp.concatenate(kept_rows, axis=1)
    hidden_all = jnp.concatenate(kept_hidden, axis=1)
    dmade_cat = jnp.concatenate(kept_dmade, axis=1)
    dpre_all = jnp.concatenate(kept_dpre, axis=1)
    in_total = jnp.einsum("erd,erf->edf", rows_all, dpre_all, preferred_element_type=jnp.float32)
    out_turned_total = jnp.einsum(
        "erd,erf->edf", dmade_cat, hidden_all, preferred_element_type=jnp.float32
    )
    in_share, out_turned_share = (
        lax.psum_scatter(
            in_total.astype(jnp.bfloat16), "dp", scatter_dimension=1, tiled=True
        ).astype(jnp.float32),
        lax.psum_scatter(
            out_turned_total.astype(jnp.bfloat16), "dp", scatter_dimension=1, tiled=True
        ).astype(jnp.float32),
    )
    out_share = jnp.transpose(out_turned_share, (0, 2, 1))
    gain_one_sum, gain_two_sum, bias_sum, router_sum = lax.psum(
        (gain_one_total, gain_two_total, bias_total, router_total), ("dp", "expert")
    )
    output = jnp.stack(results)[:, None]
    token_grad = jnp.stack(token_grads)[:, None]
    return (
        output,
        token_grad,
        attn_share,
        gain_one_sum,
        gain_two_sum,
        bias_sum,
        router_sum,
        in_share,
        out_share,
    )


BOTH = ("dp", "expert")


def flip(tensor, bit):
    if bit == "y":
        return lax.ppermute(tensor, "dp", [(0, 1), (1, 0)])
    count = lax.axis_size("expert")
    return lax.ppermute(tensor, "expert", [(i, i ^ bit) for i in range(count)])


def own_bit(bit):
    if bit == "y":
        return lax.axis_index("dp")
    return (lax.axis_index("expert") // bit) % 2


ORDERS = ((8, "y", 4, 2), (2, "y", 8, 4), ("y", 2, 8, 4))
RS_ORDERS = ((2, "y", 8, 4), ("y", 8, 4, 2), (8, 4, 2, "y"))
PLACE = {"y": 0, 8: 1, 4: 2, 2: 3, 1: 4}


def gather_rows(shard, prepare, waiting):
    rows, width = shard.shape
    pieces, begin = [], 0
    for size in (width // 2, width // 6, width // 3):
        piece = shard[:, begin : begin + size]
        pieces.append(piece.reshape(1, 1, 1, 1, rows, size))
        begin += size

    def grow(piece, bit):
        got = flip(piece, bit)
        low = own_bit(bit) == 0
        return jnp.concatenate(
            [jnp.where(low, piece, got), jnp.where(low, got, piece)], axis=PLACE[bit]
        )

    for step in range(4):
        if step == 2:
            pieces, waiting = lax.optimization_barrier((pieces, waiting))
            ready = prepare(*waiting)
        pieces = [grow(piece, ORDERS[i][step]) for i, piece in enumerate(pieces)]
    pieces, ready = lax.optimization_barrier((pieces, ready))
    pieces = [piece.reshape(-1, rows, piece.shape[-1]) for piece in pieces]
    return pieces + [flip(piece, 1) for piece in pieces], ready


def reduce_step(total, bit):
    mine = own_bit(bit)
    axis = PLACE[bit]
    send = lax.dynamic_index_in_dim(total, 1 - mine, axis, keepdims=True).astype(jnp.bfloat16)
    keep = lax.dynamic_index_in_dim(total, mine, axis, keepdims=True)
    return keep + flip(send, bit).astype(jnp.float32)


def scatter_rows(leaves, stays, small, late):
    late = list(late)
    pieces = []
    for index, (leave, stay) in enumerate(zip(leaves, stays)):
        bit = RS_ORDERS[index][0]
        shape = [2, 2, 2, 2, 1] + list(stay.shape[1:])
        shape[PLACE[bit]] = 1
        pieces.append((stay + flip(leave, bit).astype(jnp.float32)).reshape(shape))
    for bit in (1, 2):
        small = small + flip(small, bit)
    for step in range(1, 4):
        pieces, late[step], small = lax.optimization_barrier((pieces, late[step], small))
        pieces = [reduce_step(piece, RS_ORDERS[i][step]) for i, piece in enumerate(pieces)]
        small = small + flip(small, ("y", 8, 4)[step - 1])
    whole = jnp.concatenate(pieces, axis=-1)
    return whole.reshape(whole.shape[-2], whole.shape[-1]), small, late


def dot(left, right, dims, **more):
    return lax.dot_general(
        left, right, (dims, ((), ())), preferred_element_type=jnp.float32, **more
    )


def call(kernel, mib, outs, scratch, *operands, plain_in=(), plain_out=()):
    def spec(shape):
        return pl.BlockSpec(
            shape, lambda i: (0,) * len(shape), pipeline_mode=pl.Buffered(1)
        )

    left = pl.BlockSpec(memory_space=pl.ANY)
    operands = operands[:1] + tuple(
        pltpu.with_memory_space_constraint(operand, pltpu.HBM) for operand in operands[1:]
    )
    return pl.pallas_call(
        kernel,
        grid=(1,),
        out_shape=tuple(pltpu.HBM(*out) for out in outs),
        in_specs=[pl.BlockSpec(memory_space=pltpu.SMEM)]
        + [left if i in plain_in else spec(operand.shape) for i, operand in enumerate(operands) if i],
        out_specs=tuple(left if i in plain_out else spec(out[0]) for i, out in enumerate(outs)),
        scratch_shapes=scratch,
        compiler_params=pltpu.CompilerParams(vmem_limit_bytes=mib * 2**20),
    )(*operands)


def prepare_kernel(
    places, capacity, table_ref, buckets_ref, routes_ref, slots_ref,
    square_ref, tiled_ref, dispatch_ref, padded_ref,
):
    heads, count, _ = square_ref.shape
    turned = buckets_ref[...].astype(jnp.float32).T.astype(jnp.int32)
    wide = jnp.concatenate([turned, turned], axis=1)
    tiled_ref[...] = wide
    buckets = jnp.concatenate([wide, wide], axis=0)
    row = lax.broadcasted_iota(jnp.int32, (count, count), 0)
    column = lax.broadcasted_iota(jnp.int32, (count, count), 1)
    half = count // 2
    same = (row < half) == (column < half)
    for head in range(heads):
        total = jnp.where(same, 0.0, -jnp.inf)
        for bucket in range(table_ref.shape[0]):
            total = jnp.where(same & (buckets == bucket), table_ref[bucket, head], total)
        square_ref[head] = total
    routes = jnp.concatenate([routes_ref[0], routes_ref[1]], axis=1)
    slots = jnp.concatenate([slots_ref[0], slots_ref[1]], axis=1)
    second = lax.broadcasted_iota(jnp.int32, (1, count), 1) >= half
    at = slots + jnp.where(second, capacity, 0)
    chip = (routes & 1) * 8 + (routes >> 1)
    for ref, size in ((dispatch_ref, places), (padded_ref, 16)):
        flat = jnp.where(slots < capacity, chip * size + at, -1)
        rows = lax.broadcasted_iota(jnp.int32, ref.shape, 0)
        ref[...] = jnp.where(rows == flat, 1.0, 0.0).astype(jnp.bfloat16)


def attend_kernel(
    place_ref, x_ref, *rest,
):
    pieces, rest = rest[:6], rest[6:]
    (
        gain_one_ref, gain_two_ref, bias_ref, dispatch_ref, dy_ref,
        wt_qkv_ref, wt_o_ref, n1b_ref, qkv_ref, probs_ref, mixed_ref, resid_ref, n2b_ref, rows_ref,
        mixed_t, wt_ref, come, go_qkv, go_o,
    ) = rest
    core = place_ref[0]
    pairs = pieces[0].shape[0]
    for side, part in ((core, pieces[:3]), (1 - core, pieces[3:])):
        begin = 0
        for piece in part:
            size = piece.shape[2]
            pltpu.make_async_copy(
                piece, wt_ref.at[:, side, :, pl.ds(begin, size)], come
            ).start()
            begin += size
    heads = probs_ref.shape[0]
    width = x_ref.shape[1]
    size = width // heads
    x = x_ref[...].astype(jnp.float32)
    n1b_ref[...] = (x * rms_scale(x) * gain_one_ref[...]).astype(jnp.bfloat16)
    pltpu.make_async_copy(wt_ref, wt_ref, come).wait()
    most = pairs * 3 // 4
    leave_qkv = pltpu.make_async_copy(wt_ref.at[pl.ds(0, most)], wt_qkv_ref, go_qkv)
    leave_o = pltpu.make_async_copy(wt_ref.at[pl.ds(most, pairs - most)], wt_o_ref, go_o)
    leave_qkv.start()
    leave_o.start()
    qkv_ref[...] = dot(wt_ref[:most].reshape(3 * width, width), n1b_ref[...], ((1,), (1,))).astype(jnp.bfloat16)
    for head in range(heads):
        query = qkv_ref[head * size : (head + 1) * size]
        keys = qkv_ref[width + head * size : width + (head + 1) * size]
        values = qkv_ref[2 * width + head * size : 2 * width + (head + 1) * size]
        scores = dot(keys, query, ((0,), (0,))) + bias_ref[head]
        raised = jnp.exp(scores - jnp.max(scores, axis=0, keepdims=True))
        probs = raised / jnp.sum(raised, axis=0, keepdims=True)
        probs_ref[head] = probs
        mixed_t[head * size : (head + 1) * size] = dot(
            values, probs.astype(jnp.bfloat16), ((1,), (0,))
        )
    mixed_ref[...] = mixed_t[...].T.astype(jnp.bfloat16)
    resid = x + dot(
        mixed_ref[...], wt_ref[most:].reshape(width, width), ((1,), (1,))
    )
    resid_ref[...] = resid
    n2b_ref[...] = (resid * rms_scale(resid) * gain_two_ref[...]).astype(jnp.bfloat16)
    chips, places, _ = rows_ref.shape
    rows = dot(dispatch_ref[...], n2b_ref[...], ((1,), (0,))).reshape(chips, -1, width)
    rows_ref[:, :, :width] = rows[:, :places].astype(jnp.bfloat16)
    dy_rows = dot(dispatch_ref[...], dy_ref[...], ((1,), (0,))).reshape(chips, -1, width)
    rows_ref[:, :, width:] = dy_rows[:, :places].astype(jnp.bfloat16)
    leave_qkv.wait()
    leave_o.wait()


def attend_back_kernel(
    core_ref, dn2_ref, dispatch_ref, resid_ref, dy_ref, gain_two_ref, wt_ref, qkv_ref, probs_ref,
    n1b_ref, mixed_ref, dresid_ref, gain_ref, dqkv_ref, fold_ref, send_ref, keep_ref, columns,
):
    heads = probs_ref.shape[0]
    count, width = resid_ref.shape
    size = width // heads
    core = core_ref[0]
    resid = resid_ref[...]
    scale = rms_scale(resid)
    n2hat = resid * scale
    dn2 = dot(dispatch_ref[...], dn2_ref[:, :width], ((0,), (0,)))
    gain_ref[...] = jnp.sum(dn2 * n2hat, axis=0, keepdims=True)
    dhat = dn2 * gain_two_ref[...]
    dresid = dy_ref[...].astype(jnp.float32) + scale * (
        dhat - n2hat * jnp.mean(dhat * n2hat, axis=-1, keepdims=True)
    )
    dresid_ref[...] = dresid
    dattn = dresid.astype(jnp.bfloat16)
    dab = dot(dattn, wt_ref[...], ((1,), (0,)))
    dab_t = dab.T.astype(jnp.bfloat16)
    columns[3 * width :] = dresid.T.astype(jnp.bfloat16)
    for head in range(heads):
        at = slice(head * size, (head + 1) * size)
        query = qkv_ref[head * size : (head + 1) * size]
        keys = qkv_ref[width + head * size : width + (head + 1) * size]
        values = qkv_ref[2 * width + head * size : 2 * width + (head + 1) * size]
        dab_head = dab_t[at]
        probs = probs_ref[head]
        dvalue = dot(dab_head, probs.astype(jnp.bfloat16), ((1,), (1,)))
        dprobs = dot(values, dab_head, ((0,), (0,)))
        dscores = probs * (dprobs - jnp.sum(probs * dprobs, axis=0, keepdims=True))
        half = count // 2
        fold_ref[head] = dscores[:half] + dscores[half:]
        dscores_b = dscores.astype(jnp.bfloat16)
        dquery = dot(keys, dscores_b, ((1,), (0,)))
        dkey = dot(query, dscores_b, ((1,), (1,)))
        columns[head * size : (head + 1) * size] = dquery.astype(jnp.bfloat16)
        columns[width + head * size : width + (head + 1) * size] = dkey.astype(jnp.bfloat16)
        columns[2 * width + head * size : 2 * width + (head + 1) * size] = dvalue.astype(
            jnp.bfloat16
        )
    dqkv_ref[...] = columns[: 3 * width]
    block = width // 8
    sent = []
    for pair in range(16):
        theirs = pl.multiple_of((2 * pair + 1 - core) * block, block)
        mine = pl.multiple_of((2 * pair + core) * block, block)
        keep_ref[pair * block : (pair + 1) * block] = columns[pl.ds(mine, block), :]
        sent.append(columns[pl.ds(theirs, block), :])
    sent = jnp.concatenate(sent, axis=0)
    split = 12 * block
    send_ref[:split] = dot(sent[:split], n1b_ref[...], ((1,), (0,))).astype(jnp.bfloat16)
    send_ref[split:] = dot(sent[split:], mixed_ref[...], ((1,), (0,))).astype(jnp.bfloat16)


def token_back_kernel(
    bucket_count, _, x_ref, dqkv_ref, wt_ref, gain_one_ref, dresid_ref, fold_ref, buckets_ref, gain_part_ref,
    router_part_ref, grad_ref, small_ref,
):
    x = x_ref[...].astype(jnp.float32)
    scale = rms_scale(x)
    n1hat = x * scale
    width = x.shape[1]
    dn1 = dot(dqkv_ref[...], wt_ref[...], ((0,), (0,)))
    gain_part = jnp.sum(dn1 * n1hat, axis=0, keepdims=True)
    dhat = dn1 * gain_one_ref[...]
    grad_ref[...] = dresid_ref[...] + scale * (
        dhat - n1hat * jnp.mean(dhat * n1hat, axis=-1, keepdims=True)
    )
    experts = router_part_ref.shape[0]
    tiles = width // 128
    small_ref[...] = jnp.zeros(small_ref.shape, jnp.float32)
    for tile in range(tiles):
        at = slice(tile * 128, (tile + 1) * 128)
        small_ref[tile * experts : (tile + 1) * experts] = router_part_ref[:, at]
        base = tiles * experts + tile
        small_ref[base : base + 1] = gain_part[:, at]
        small_ref[base + 8 : base + 9] = gain_part_ref[:, at]
    heads = fold_ref.shape[0]
    lane = lax.broadcasted_iota(jnp.int32, (1, 128), 1)
    table = jnp.zeros((heads, 128), jnp.float32)
    buckets = buckets_ref[: fold_ref.shape[1]]
    fold = fold_ref[...]
    for bucket in range(bucket_count):
        column = jnp.sum(jnp.where((buckets == bucket)[None], fold, 0.0), axis=1)
        column = jnp.sum(column, axis=-1, keepdims=True)
        table = table + jnp.where(lane == bucket, column, 0.0)
    start = tiles * experts + 16
    small_ref[start : start + heads] = table


def split_kernel(
    place_ref, keep_ref, n1b_ref, mixed_ref, got_ref,
    send_a, send_b, send_c, keep_a, keep_b, keep_c, total,
):
    split = keep_ref.shape[0] * 3 // 4
    blocks, block, width = total.shape
    first = dot(keep_ref[:split], n1b_ref[...], ((1,), (0,)))
    first = first + got_ref[:split].astype(jnp.float32)
    total[: blocks * 3 // 4] = first.reshape(blocks * 3 // 4, block, width)
    last = dot(keep_ref[split:], mixed_ref[...], ((1,), (0,)))
    last = last + got_ref[split:].astype(jnp.float32)
    total[blocks * 3 // 4 :] = last.reshape(blocks // 4, block, width)
    begin = 0
    for index, (send, keep) in enumerate(((send_a, keep_a), (send_b, keep_b), (send_c, keep_c))):
        mine = place_ref[3 + index]
        stride = {2: 1, 4: 2, 8: 4, "y": 8}[RS_ORDERS[index][0]]
        columns = slice(begin, begin + send.shape[2])
        begin += send.shape[2]
        for j in range(blocks // 2):
            low = j // stride * 2 * stride + j % stride
            send[j] = total[low + (1 - mine) * stride, :, columns].astype(jnp.bfloat16)
            keep[j] = total[low + mine * stride, :, columns]


def expert_kernel(
    place_ref, own_ref, got_ref, router_ref,
    in_near_ref, in_arrived_ref, in_far_ref, out_near_ref, out_arrived_ref, out_far_ref,
    rows_ref, hidden_ref, du_ref, dmade_ref, mine_ref, theirs_ref, probs_ref, in_full, out_full,
):
    core, host = place_ref[0], place_ref[1]
    half, units = in_far_ref.shape
    own, width = got_ref.shape[0], got_ref.shape[1] // 2
    for side in range(2):

        at, other = slice(side * half, (side + 1) * half), slice((1 - side) * half, (2 - side) * half)

        @pl.when(core == side)
        def _():
            in_full[other] = in_far_ref[...]
            out_full[:, other] = out_far_ref[...]

        @pl.when((core == side) & (place_ref[2] == 1))
        def _():
            in_full[at] = in_near_ref[...]
            out_full[:, at] = out_near_ref[...]

        @pl.when((core == side) & (place_ref[2] == 0))
        def _():
            in_full[at] = in_arrived_ref[...]
            out_full[:, at] = out_arrived_ref[...]

    rows = jnp.concatenate([own_ref[:, :width], got_ref[:, :width]], axis=0)
    dy = jnp.concatenate([own_ref[:, width:], got_ref[:, width:]], axis=0)
    rows_ref[...] = rows
    logits = dot(rows, router_ref[...], ((1,), (0,)))
    raised = jnp.exp(logits - jnp.max(logits, axis=-1, keepdims=True))
    probs = raised / jnp.sum(raised, axis=-1, keepdims=True)
    probs_ref[...] = probs[:own]
    chosen = lax.broadcasted_iota(jnp.int32, probs.shape, 1) == host
    gate = jnp.sum(jnp.where(chosen, probs, 0.0), axis=-1, keepdims=True)
    dmade_ref[...] = (gate * dy.astype(jnp.float32)).astype(jnp.bfloat16)
    dmade = dmade_ref[...]
    made = jnp.zeros(rows.shape, jnp.float32)
    drows = jnp.zeros(rows.shape, jnp.float32)
    step = units // 3
    for begin in range(0, units, step):
        at = slice(begin, begin + step)
        upre = dot(rows, in_full[:, at], ((1,), (0,)))
        square = upre * upre
        bent = jnp.tanh(0.7978845608028654 * (upre + 0.044715 * upre * square))
        hidden = (0.5 * upre * (1.0 + bent)).astype(jnp.bfloat16)
        slope = 0.5 * (1.0 + bent) + 0.5 * upre * (1.0 - bent * bent) * (
            0.7978845608028654 * (1.0 + 3.0 * 0.044715 * square)
        )
        dhidden = dot(dmade, out_full[at, :], ((1,), (1,)))
        du = (dhidden * slope).astype(jnp.bfloat16)
        hidden_ref[:, at] = hidden
        du_ref[:, at] = du
        made = made + dot(hidden, out_full[at, :], ((1,), (0,)))
        drows = drows + dot(du, in_full[:, at], ((1,), (1,)))
    mine_ref[0] = made[:own]
    mine_ref[1] = drows[:own]
    theirs_ref[0] = made[own:]
    theirs_ref[1] = drows[own:]


def settle_kernel(
    place_ref, mine_ref, got_ref, own_ref, probs_ref, router_ref, back_ref, router_part_ref
):
    width = own_ref.shape[1] // 2
    chips, places, _ = back_ref.shape
    made = (mine_ref[0] + got_ref[0]).astype(jnp.bfloat16)
    row = lax.broadcasted_iota(jnp.int32, (chips * 16, made.shape[0]), 0)
    column = lax.broadcasted_iota(jnp.int32, row.shape, 1)
    spread = jnp.zeros(row.shape, jnp.float32)
    for chip in range(chips):
        inside = (row >= chip * 16) & (row < chip * 16 + places)
        spread = jnp.where(inside & (column == row - chip * (16 - places)), 1.0, spread)
    spread = spread.astype(jnp.bfloat16)

    def padded(values):
        wide = dot(spread, values, ((1,), (0,))).reshape(chips, 16, width)
        return wide[:, :places].astype(jnp.bfloat16)

    back_ref[:, :, width:] = padded(made)
    drows = (mine_ref[1] + got_ref[1]).astype(jnp.bfloat16).astype(jnp.float32)
    probs = probs_ref[...]
    chosen = (lax.broadcasted_iota(jnp.int32, probs.shape, 1) == place_ref[1]).astype(jnp.float32)
    gate = jnp.sum(probs * chosen, axis=-1, keepdims=True)
    dgate = jnp.sum(
        own_ref[:, width:].astype(jnp.float32) * made.astype(jnp.float32),
        axis=-1,
        keepdims=True,
    )
    dlogits = probs * dgate * (chosen - gate)
    router_part_ref[...] = dot(
        dlogits, own_ref[:, :width].astype(jnp.float32), ((0,), (0,)), precision=HIGH
    )
    dn2 = drows + dot(dlogits, router_ref[...].astype(jnp.float32), ((1,), (1,)), precision=HIGH)
    back_ref[:, :, :width] = padded(dn2.astype(jnp.bfloat16))


def paired_body(
    tokens,
    attn_weight,
    gain_attn,
    gain_expert,
    bias_table,
    router_weight,
    expert_in,
    expert_out,
    routes,
    slots,
    buckets,
    cotangent,
):
    f32, bf16 = jnp.float32, jnp.bfloat16
    micro, _, seq_len, width = tokens.shape
    count = micro * seq_len
    heads = bias_table.shape[1]
    head_size = width // heads
    bucket_count = bias_table.shape[0]
    experts = lax.axis_size("expert")
    capacity = (5 * seq_len + 4 * experts - 1) // (4 * experts)
    places = micro * capacity
    hidden_half = expert_in.shape[2] // 2
    width_half = width // 2
    dp_at, expert_at = lax.axis_index("dp"), lax.axis_index("expert")
    core = expert_at % 2
    home = core == dp_at
    host = expert_at - core + dp_at
    gain_one, gain_two = gain_attn.astype(f32), gain_expert.astype(f32)

    across, first = [], []
    for dp in range(2):
        for e in range(experts):
            here = dp * experts + e
            if e % 2 == dp:
                first.append((here, dp * experts + (e ^ 1), (1 - dp) * experts + e))
            else:
                across.append((here, (1 - dp) * experts + (e ^ 1)))
                first.append((here, (1 - dp) * experts + e, dp * experts + (e ^ 1)))
    outward = [(here, there) for here, there, _ in first]
    homeward = [(here, there) for here, _, there in first]

    groups = [
        [dp * experts + 2 * pair + side for dp in range(2) for pair in range(experts // 2)]
        for side in range(2)
    ]

    def to_chips(tensor):
        return lax.all_to_all(
            tensor, BOTH, split_axis=0, concat_axis=0, tiled=True, axis_index_groups=groups
        )

    row_count = experts * places
    upstream_b = cotangent.reshape(count, width)
    def parts_of(local, axis):
        near = lax.dynamic_slice_in_dim(local, dp_at * hidden_half, hidden_half, axis)
        far = lax.dynamic_slice_in_dim(local, (1 - dp_at) * hidden_half, hidden_half, axis)
        return near, far

    in_near, in_far = parts_of(expert_in[0], 1)
    def halves(tensor):
        return (
            lax.dynamic_slice_in_dim(tensor, core * width_half, width_half, 1),
            lax.dynamic_slice_in_dim(tensor, (1 - core) * width_half, width_half, 1),
        )

    def whole(keep, got, axis):
        low = core == 0
        return jnp.concatenate(
            [jnp.where(low, keep, got), jnp.where(low, got, keep)], axis=axis
        )

    def prepare(table, ids, route_ids, slot_ids, near, far, out_local):
        made = call(
            functools.partial(prepare_kernel, places, capacity),
            16,
            (
                ((heads, count, count), f32),
                ((seq_len, count), jnp.int32),
                ((row_count, count), bf16),
                ((experts * 16, count), bf16),
            ),
            [],
            table, ids, route_ids, slot_ids,
        )
        in_arrived = lax.ppermute(near, BOTH, across)
        in_far = lax.ppermute(far, BOTH, outward)
        return tuple(made) + (in_arrived, in_far) + parts_of(out_local, 0)

    pieces, ready = gather_rows(
        attn_weight.T,
        prepare,
        (bias_table.astype(f32), buckets, routes, slots, in_near, in_far, expert_out[0]),
    )
    square, tiled, dispatch, padded, in_arrived, in_far, out_near, out_far = ready
    out_arrived = lax.ppermute(out_near, BOTH, across)
    place = jnp.stack(
        [core, host, home.astype(jnp.int32)] + [own_bit(order[0]) for order in RS_ORDERS]
    ).astype(jnp.int32)
    gain_one, gain_two = gain_one[None], gain_two[None]
    local = tokens.reshape(count, width)
    wt_qkv, wt_o, n1b, qkv, probs, mixed_b, resid, n2b, outgoing = call(
        attend_kernel,
        26,
        (
            ((12, 2, width // 8, width), bf16),
            ((4, 2, width // 8, width), bf16),
            ((count, width), bf16),
            ((3 * width, count), bf16),
            ((heads, count, count), f32),
            ((count, width), bf16),
            ((count, width), f32),
            ((count, width), bf16),
            ((experts, places, 2 * width), bf16),
        ),
        [
            pltpu.VMEM((width, count), f32),
            pltpu.VMEM((16, 2, width // 8, width), bf16),
            pltpu.SemaphoreType.DMA,
            pltpu.SemaphoreType.DMA,
            pltpu.SemaphoreType.DMA,
        ],
        place, local, *pieces, gain_one, gain_two, square, padded, upstream_b,
        plain_in=range(2, 8),
        plain_out=(0, 1),
    )
    wt_qkv, wt_o = wt_qkv.reshape(3 * width, width), wt_o.reshape(width, width)
    outgoing, out_arrived, out_far = lax.optimization_barrier((outgoing, out_arrived, out_far))
    own_rows = to_chips(outgoing).reshape(row_count, 2 * width)
    in_parts = (in_near, in_arrived, in_far)
    out_parts = (out_near, out_arrived, lax.ppermute(out_far, BOTH, outward))
    rows, hidden, du, dmade, mine, theirs, row_probs = call(
        expert_kernel,
        34,
        (
            ((2 * row_count, width), bf16),
            ((2 * row_count, hidden_half), bf16),
            ((2 * row_count, hidden_half), bf16),
            ((2 * row_count, width), bf16),
            ((2, row_count, width), f32),
            ((2, row_count, width), f32),
            ((row_count, experts), f32),
        ),
        [pltpu.VMEM((width, hidden_half), bf16), pltpu.VMEM((hidden_half, width), bf16)],
        place, own_rows, flip(own_rows, 1), router_weight, *in_parts, *out_parts,
    )
    back_rows, router_part = call(
        settle_kernel,
        10,
        (
            ((experts, places, 2 * width), bf16),
            ((experts, width), f32),
        ),
        [],
        place, mine, flip(theirs, 1), own_rows, row_probs, router_weight,
    )
    in_other = dot(halves(rows)[1], du, ((0,), (0,))).astype(bf16)
    back_rows, rows, hidden, du, dmade = lax.optimization_barrier(
        (back_rows, rows, hidden, du, dmade)
    )
    home_rows = to_chips(back_rows).reshape(row_count, 2 * width)
    rows_keep, _ = halves(rows)
    dmade_keep, dmade_got = halves(dmade)

    in_homely = lax.ppermute(in_other, BOTH, homeward)
    in_mine = dot(rows_keep, du, ((0,), (0,)))
    out_other = dot(hidden, dmade_got, ((0,), (0,))).astype(bf16)
    out_homely = lax.ppermute(out_other, BOTH, homeward)
    out_mine = dot(hidden, dmade_keep, ((0,), (0,)))
    home_rows, in_homely, out_homely, in_leave, out_leave = lax.optimization_barrier(
        (home_rows, in_homely, out_homely, in_mine.astype(bf16), out_mine.astype(bf16))
    )
    in_arrived = lax.ppermute(in_leave, BOTH, across)
    out_arrived = lax.ppermute(out_leave, BOTH, across)

    dresid, gain_two_part, dqkv, fold, send, keep = call(
        attend_back_kernel,
        26,
        (
            ((count, width), f32),
            ((1, width), f32),
            ((3 * width, count), bf16),
            ((heads, count // 2, count), f32),
            ((2 * width, width), bf16),
            ((2 * width, count), bf16),
        ),
        [pltpu.VMEM((4 * width, count), bf16)],
        place, home_rows, dispatch, resid, upstream_b, gain_two, wt_o, qkv, probs, n1b, mixed_b,
    )
    got = flip(send, 1)
    small_rows = (width // 128) * experts + 16 + (heads + 7) // 8 * 8
    token_grad, small = call(
        functools.partial(token_back_kernel, bucket_count),
        26,
        (
            ((count, width), f32),
            ((small_rows, 128), f32),
        ),
        [],
        place, local, dqkv, wt_qkv, gain_one, dresid, fold, tiled, gain_two_part,
        router_part,
    )
    block = width // 8
    pieces = (width // 2, width // 3, width // 6)
    cut = call(
        split_kernel,
        30,
        tuple(((8, block, piece), bf16) for piece in pieces)
        + tuple(((8, block, piece), f32) for piece in pieces),
        [pltpu.VMEM((16, block, width), f32)],
        place, keep, n1b, mixed_b, got,
    )
    attn_share, small, late = scatter_rows(
        cut[:3],
        cut[3:],
        small,
        (
            (),
            (in_arrived, in_mine, in_homely),
            (out_arrived, out_mine, out_homely),
            (home_rows, routes),
        ),
    )
    _, in_late, out_late, (home_rows, routes) = late
    route_ids = routes[:, 0]
    in_arrived, in_mine, in_homely = in_late
    out_arrived, out_mine, out_homely = out_late
    in_back = (in_mine, in_homely, in_arrived)
    out_back = (out_mine, out_homely, out_arrived)

    def settled(parts, axis):
        near, homely, arrived = parts
        mine = jnp.where(home, near, homely.astype(f32))
        other = jnp.where(home, homely.astype(f32), arrived.astype(f32))
        return whole(mine, other, axis)

    in_share, out_share = settled(in_back, 1), settled(out_back, 0)
    router_probs = jax.nn.softmax(dot(n2b, router_weight, ((1,), (0,))), axis=-1)
    picked = (route_ids.reshape(count, 1) == jnp.arange(experts)).astype(f32)
    gate = jnp.sum(router_probs * picked, axis=-1, keepdims=True)
    returned = dot(dispatch, home_rows[:, width:], ((0,), (0,)))
    output = (resid + gate * returned).astype(bf16)

    attn_share = attn_share.T
    routed = (width // 128) * experts
    return (
        output.reshape(tokens.shape),
        token_grad.reshape(tokens.shape),
        attn_share,
        small[routed : routed + width // 128].reshape(width),
        small[routed + 8 : routed + 8 + width // 128].reshape(width),
        small[routed + 16 : routed + 16 + heads, :bucket_count].T,
        jnp.transpose(small[:routed].reshape(-1, experts, 128), (0, 2, 1)).reshape(width, experts),
        in_share[None],
        out_share[None],
    )


def solution(mesh):
    paired = mesh.shape["dp"] == 2 and mesh.shape["expert"] == 16
    chosen = paired_body if paired else body
    placed = (
        P(None, ("dp", "expert"), None, None),
        P(None, ("dp", "expert")),
        P(),
        P(),
        P(),
        P(),
        P("expert", "dp", None),
        P("expert", None, "dp"),
        P(None, ("dp", "expert"), None),
        P(None, ("dp", "expert"), None),
        P(),
        P(None, ("dp", "expert"), None, None),
    )
    return jax.shard_map(
        chosen,
        mesh=mesh,
        in_specs=placed,
        out_specs=(
            P(None, ("dp", "expert"), None, None),
            P(None, ("dp", "expert"), None, None),
            P(None, ("dp", "expert")),
            P(),
            P(),
            P(),
            P(),
            P("expert", "dp", None),
            P("expert", None, "dp"),
        ),
        check_vma=False,
    )
```

```python
import functools
import jax
import jax.numpy as jnp
from jax import lax
from jax.experimental import pallas as pl
from jax.experimental.pallas import tpu as pltpu
from jax.sharding import PartitionSpec as P

EPSILON = 1e-06
HIGH = lax.Precision.HIGHEST


def smooth_gate(values):
    return jax.nn.gelu(values, approximate=True)


def rms_scale(values):
    return lax.rsqrt(jnp.mean(values * values, axis=-1, keepdims=True) + EPSILON)


def body(
    tokens,
    attn_weight,
    gain_attn,
    gain_expert,
    bias_table,
    router_weight,
    expert_in,
    expert_out,
    routes,
    slots,
    buckets,
    cotangent,
):
    micro = tokens.shape[0]
    seq_len = tokens.shape[2]
    width = tokens.shape[3]
    heads = bias_table.shape[1]
    head_size = width // heads
    bucket_count = bias_table.shape[0]
    local_experts = expert_in.shape[0]
    expert_devices = lax.axis_size("expert")
    total_experts = local_experts * expert_devices
    capacity = (5 * seq_len + 4 * total_experts - 1) // (4 * total_experts)
    slot_total = total_experts * capacity
    gain_one = gain_attn.astype(jnp.float32)
    gain_two = gain_expert.astype(jnp.float32)
    router_full = router_weight.astype(jnp.float32)
    bucket_hot = (buckets[:, :, None] == jnp.arange(bucket_count)).astype(jnp.float32)
    bias_term = jnp.einsum(
        "ijb,bh->hij", bucket_hot, bias_table.astype(jnp.float32), precision=HIGH
    )

    def to_experts(tensor):
        tensor = tensor.reshape(expert_devices, local_experts, capacity, width)
        return jnp.transpose(tensor, (1, 0, 2, 3)).reshape(
            local_experts, expert_devices * capacity, width
        )

    def from_experts(tensor):
        tensor = tensor.reshape(local_experts, expert_devices, capacity, width)
        return jnp.transpose(tensor, (1, 0, 2, 3)).reshape(total_experts, capacity, width)

    gain_one_total = jnp.zeros((width,), jnp.float32)
    gain_two_total = jnp.zeros((width,), jnp.float32)
    bias_total = jnp.zeros((bucket_count, heads), jnp.float32)
    router_total = jnp.zeros((width, total_experts), jnp.float32)
    results = []
    token_grads = []
    kept_rows = []
    kept_hidden = []
    kept_dmade = []
    kept_dpre = []
    kept_mixed = []
    kept_dattn = []
    kept_normed = []
    kept_dqkv = []
    for micro_index in range(micro):
        inputs = tokens[micro_index, 0].astype(jnp.float32)
        full_attn = lax.all_gather(attn_weight, ("dp", "expert"), axis=1, tiled=True)
        scale_one = rms_scale(inputs)
        n1hat = inputs * scale_one
        n1b = (n1hat * gain_one).astype(jnp.bfloat16)
        qkv = jnp.dot(n1b, full_attn[:, : 3 * width], preferred_element_type=jnp.float32).astype(
            jnp.bfloat16
        )
        query = qkv[:, :width].reshape(seq_len, heads, head_size)
        key_part = qkv[:, width : 2 * width].reshape(seq_len, heads, head_size)
        value_part = qkv[:, 2 * width :].reshape(seq_len, heads, head_size)
        scores = (
            jnp.einsum("ihd,jhd->hij", query, key_part, preferred_element_type=jnp.float32)
            + bias_term
        )
        log_total = jax.nn.logsumexp(scores, axis=-1, keepdims=True)
        probs_b = jnp.exp(scores - log_total).astype(jnp.bfloat16)
        mixed = jnp.einsum("hij,jhd->ihd", probs_b, value_part, preferred_element_type=jnp.float32)
        mixed_b = mixed.reshape(seq_len, width).astype(jnp.bfloat16)
        resid = inputs + jnp.dot(
            mixed_b, full_attn[:, 3 * width :], preferred_element_type=jnp.float32
        )
        scale_two = rms_scale(resid)
        n2hat = resid * scale_two
        n2b = (n2hat * gain_two).astype(jnp.bfloat16)
        logits = jnp.dot(n2b, router_weight, preferred_element_type=jnp.float32)
        router_probs = jax.nn.softmax(logits, axis=-1)
        route_ids = routes[micro_index, 0]
        slot_ids = slots[micro_index, 0]
        picked = (route_ids[:, None] == jnp.arange(total_experts)).astype(jnp.float32)
        gate = jnp.sum(router_probs * picked, axis=-1)
        flat = route_ids * capacity + slot_ids
        dispatch = (
            (flat[:, None] == jnp.arange(slot_total)) & (slot_ids[:, None] < capacity)
        ).astype(jnp.bfloat16)
        outgoing = jnp.einsum(
            "sk,sd->kd", dispatch, n2b, preferred_element_type=jnp.float32
        ).astype(jnp.bfloat16)
        arrived = lax.all_to_all(
            outgoing.reshape(total_experts, capacity, width),
            "expert",
            split_axis=0,
            concat_axis=0,
            tiled=True,
        )
        expert_rows = to_experts(arrived)
        full_in, full_out = (
            lax.all_gather(expert_in, "dp", axis=1, tiled=True),
            lax.all_gather(expert_out, "dp", axis=2, tiled=True),
        )
        hidden_pre = jnp.einsum(
            "erd,edf->erf", expert_rows, full_in, preferred_element_type=jnp.float32
        )
        hidden = smooth_gate(hidden_pre).astype(jnp.bfloat16)
        made = jnp.einsum(
            "erf,efd->erd", hidden, full_out, preferred_element_type=jnp.float32
        ).astype(jnp.bfloat16)
        kept_rows.append(expert_rows)
        kept_hidden.append(hidden)
        came_back = lax.all_to_all(
            from_experts(made), "expert", split_axis=0, concat_axis=0, tiled=True
        )
        returned = jnp.einsum(
            "sk,kd->sd",
            dispatch,
            came_back.reshape(slot_total, width),
            preferred_element_type=jnp.float32,
        )
        results.append((resid + gate[:, None] * returned).astype(jnp.bfloat16))
        upstream = cotangent[micro_index, 0].astype(jnp.float32)
        dgate = jnp.sum(upstream * returned, axis=-1)
        dreturned = (gate[:, None] * upstream).astype(jnp.bfloat16)
        dslots = jnp.einsum(
            "sk,sd->kd", dispatch, dreturned, preferred_element_type=jnp.float32
        ).astype(jnp.bfloat16)
        dmade = to_experts(
            lax.all_to_all(
                dslots.reshape(total_experts, capacity, width),
                "expert",
                split_axis=0,
                concat_axis=0,
                tiled=True,
            )
        )
        back_attn = lax.all_gather(attn_weight, ("dp", "expert"), axis=1, tiled=True)
        back_in, back_out = (
            lax.all_gather(expert_in, "dp", axis=1, tiled=True),
            lax.all_gather(expert_out, "dp", axis=2, tiled=True),
        )
        dhidden = jnp.einsum("erd,efd->erf", dmade, back_out, preferred_element_type=jnp.float32)
        dpre = jax.vjp(smooth_gate, hidden_pre)[1](dhidden)[0].astype(jnp.bfloat16)
        kept_dmade.append(dmade)
        kept_dpre.append(dpre)
        drows = jnp.einsum(
            "erf,edf->erd", dpre, back_in, preferred_element_type=jnp.float32
        ).astype(jnp.bfloat16)
        drows_home = lax.all_to_all(
            from_experts(drows), "expert", split_axis=0, concat_axis=0, tiled=True
        )
        dnormed = jnp.einsum(
            "sk,kd->sd",
            dispatch,
            drows_home.reshape(slot_total, width),
            preferred_element_type=jnp.float32,
        )
        dpick = picked * dgate[:, None]
        dlogits = router_probs * (dpick - jnp.sum(router_probs * dpick, axis=-1, keepdims=True))
        router_total = router_total + jnp.dot(n2b.astype(jnp.float32).T, dlogits, precision=HIGH)
        dnormed = dnormed + jnp.dot(dlogits, router_full.T, precision=HIGH)
        gain_two_total = gain_two_total + jnp.sum(dnormed * n2hat, axis=0)
        dhat_two = dnormed * gain_two
        dresid = upstream + scale_two * (
            dhat_two - n2hat * jnp.mean(dhat_two * n2hat, axis=-1, keepdims=True)
        )
        dattn = dresid.astype(jnp.bfloat16)
        dmixed = jnp.einsum(
            "se,de->sd", dattn, back_attn[:, 3 * width :], preferred_element_type=jnp.float32
        )
        dmixed = dmixed.astype(jnp.bfloat16).reshape(seq_len, heads, head_size)
        again_scores = (
            jnp.einsum("ihd,jhd->hij", query, key_part, preferred_element_type=jnp.float32)
            + bias_term
        )
        probs = jnp.exp(again_scores - log_total)
        again_b = probs.astype(jnp.bfloat16)
        dvalue = jnp.einsum("hij,ihd->jhd", again_b, dmixed, preferred_element_type=jnp.float32)
        dprobs = jnp.einsum("ihd,jhd->hij", dmixed, value_part, preferred_element_type=jnp.float32)
        dscores = probs * (dprobs - jnp.sum(probs * dprobs, axis=-1, keepdims=True))
        bias_total = bias_total + jnp.einsum("hij,ijb->bh", dscores, bucket_hot, precision=HIGH)
        dscores_b = dscores.astype(jnp.bfloat16)
        dquery = jnp.einsum("hij,jhd->ihd", dscores_b, key_part, preferred_element_type=jnp.float32)
        dkey = jnp.einsum("hij,ihd->jhd", dscores_b, query, preferred_element_type=jnp.float32)
        dqkv = jnp.concatenate(
            [
                dquery.reshape(seq_len, width),
                dkey.reshape(seq_len, width),
                dvalue.reshape(seq_len, width),
            ],
            axis=1,
        ).astype(jnp.bfloat16)
        kept_mixed.append(mixed_b)
        kept_dattn.append(dattn)
        kept_normed.append(n1b)
        kept_dqkv.append(dqkv)
        dnormed_one = jnp.einsum(
            "se,de->sd", dqkv, back_attn[:, : 3 * width], preferred_element_type=jnp.float32
        )
        gain_one_total = gain_one_total + jnp.sum(dnormed_one * n1hat, axis=0)
        dhat_one = dnormed_one * gain_one
        token_grads.append(
            dresid
            + scale_one * (dhat_one - n1hat * jnp.mean(dhat_one * n1hat, axis=-1, keepdims=True))
        )
    normed_all = jnp.concatenate(kept_normed, axis=0)
    dqkv_all = jnp.concatenate(kept_dqkv, axis=0)
    mixed_all = jnp.concatenate(kept_mixed, axis=0)
    dattn_all = jnp.concatenate(kept_dattn, axis=0)
    dqkv_proj = jnp.einsum("sd,se->de", normed_all, dqkv_all, preferred_element_type=jnp.float32)
    dout_proj = jnp.einsum("sd,se->de", mixed_all, dattn_all, preferred_element_type=jnp.float32)
    attn_total = jnp.concatenate([dqkv_proj, dout_proj], axis=1)
    attn_share = lax.psum_scatter(attn_total, ("dp", "expert"), scatter_dimension=1, tiled=True)
    rows_all = jnp.concatenate(kept_rows, axis=1)
    hidden_all = jnp.concatenate(kept_hidden, axis=1)
    dmade_cat = jnp.concatenate(kept_dmade, axis=1)
    dpre_all = jnp.concatenate(kept_dpre, axis=1)
    in_total = jnp.einsum("erd,erf->edf", rows_all, dpre_all, preferred_element_type=jnp.float32)
    out_turned_total = jnp.einsum(
        "erd,erf->edf", dmade_cat, hidden_all, preferred_element_type=jnp.float32
    )
    in_share, out_turned_share = (
        lax.psum_scatter(
            in_total.astype(jnp.bfloat16), "dp", scatter_dimension=1, tiled=True
        ).astype(jnp.float32),
        lax.psum_scatter(
            out_turned_total.astype(jnp.bfloat16), "dp", scatter_dimension=1, tiled=True
        ).astype(jnp.float32),
    )
    out_share = jnp.transpose(out_turned_share, (0, 2, 1))
    gain_one_sum, gain_two_sum, bias_sum, router_sum = lax.psum(
        (gain_one_total, gain_two_total, bias_total, router_total), ("dp", "expert")
    )
    output = jnp.stack(results)[:, None]
    token_grad = jnp.stack(token_grads)[:, None]
    return (
        output,
        token_grad,
        attn_share,
        gain_one_sum,
        gain_two_sum,
        bias_sum,
        router_sum,
        in_share,
        out_share,
    )


BOTH = ("dp", "expert")


def flip(tensor, bit):
    if bit == "y":
        return lax.ppermute(tensor, "dp", [(0, 1), (1, 0)])
    count = lax.axis_size("expert")
    return lax.ppermute(tensor, "expert", [(i, i ^ bit) for i in range(count)])


def own_bit(bit):
    if bit == "y":
        return lax.axis_index("dp")
    return (lax.axis_index("expert") // bit) % 2


ORDERS = (("y", 2, 8, 4), (2, "y", 8, 4), (8, "y", 4, 2))
RS_ORDERS = ((8, 4, 2, "y"), ("y", 8, 4, 2), (2, "y", 8, 4))
PLACE = {"y": 0, 8: 1, 4: 2, 2: 3, 1: 4}


def gather_rows(shard, prepare, waiting, divide, last):
    rows, width = shard.shape
    pieces, begin = [], 0
    for size in (width // 3, width // 6, width // 2):
        piece = shard[:, begin : begin + size]
        pieces.append(piece.reshape(1, 1, 1, 1, rows, size))
        begin += size

    def grow(piece, bit):
        got = flip(piece, bit)
        low = own_bit(bit) == 0
        return jnp.concatenate(
            [jnp.where(low, piece, got), jnp.where(low, got, piece)], axis=PLACE[bit]
        )

    for step in range(4):
        if step == 2:
            pieces, waiting = lax.optimization_barrier((pieces, waiting))
            ready = prepare(*waiting)
        if step == 3:
            pieces, last = lax.optimization_barrier((pieces, last))
            last = divide(last, 0)
        pieces = [grow(piece, ORDERS[i][step]) for i, piece in enumerate(pieces)]
    pieces, ready, last = lax.optimization_barrier((pieces, ready, last))
    pieces = [piece.reshape(-1, rows, piece.shape[-1]) for piece in pieces]
    return pieces + [flip(piece, 1) for piece in pieces], ready, last


def reduce_step(total, bit):
    mine = own_bit(bit)
    axis = PLACE[bit]
    send = lax.dynamic_index_in_dim(total, 1 - mine, axis, keepdims=True).astype(jnp.bfloat16)
    keep = lax.dynamic_index_in_dim(total, mine, axis, keepdims=True)
    return keep + flip(send, bit).astype(jnp.float32)


def scatter_rows(leaves, stays, small, late):
    late = list(late)
    pieces = []
    for index, (leave, stay) in enumerate(zip(leaves, stays)):
        bit = RS_ORDERS[index][0]
        shape = [2, 2, 2, 2, 1] + list(stay.shape[1:])
        shape[PLACE[bit]] = 1
        pieces.append((stay + flip(leave, bit).astype(jnp.float32)).reshape(shape))
    for bit in (1, 2):
        small = small + flip(small, bit)
    for step in range(1, 4):
        pieces, late[step], small = lax.optimization_barrier((pieces, late[step], small))
        pieces = [reduce_step(piece, RS_ORDERS[i][step]) for i, piece in enumerate(pieces)]
        small = small + flip(small, ("y", 8, 4)[step - 1])
    whole = jnp.concatenate(pieces, axis=-1)
    return whole.reshape(whole.shape[-2], whole.shape[-1]), small, late


def dot(left, right, dims, **more):
    return lax.dot_general(
        left, right, (dims, ((), ())), preferred_element_type=jnp.float32, **more
    )


def call(kernel, mib, outs, scratch, *operands, plain_in=(), plain_out=(), free=()):
    def spec(shape):
        return pl.BlockSpec(
            shape, lambda i: (0,) * len(shape), pipeline_mode=pl.Buffered(1)
        )

    left = pl.BlockSpec(memory_space=pl.ANY)
    operands = operands[:1] + tuple(
        operand if i in free else pltpu.with_memory_space_constraint(operand, pltpu.HBM)
        for i, operand in enumerate(operands)
        if i
    )
    return pl.pallas_call(
        kernel,
        grid=(1,),
        out_shape=tuple(pltpu.HBM(*out) for out in outs),
        in_specs=[pl.BlockSpec(memory_space=pltpu.SMEM)]
        + [left if i in plain_in else spec(operand.shape) for i, operand in enumerate(operands) if i],
        out_specs=tuple(left if i in plain_out else spec(out[0]) for i, out in enumerate(outs)),
        scratch_shapes=scratch,
        compiler_params=pltpu.CompilerParams(vmem_limit_bytes=mib * 2**20),
    )(*operands)


def prepare_kernel(
    places, capacity, table_ref, buckets_ref, routes_ref, slots_ref,
    square_ref, tiled_ref, dispatch_ref, padded_ref,
):
    heads, count, _ = square_ref.shape
    turned = buckets_ref[...].astype(jnp.float32).T.astype(jnp.int32)
    wide = jnp.concatenate([turned, turned], axis=1)
    tiled_ref[...] = wide
    buckets = jnp.concatenate([wide, wide], axis=0)
    row = lax.broadcasted_iota(jnp.int32, (count, count), 0)
    column = lax.broadcasted_iota(jnp.int32, (count, count), 1)
    half = count // 2
    same = (row < half) == (column < half)
    for head in range(heads):
        total = jnp.where(same, 0.0, -jnp.inf)
        for bucket in range(table_ref.shape[0]):
            total = jnp.where(same & (buckets == bucket), table_ref[bucket, head], total)
        square_ref[head] = total
    routes = jnp.concatenate([routes_ref[0], routes_ref[1]], axis=1)
    slots = jnp.concatenate([slots_ref[0], slots_ref[1]], axis=1)
    second = lax.broadcasted_iota(jnp.int32, (1, count), 1) >= half
    at = slots + jnp.where(second, capacity, 0)
    chip = (routes & 1) * 8 + (routes >> 1)
    for ref, size in ((dispatch_ref, places), (padded_ref, 16)):
        flat = jnp.where(slots < capacity, chip * size + at, -1)
        rows = lax.broadcasted_iota(jnp.int32, ref.shape, 0)
        ref[...] = jnp.where(rows == flat, 1.0, 0.0).astype(jnp.bfloat16)


def attend_kernel(
    place_ref, x_ref, *rest,
):
    pieces, rest = rest[:6], rest[6:]
    (
        gain_one_ref, gain_two_ref, bias_ref, dispatch_ref, dy_ref,
        wt_qkv_ref, wt_o_ref, n1b_ref, qkv_ref, probs_ref, mixed_ref, resid_ref, n2b_ref, rows_ref,
        mixed_t, wt_ref, come, go_qkv, go_o,
    ) = rest
    core = place_ref[0]
    pairs = pieces[0].shape[0]
    for side, part in ((core, pieces[:3]), (1 - core, pieces[3:])):
        begin = 0
        for piece in part:
            size = piece.shape[2]
            pltpu.make_async_copy(
                piece, wt_ref.at[:, side, :, pl.ds(begin, size)], come
            ).start()
            begin += size
    heads = probs_ref.shape[0]
    width = x_ref.shape[1]
    size = width // heads
    x = x_ref[...].astype(jnp.float32)
    n1b_ref[...] = (x * rms_scale(x) * gain_one_ref[...]).astype(jnp.bfloat16)
    pltpu.make_async_copy(wt_ref, wt_ref, come).wait()
    most = pairs * 3 // 4
    leave_qkv = pltpu.make_async_copy(wt_ref.at[pl.ds(0, most)], wt_qkv_ref, go_qkv)
    leave_o = pltpu.make_async_copy(wt_ref.at[pl.ds(most, pairs - most)], wt_o_ref, go_o)
    leave_qkv.start()
    leave_o.start()
    qkv_ref[...] = dot(wt_ref[:most].reshape(3 * width, width), n1b_ref[...], ((1,), (1,))).astype(jnp.bfloat16)
    for head in range(heads):
        query = qkv_ref[head * size : (head + 1) * size]
        keys = qkv_ref[width + head * size : width + (head + 1) * size]
        values = qkv_ref[2 * width + head * size : 2 * width + (head + 1) * size]
        scores = dot(keys, query, ((0,), (0,))) + bias_ref[head]
        raised = jnp.exp(scores - jnp.max(scores, axis=0, keepdims=True))
        probs = raised / jnp.sum(raised, axis=0, keepdims=True)
        probs_ref[head] = probs
        mixed_t[head * size : (head + 1) * size] = dot(
            values, probs.astype(jnp.bfloat16), ((1,), (0,))
        )
    mixed_ref[...] = mixed_t[...].T.astype(jnp.bfloat16)
    resid = x + dot(
        mixed_ref[...], wt_ref[most:].reshape(width, width), ((1,), (1,))
    )
    resid_ref[...] = resid
    n2b_ref[...] = (resid * rms_scale(resid) * gain_two_ref[...]).astype(jnp.bfloat16)
    chips, places, _ = rows_ref.shape
    rows = dot(dispatch_ref[...], n2b_ref[...], ((1,), (0,))).reshape(chips, -1, width)
    rows_ref[:, :, :width] = rows[:, :places].astype(jnp.bfloat16)
    dy_rows = dot(dispatch_ref[...], dy_ref[...], ((1,), (0,))).reshape(chips, -1, width)
    rows_ref[:, :, width:] = dy_rows[:, :places].astype(jnp.bfloat16)
    leave_qkv.wait()
    leave_o.wait()


def attend_back_kernel(
    core_ref, dn2_ref, dispatch_ref, resid_ref, dy_ref, gain_two_ref, wt_ref, qkv_ref, probs_ref,
    n1b_ref, mixed_ref, dresid_ref, gain_ref, dqkv_ref, fold_ref, send_ref, keep_ref, columns,
):
    heads = probs_ref.shape[0]
    count, width = resid_ref.shape
    size = width // heads
    core = core_ref[0]
    resid = resid_ref[...]
    scale = rms_scale(resid)
    n2hat = resid * scale
    dn2 = dot(dispatch_ref[...], dn2_ref[:, :width], ((0,), (0,)))
    gain_ref[...] = jnp.sum(dn2 * n2hat, axis=0, keepdims=True)
    dhat = dn2 * gain_two_ref[...]
    dresid = dy_ref[...].astype(jnp.float32) + scale * (
        dhat - n2hat * jnp.mean(dhat * n2hat, axis=-1, keepdims=True)
    )
    dresid_ref[...] = dresid
    dattn = dresid.astype(jnp.bfloat16)
    dab = dot(dattn, wt_ref[...], ((1,), (0,)))
    dab_t = dab.T.astype(jnp.bfloat16)
    columns[3 * width :] = dresid.T.astype(jnp.bfloat16)
    for head in range(heads):
        at = slice(head * size, (head + 1) * size)
        query = qkv_ref[head * size : (head + 1) * size]
        keys = qkv_ref[width + head * size : width + (head + 1) * size]
        values = qkv_ref[2 * width + head * size : 2 * width + (head + 1) * size]
        dab_head = dab_t[at]
        probs = probs_ref[head]
        dvalue = dot(dab_head, probs.astype(jnp.bfloat16), ((1,), (1,)))
        dprobs = dot(values, dab_head, ((0,), (0,)))
        dscores = probs * (dprobs - jnp.sum(probs * dprobs, axis=0, keepdims=True))
        half = count // 2
        fold_ref[head] = dscores[:half] + dscores[half:]
        dscores_b = dscores.astype(jnp.bfloat16)
        dquery = dot(keys, dscores_b, ((1,), (0,)))
        dkey = dot(query, dscores_b, ((1,), (1,)))
        columns[head * size : (head + 1) * size] = dquery.astype(jnp.bfloat16)
        columns[width + head * size : width + (head + 1) * size] = dkey.astype(jnp.bfloat16)
        columns[2 * width + head * size : 2 * width + (head + 1) * size] = dvalue.astype(
            jnp.bfloat16
        )
    dqkv_ref[...] = columns[: 3 * width]
    block = width // 8
    sent = []
    for pair in range(16):
        theirs = pl.multiple_of((2 * pair + 1 - core) * block, block)
        mine = pl.multiple_of((2 * pair + core) * block, block)
        keep_ref[pair * block : (pair + 1) * block] = columns[pl.ds(mine, block), :]
        sent.append(columns[pl.ds(theirs, block), :])
    sent = jnp.concatenate(sent, axis=0)
    split = 12 * block
    send_ref[:split] = dot(sent[:split], n1b_ref[...], ((1,), (0,))).astype(jnp.bfloat16)
    send_ref[split:] = dot(sent[split:], mixed_ref[...], ((1,), (0,))).astype(jnp.bfloat16)


def token_back_kernel(
    bucket_count, _, x_ref, dqkv_ref, wt_ref, gain_one_ref, dresid_ref, fold_ref, buckets_ref, gain_part_ref,
    router_part_ref, grad_ref, small_ref,
):
    x = x_ref[...].astype(jnp.float32)
    scale = rms_scale(x)
    n1hat = x * scale
    width = x.shape[1]
    dn1 = dot(dqkv_ref[...], wt_ref[...], ((0,), (0,)))
    gain_part = jnp.sum(dn1 * n1hat, axis=0, keepdims=True)
    dhat = dn1 * gain_one_ref[...]
    grad_ref[...] = dresid_ref[...] + scale * (
        dhat - n1hat * jnp.mean(dhat * n1hat, axis=-1, keepdims=True)
    )
    experts = router_part_ref.shape[0]
    tiles = width // 128
    small_ref[...] = jnp.zeros(small_ref.shape, jnp.float32)
    for tile in range(tiles):
        at = slice(tile * 128, (tile + 1) * 128)
        small_ref[tile * experts : (tile + 1) * experts] = router_part_ref[:, at]
        base = tiles * experts + tile
        small_ref[base : base + 1] = gain_part[:, at]
        small_ref[base + 8 : base + 9] = gain_part_ref[:, at]
    heads = fold_ref.shape[0]
    lane = lax.broadcasted_iota(jnp.int32, (1, 128), 1)
    table = jnp.zeros((heads, 128), jnp.float32)
    buckets = buckets_ref[: fold_ref.shape[1]]
    fold = fold_ref[...]
    for bucket in range(bucket_count):
        column = jnp.sum(jnp.where((buckets == bucket)[None], fold, 0.0), axis=1)
        column = jnp.sum(column, axis=-1, keepdims=True)
        table = table + jnp.where(lane == bucket, column, 0.0)
    start = tiles * experts + 16
    small_ref[start : start + heads] = table


def split_kernel(
    place_ref, keep_ref, n1b_ref, mixed_ref, got_ref,
    send_a, send_b, send_c, keep_a, keep_b, keep_c, total,
):
    split = keep_ref.shape[0] * 3 // 4
    blocks, block, width = total.shape
    first = dot(keep_ref[:split], n1b_ref[...], ((1,), (0,)))
    first = first + got_ref[:split].astype(jnp.float32)
    total[: blocks * 3 // 4] = first.reshape(blocks * 3 // 4, block, width)
    last = dot(keep_ref[split:], mixed_ref[...], ((1,), (0,)))
    last = last + got_ref[split:].astype(jnp.float32)
    total[blocks * 3 // 4 :] = last.reshape(blocks // 4, block, width)
    begin = 0
    for index, (send, keep) in enumerate(((send_a, keep_a), (send_b, keep_b), (send_c, keep_c))):
        mine = place_ref[3 + index]
        stride = {2: 1, 4: 2, 8: 4, "y": 8}[RS_ORDERS[index][0]]
        columns = slice(begin, begin + send.shape[2])
        begin += send.shape[2]
        for j in range(blocks // 2):
            low = j // stride * 2 * stride + j % stride
            send[j] = total[low + (1 - mine) * stride, :, columns].astype(jnp.bfloat16)
            keep[j] = total[low + mine * stride, :, columns]


def expert_kernel(
    place_ref, own_ref, got_ref, router_ref,
    in_near_ref, in_arrived_ref, in_far_ref, out_near_ref, out_arrived_ref, out_far_ref,
    rows_ref, hidden_ref, du_ref, dmade_ref, mine_ref, theirs_ref, probs_ref, in_full, out_full,
    come_in, come_out,
):
    core, host = place_ref[0], place_ref[1]
    half, units = in_far_ref.shape
    own, width = got_ref.shape[0], got_ref.shape[1] // 2
    for side in range(2):

        at, other = pl.ds(side * half, half), pl.ds((1 - side) * half, half)

        @pl.when(core == side)
        def _():
            pltpu.make_async_copy(in_far_ref, in_full.at[other], come_in).start()
            pltpu.make_async_copy(out_far_ref, out_full.at[:, other], come_out).start()

        @pl.when((core == side) & (place_ref[2] == 1))
        def _():
            pltpu.make_async_copy(in_near_ref, in_full.at[at], come_in).start()
            pltpu.make_async_copy(out_near_ref, out_full.at[:, at], come_out).start()

        @pl.when((core == side) & (place_ref[2] == 0))
        def _():
            pltpu.make_async_copy(in_arrived_ref, in_full.at[at], come_in).start()
            pltpu.make_async_copy(out_arrived_ref, out_full.at[:, at], come_out).start()

    rows = jnp.concatenate([own_ref[:, :width], got_ref[:, :width]], axis=0)
    dy = jnp.concatenate([own_ref[:, width:], got_ref[:, width:]], axis=0)
    rows_ref[...] = rows
    logits = dot(rows, router_ref[...], ((1,), (1,)))
    raised = jnp.exp(logits - jnp.max(logits, axis=-1, keepdims=True))
    probs = raised / jnp.sum(raised, axis=-1, keepdims=True)
    probs_ref[...] = probs[:own]
    chosen = lax.broadcasted_iota(jnp.int32, probs.shape, 1) == host
    gate = jnp.sum(jnp.where(chosen, probs, 0.0), axis=-1, keepdims=True)
    dmade_ref[...] = (gate * dy.astype(jnp.float32)).astype(jnp.bfloat16)
    dmade = dmade_ref[...]
    pltpu.make_async_copy(in_full, in_full, come_in).wait()
    pltpu.make_async_copy(out_full, out_full, come_out).wait()
    made = jnp.zeros(rows.shape, jnp.float32)
    drows = jnp.zeros(rows.shape, jnp.float32)
    step = units // 3
    for begin in range(0, units, step):
        at = slice(begin, begin + step)
        upre = dot(rows, in_full[:, at], ((1,), (0,)))
        square = upre * upre
        bent = jnp.tanh(0.7978845608028654 * (upre + 0.044715 * upre * square))
        hidden = (0.5 * upre * (1.0 + bent)).astype(jnp.bfloat16)
        slope = 0.5 * (1.0 + bent) + 0.5 * upre * (1.0 - bent * bent) * (
            0.7978845608028654 * (1.0 + 3.0 * 0.044715 * square)
        )
        dhidden = dot(dmade, out_full[at, :], ((1,), (1,)))
        du = (dhidden * slope).astype(jnp.bfloat16)
        hidden_ref[:, at] = hidden
        du_ref[:, at] = du
        made = made + dot(hidden, out_full[at, :], ((1,), (0,)))
        drows = drows + dot(du, in_full[:, at], ((1,), (1,)))
    mine_ref[0] = made[:own]
    mine_ref[1] = drows[:own]
    theirs_ref[0] = made[own:]
    theirs_ref[1] = drows[own:]


def settle_kernel(
    place_ref, mine_ref, got_ref, own_ref, probs_ref, router_ref, back_ref, router_part_ref
):
    width = own_ref.shape[1] // 2
    chips, places, _ = back_ref.shape
    made = (mine_ref[0] + got_ref[0]).astype(jnp.bfloat16)
    row = lax.broadcasted_iota(jnp.int32, (chips * 16, made.shape[0]), 0)
    column = lax.broadcasted_iota(jnp.int32, row.shape, 1)
    inside = (row & 15) < places
    spread = jnp.where(inside & (column == (row >> 4) * places + (row & 15)), 1.0, 0.0)
    spread = spread.astype(jnp.bfloat16)

    def padded(values):
        wide = dot(spread, values, ((1,), (0,))).reshape(chips, 16, width)
        return wide[:, :places].astype(jnp.bfloat16)

    back_ref[:, :, width:] = padded(made)
    drows = (mine_ref[1] + got_ref[1]).astype(jnp.bfloat16).astype(jnp.float32)
    probs = probs_ref[...]
    chosen = (lax.broadcasted_iota(jnp.int32, probs.shape, 1) == place_ref[1]).astype(jnp.float32)
    gate = jnp.sum(probs * chosen, axis=-1, keepdims=True)
    dgate = jnp.sum(
        own_ref[:, width:].astype(jnp.float32) * made.astype(jnp.float32),
        axis=-1,
        keepdims=True,
    )
    dlogits = probs * dgate * (chosen - gate)
    router_part_ref[...] = dot(
        dlogits, own_ref[:, :width].astype(jnp.float32), ((0,), (0,)), precision=HIGH
    )
    dn2 = drows + dot(dlogits, router_ref[...].astype(jnp.float32), ((1,), (0,)), precision=HIGH)
    back_ref[:, :, :width] = padded(dn2.astype(jnp.bfloat16))


def paired_body(
    tokens,
    attn_weight,
    gain_attn,
    gain_expert,
    bias_table,
    router_weight,
    expert_in,
    expert_out,
    routes,
    slots,
    buckets,
    cotangent,
):
    f32, bf16 = jnp.float32, jnp.bfloat16
    micro, _, seq_len, width = tokens.shape
    count = micro * seq_len
    heads = bias_table.shape[1]
    head_size = width // heads
    bucket_count = bias_table.shape[0]
    experts = lax.axis_size("expert")
    capacity = (5 * seq_len + 4 * experts - 1) // (4 * experts)
    places = micro * capacity
    hidden_half = expert_in.shape[2] // 2
    width_half = width // 2
    dp_at, expert_at = lax.axis_index("dp"), lax.axis_index("expert")
    core = expert_at % 2
    home = core == dp_at
    host = expert_at - core + dp_at
    gain_one, gain_two = gain_attn.astype(f32), gain_expert.astype(f32)

    across, first = [], []
    for dp in range(2):
        for e in range(experts):
            here = dp * experts + e
            if e % 2 == dp:
                first.append((here, dp * experts + (e ^ 1), (1 - dp) * experts + e))
            else:
                across.append((here, (1 - dp) * experts + (e ^ 1)))
                first.append((here, (1 - dp) * experts + e, dp * experts + (e ^ 1)))
    outward = [(here, there) for here, there, _ in first]
    homeward = [(here, there) for here, _, there in first]

    groups = [
        [dp * experts + 2 * pair + side for dp in range(2) for pair in range(experts // 2)]
        for side in range(2)
    ]

    def to_chips(tensor):
        return lax.all_to_all(
            tensor, BOTH, split_axis=0, concat_axis=0, tiled=True, axis_index_groups=groups
        )

    row_count = experts * places
    upstream_b = cotangent.reshape(count, width)
    def parts_of(local, axis):
        near = lax.dynamic_slice_in_dim(local, dp_at * hidden_half, hidden_half, axis)
        far = lax.dynamic_slice_in_dim(local, (1 - dp_at) * hidden_half, hidden_half, axis)
        return near, far

    in_near, in_far = parts_of(expert_in[0], 1)
    def halves(tensor):
        return (
            lax.dynamic_slice_in_dim(tensor, core * width_half, width_half, 1),
            lax.dynamic_slice_in_dim(tensor, (1 - core) * width_half, width_half, 1),
        )

    def whole(keep, got, axis):
        low = core == 0
        return jnp.concatenate(
            [jnp.where(low, keep, got), jnp.where(low, got, keep)], axis=axis
        )

    moved = []

    def prepare(table, ids, route_ids, slot_ids, near, far):
        made = call(
            functools.partial(prepare_kernel, places, capacity),
            16,
            (
                ((heads, count, count), f32),
                ((seq_len, count), jnp.int32),
                ((row_count, count), bf16),
                ((experts * 16, count), bf16),
            ),
            [],
            table, ids, route_ids, slot_ids,
        )
        in_arrived = lax.ppermute(near, BOTH, across)
        moved.append(lax.ppermute(far, BOTH, outward))
        return tuple(made) + (in_arrived,)

    pieces, ready, (out_near, out_far) = gather_rows(
        attn_weight.T,
        prepare,
        (bias_table.astype(f32), buckets, routes, slots, in_near, in_far),
        parts_of,
        expert_out[0],
    )
    square, tiled, dispatch, padded, in_arrived = ready
    pieces, in_far = lax.optimization_barrier((pieces, moved[0]))
    out_arrived = lax.ppermute(out_near, BOTH, across)
    place = jnp.stack(
        [core, host, home.astype(jnp.int32)] + [own_bit(order[0]) for order in RS_ORDERS]
    ).astype(jnp.int32)
    gain_one, gain_two = gain_one[None], gain_two[None]
    local = tokens.reshape(count, width)
    wt_qkv, wt_o, n1b, qkv, probs, mixed_b, resid, n2b, outgoing = call(
        attend_kernel,
        26,
        (
            ((12, 2, width // 8, width), bf16),
            ((4, 2, width // 8, width), bf16),
            ((count, width), bf16),
            ((3 * width, count), bf16),
            ((heads, count, count), f32),
            ((count, width), bf16),
            ((count, width), f32),
            ((count, width), bf16),
            ((experts, places, 2 * width), bf16),
        ),
        [
            pltpu.VMEM((width, count), f32),
            pltpu.VMEM((16, 2, width // 8, width), bf16),
            pltpu.SemaphoreType.DMA,
            pltpu.SemaphoreType.DMA,
            pltpu.SemaphoreType.DMA,
        ],
        place, local, *pieces, gain_one, gain_two, square, padded, upstream_b,
        plain_in=range(2, 8),
        plain_out=(0, 1),
    )
    wt_qkv, wt_o = wt_qkv.reshape(3 * width, width), wt_o.reshape(width, width)
    outgoing, out_arrived, out_far = lax.optimization_barrier((outgoing, out_arrived, out_far))
    own_rows = to_chips(outgoing).reshape(row_count, 2 * width)
    in_parts = (in_near, in_arrived, in_far)
    out_parts = (out_near, out_arrived, lax.ppermute(out_far, BOTH, outward))
    rows, hidden, du, dmade, mine, theirs, row_probs = call(
        expert_kernel,
        34,
        (
            ((2 * row_count, width), bf16),
            ((2 * row_count, hidden_half), bf16),
            ((2 * row_count, hidden_half), bf16),
            ((2 * row_count, width), bf16),
            ((2, row_count, width), f32),
            ((2, row_count, width), f32),
            ((row_count, experts), f32),
        ),
        [
            pltpu.VMEM((width, hidden_half), bf16),
            pltpu.VMEM((hidden_half, width), bf16),
            pltpu.SemaphoreType.DMA,
            pltpu.SemaphoreType.DMA,
        ],
        place, own_rows, flip(own_rows, 1), router_weight.T, *in_parts, *out_parts,
        plain_in=range(4, 10),
        free=(2,),
    )
    back_rows, router_part = call(
        settle_kernel,
        10,
        (
            ((experts, places, 2 * width), bf16),
            ((experts, width), f32),
        ),
        [],
        place, mine, flip(theirs, 1), own_rows, row_probs, router_weight.T,
        free=(2,),
    )
    in_other = dot(halves(rows)[1], du, ((0,), (0,))).astype(bf16)
    back_rows, rows, hidden, du, dmade = lax.optimization_barrier(
        (back_rows, rows, hidden, du, dmade)
    )
    home_rows = to_chips(back_rows).reshape(row_count, 2 * width)
    rows_keep, _ = halves(rows)
    dmade_keep, dmade_got = halves(dmade)

    in_homely = lax.ppermute(in_other, BOTH, homeward)
    in_mine = dot(rows_keep, du, ((0,), (0,)))
    out_other = dot(hidden, dmade_got, ((0,), (0,))).astype(bf16)
    out_homely = lax.ppermute(out_other, BOTH, homeward)
    out_mine = dot(hidden, dmade_keep, ((0,), (0,)))
    home_rows, in_homely, out_homely, in_leave, out_leave = lax.optimization_barrier(
        (home_rows, in_homely, out_homely, in_mine.astype(bf16), out_mine.astype(bf16))
    )
    in_arrived = lax.ppermute(in_leave, BOTH, across)
    out_arrived = lax.ppermute(out_leave, BOTH, across)

    dresid, gain_two_part, dqkv, fold, send, keep = call(
        attend_back_kernel,
        26,
        (
            ((count, width), f32),
            ((1, width), f32),
            ((3 * width, count), bf16),
            ((heads, count // 2, count), f32),
            ((2 * width, width), bf16),
            ((2 * width, count), bf16),
        ),
        [pltpu.VMEM((4 * width, count), bf16)],
        place, home_rows, dispatch, resid, upstream_b, gain_two, wt_o, qkv, probs, n1b, mixed_b,
    )
    got = flip(send, 1)
    small_rows = (width // 128) * experts + 16 + (heads + 7) // 8 * 8
    token_grad, small = call(
        functools.partial(token_back_kernel, bucket_count),
        26,
        (
            ((count, width), f32),
            ((small_rows, 128), f32),
        ),
        [],
        place, local, dqkv, wt_qkv, gain_one, dresid, fold, tiled, gain_two_part,
        router_part,
    )
    block = width // 8
    pieces = (width // 6, width // 3, width // 2)
    cut = call(
        split_kernel,
        30,
        tuple(((8, block, piece), bf16) for piece in pieces)
        + tuple(((8, block, piece), f32) for piece in pieces),
        [pltpu.VMEM((16, block, width), f32)],
        place, keep, n1b, mixed_b, got,
        free=(4,),
    )
    attn_share, small, late = scatter_rows(
        cut[:3],
        cut[3:],
        small,
        (
            (),
            (in_arrived, in_mine, in_homely),
            (out_arrived, out_mine, out_homely),
            (home_rows, routes),
        ),
    )
    _, in_late, out_late, (home_rows, routes) = late
    route_ids = routes[:, 0]
    in_arrived, in_mine, in_homely = in_late
    out_arrived, out_mine, out_homely = out_late
    in_back = (in_mine, in_homely, in_arrived)
    out_back = (out_mine, out_homely, out_arrived)

    def settled(parts, axis):
        near, homely, arrived = parts
        mine = jnp.where(home, near, homely.astype(f32))
        other = jnp.where(home, homely.astype(f32), arrived.astype(f32))
        return whole(mine, other, axis)

    in_share, out_share = settled(in_back, 1), settled(out_back, 0)
    router_probs = jax.nn.softmax(dot(n2b, router_weight, ((1,), (0,))), axis=-1)
    picked = (route_ids.reshape(count, 1) == jnp.arange(experts)).astype(f32)
    gate = jnp.sum(router_probs * picked, axis=-1, keepdims=True)
    returned = dot(dispatch, home_rows[:, width:], ((0,), (0,)))
    output = (resid + gate * returned).astype(bf16)

    attn_share = attn_share.T
    routed = (width // 128) * experts
    return (
        output.reshape(tokens.shape),
        token_grad.reshape(tokens.shape),
        attn_share,
        small[routed : routed + width // 128].reshape(width),
        small[routed + 8 : routed + 8 + width // 128].reshape(width),
        small[routed + 16 : routed + 16 + heads, :bucket_count].T,
        jnp.transpose(small[:routed].reshape(-1, experts, 128), (0, 2, 1)).reshape(width, experts),
        in_share[None],
        out_share[None],
    )


def solution(mesh):
    paired = mesh.shape["dp"] == 2 and mesh.shape["expert"] == 16
    chosen = paired_body if paired else body
    placed = (
        P(None, ("dp", "expert"), None, None),
        P(None, ("dp", "expert")),
        P(),
        P(),
        P(),
        P(),
        P("expert", "dp", None),
        P("expert", None, "dp"),
        P(None, ("dp", "expert"), None),
        P(None, ("dp", "expert"), None),
        P(),
        P(None, ("dp", "expert"), None, None),
    )
    return jax.shard_map(
        chosen,
        mesh=mesh,
        in_specs=placed,
        out_specs=(
            P(None, ("dp", "expert"), None, None),
            P(None, ("dp", "expert"), None, None),
            P(None, ("dp", "expert")),
            P(),
            P(),
            P(),
            P(),
            P("expert", "dp", None),
            P("expert", None, "dp"),
        ),
        check_vma=False,
    )
```

```python
import functools
import jax
import jax.numpy as jnp
from jax import lax
from jax.experimental import pallas as pl
from jax.experimental.pallas import tpu as pltpu
from jax.sharding import PartitionSpec as P

EPSILON = 1e-06
HIGH = lax.Precision.HIGHEST


def smooth_gate(values):
    return jax.nn.gelu(values, approximate=True)


def rms_scale(values):
    return lax.rsqrt(jnp.mean(values * values, axis=-1, keepdims=True) + EPSILON)


def body(
    tokens,
    attn_weight,
    gain_attn,
    gain_expert,
    bias_table,
    router_weight,
    expert_in,
    expert_out,
    routes,
    slots,
    buckets,
    cotangent,
):
    micro = tokens.shape[0]
    seq_len = tokens.shape[2]
    width = tokens.shape[3]
    heads = bias_table.shape[1]
    head_size = width // heads
    bucket_count = bias_table.shape[0]
    local_experts = expert_in.shape[0]
    expert_devices = lax.axis_size("expert")
    total_experts = local_experts * expert_devices
    capacity = (5 * seq_len + 4 * total_experts - 1) // (4 * total_experts)
    slot_total = total_experts * capacity
    gain_one = gain_attn.astype(jnp.float32)
    gain_two = gain_expert.astype(jnp.float32)
    router_full = router_weight.astype(jnp.float32)
    bucket_hot = (buckets[:, :, None] == jnp.arange(bucket_count)).astype(jnp.float32)
    bias_term = jnp.einsum(
        "ijb,bh->hij", bucket_hot, bias_table.astype(jnp.float32), precision=HIGH
    )

    def to_experts(tensor):
        tensor = tensor.reshape(expert_devices, local_experts, capacity, width)
        return jnp.transpose(tensor, (1, 0, 2, 3)).reshape(
            local_experts, expert_devices * capacity, width
        )

    def from_experts(tensor):
        tensor = tensor.reshape(local_experts, expert_devices, capacity, width)
        return jnp.transpose(tensor, (1, 0, 2, 3)).reshape(total_experts, capacity, width)

    gain_one_total = jnp.zeros((width,), jnp.float32)
    gain_two_total = jnp.zeros((width,), jnp.float32)
    bias_total = jnp.zeros((bucket_count, heads), jnp.float32)
    router_total = jnp.zeros((width, total_experts), jnp.float32)
    results = []
    token_grads = []
    kept_rows = []
    kept_hidden = []
    kept_dmade = []
    kept_dpre = []
    kept_mixed = []
    kept_dattn = []
    kept_normed = []
    kept_dqkv = []
    for micro_index in range(micro):
        inputs = tokens[micro_index, 0].astype(jnp.float32)
        full_attn = lax.all_gather(attn_weight, ("dp", "expert"), axis=1, tiled=True)
        scale_one = rms_scale(inputs)
        n1hat = inputs * scale_one
        n1b = (n1hat * gain_one).astype(jnp.bfloat16)
        qkv = jnp.dot(n1b, full_attn[:, : 3 * width], preferred_element_type=jnp.float32).astype(
            jnp.bfloat16
        )
        query = qkv[:, :width].reshape(seq_len, heads, head_size)
        key_part = qkv[:, width : 2 * width].reshape(seq_len, heads, head_size)
        value_part = qkv[:, 2 * width :].reshape(seq_len, heads, head_size)
        scores = (
            jnp.einsum("ihd,jhd->hij", query, key_part, preferred_element_type=jnp.float32)
            + bias_term
        )
        log_total = jax.nn.logsumexp(scores, axis=-1, keepdims=True)
        probs_b = jnp.exp(scores - log_total).astype(jnp.bfloat16)
        mixed = jnp.einsum("hij,jhd->ihd", probs_b, value_part, preferred_element_type=jnp.float32)
        mixed_b = mixed.reshape(seq_len, width).astype(jnp.bfloat16)
        resid = inputs + jnp.dot(
            mixed_b, full_attn[:, 3 * width :], preferred_element_type=jnp.float32
        )
        scale_two = rms_scale(resid)
        n2hat = resid * scale_two
        n2b = (n2hat * gain_two).astype(jnp.bfloat16)
        logits = jnp.dot(n2b, router_weight, preferred_element_type=jnp.float32)
        router_probs = jax.nn.softmax(logits, axis=-1)
        route_ids = routes[micro_index, 0]
        slot_ids = slots[micro_index, 0]
        picked = (route_ids[:, None] == jnp.arange(total_experts)).astype(jnp.float32)
        gate = jnp.sum(router_probs * picked, axis=-1)
        flat = route_ids * capacity + slot_ids
        dispatch = (
            (flat[:, None] == jnp.arange(slot_total)) & (slot_ids[:, None] < capacity)
        ).astype(jnp.bfloat16)
        outgoing = jnp.einsum(
            "sk,sd->kd", dispatch, n2b, preferred_element_type=jnp.float32
        ).astype(jnp.bfloat16)
        arrived = lax.all_to_all(
            outgoing.reshape(total_experts, capacity, width),
            "expert",
            split_axis=0,
            concat_axis=0,
            tiled=True,
        )
        expert_rows = to_experts(arrived)
        full_in, full_out = (
            lax.all_gather(expert_in, "dp", axis=1, tiled=True),
            lax.all_gather(expert_out, "dp", axis=2, tiled=True),
        )
        hidden_pre = jnp.einsum(
            "erd,edf->erf", expert_rows, full_in, preferred_element_type=jnp.float32
        )
        hidden = smooth_gate(hidden_pre).astype(jnp.bfloat16)
        made = jnp.einsum(
            "erf,efd->erd", hidden, full_out, preferred_element_type=jnp.float32
        ).astype(jnp.bfloat16)
        kept_rows.append(expert_rows)
        kept_hidden.append(hidden)
        came_back = lax.all_to_all(
            from_experts(made), "expert", split_axis=0, concat_axis=0, tiled=True
        )
        returned = jnp.einsum(
            "sk,kd->sd",
            dispatch,
            came_back.reshape(slot_total, width),
            preferred_element_type=jnp.float32,
        )
        results.append((resid + gate[:, None] * returned).astype(jnp.bfloat16))
        upstream = cotangent[micro_index, 0].astype(jnp.float32)
        dgate = jnp.sum(upstream * returned, axis=-1)
        dreturned = (gate[:, None] * upstream).astype(jnp.bfloat16)
        dslots = jnp.einsum(
            "sk,sd->kd", dispatch, dreturned, preferred_element_type=jnp.float32
        ).astype(jnp.bfloat16)
        dmade = to_experts(
            lax.all_to_all(
                dslots.reshape(total_experts, capacity, width),
                "expert",
                split_axis=0,
                concat_axis=0,
                tiled=True,
            )
        )
        back_attn = lax.all_gather(attn_weight, ("dp", "expert"), axis=1, tiled=True)
        back_in, back_out = (
            lax.all_gather(expert_in, "dp", axis=1, tiled=True),
            lax.all_gather(expert_out, "dp", axis=2, tiled=True),
        )
        dhidden = jnp.einsum("erd,efd->erf", dmade, back_out, preferred_element_type=jnp.float32)
        dpre = jax.vjp(smooth_gate, hidden_pre)[1](dhidden)[0].astype(jnp.bfloat16)
        kept_dmade.append(dmade)
        kept_dpre.append(dpre)
        drows = jnp.einsum(
            "erf,edf->erd", dpre, back_in, preferred_element_type=jnp.float32
        ).astype(jnp.bfloat16)
        drows_home = lax.all_to_all(
            from_experts(drows), "expert", split_axis=0, concat_axis=0, tiled=True
        )
        dnormed = jnp.einsum(
            "sk,kd->sd",
            dispatch,
            drows_home.reshape(slot_total, width),
            preferred_element_type=jnp.float32,
        )
        dpick = picked * dgate[:, None]
        dlogits = router_probs * (dpick - jnp.sum(router_probs * dpick, axis=-1, keepdims=True))
        router_total = router_total + jnp.dot(n2b.astype(jnp.float32).T, dlogits, precision=HIGH)
        dnormed = dnormed + jnp.dot(dlogits, router_full.T, precision=HIGH)
        gain_two_total = gain_two_total + jnp.sum(dnormed * n2hat, axis=0)
        dhat_two = dnormed * gain_two
        dresid = upstream + scale_two * (
            dhat_two - n2hat * jnp.mean(dhat_two * n2hat, axis=-1, keepdims=True)
        )
        dattn = dresid.astype(jnp.bfloat16)
        dmixed = jnp.einsum(
            "se,de->sd", dattn, back_attn[:, 3 * width :], preferred_element_type=jnp.float32
        )
        dmixed = dmixed.astype(jnp.bfloat16).reshape(seq_len, heads, head_size)
        again_scores = (
            jnp.einsum("ihd,jhd->hij", query, key_part, preferred_element_type=jnp.float32)
            + bias_term
        )
        probs = jnp.exp(again_scores - log_total)
        again_b = probs.astype(jnp.bfloat16)
        dvalue = jnp.einsum("hij,ihd->jhd", again_b, dmixed, preferred_element_type=jnp.float32)
        dprobs = jnp.einsum("ihd,jhd->hij", dmixed, value_part, preferred_element_type=jnp.float32)
        dscores = probs * (dprobs - jnp.sum(probs * dprobs, axis=-1, keepdims=True))
        bias_total = bias_total + jnp.einsum("hij,ijb->bh", dscores, bucket_hot, precision=HIGH)
        dscores_b = dscores.astype(jnp.bfloat16)
        dquery = jnp.einsum("hij,jhd->ihd", dscores_b, key_part, preferred_element_type=jnp.float32)
        dkey = jnp.einsum("hij,ihd->jhd", dscores_b, query, preferred_element_type=jnp.float32)
        dqkv = jnp.concatenate(
            [
                dquery.reshape(seq_len, width),
                dkey.reshape(seq_len, width),
                dvalue.reshape(seq_len, width),
            ],
            axis=1,
        ).astype(jnp.bfloat16)
        kept_mixed.append(mixed_b)
        kept_dattn.append(dattn)
        kept_normed.append(n1b)
        kept_dqkv.append(dqkv)
        dnormed_one = jnp.einsum(
            "se,de->sd", dqkv, back_attn[:, : 3 * width], preferred_element_type=jnp.float32
        )
        gain_one_total = gain_one_total + jnp.sum(dnormed_one * n1hat, axis=0)
        dhat_one = dnormed_one * gain_one
        token_grads.append(
            dresid
            + scale_one * (dhat_one - n1hat * jnp.mean(dhat_one * n1hat, axis=-1, keepdims=True))
        )
    normed_all = jnp.concatenate(kept_normed, axis=0)
    dqkv_all = jnp.concatenate(kept_dqkv, axis=0)
    mixed_all = jnp.concatenate(kept_mixed, axis=0)
    dattn_all = jnp.concatenate(kept_dattn, axis=0)
    dqkv_proj = jnp.einsum("sd,se->de", normed_all, dqkv_all, preferred_element_type=jnp.float32)
    dout_proj = jnp.einsum("sd,se->de", mixed_all, dattn_all, preferred_element_type=jnp.float32)
    attn_total = jnp.concatenate([dqkv_proj, dout_proj], axis=1)
    attn_share = lax.psum_scatter(attn_total, ("dp", "expert"), scatter_dimension=1, tiled=True)
    rows_all = jnp.concatenate(kept_rows, axis=1)
    hidden_all = jnp.concatenate(kept_hidden, axis=1)
    dmade_cat = jnp.concatenate(kept_dmade, axis=1)
    dpre_all = jnp.concatenate(kept_dpre, axis=1)
    in_total = jnp.einsum("erd,erf->edf", rows_all, dpre_all, preferred_element_type=jnp.float32)
    out_turned_total = jnp.einsum(
        "erd,erf->edf", dmade_cat, hidden_all, preferred_element_type=jnp.float32
    )
    in_share, out_turned_share = (
        lax.psum_scatter(
            in_total.astype(jnp.bfloat16), "dp", scatter_dimension=1, tiled=True
        ).astype(jnp.float32),
        lax.psum_scatter(
            out_turned_total.astype(jnp.bfloat16), "dp", scatter_dimension=1, tiled=True
        ).astype(jnp.float32),
    )
    out_share = jnp.transpose(out_turned_share, (0, 2, 1))
    gain_one_sum, gain_two_sum, bias_sum, router_sum = lax.psum(
        (gain_one_total, gain_two_total, bias_total, router_total), ("dp", "expert")
    )
    output = jnp.stack(results)[:, None]
    token_grad = jnp.stack(token_grads)[:, None]
    return (
        output,
        token_grad,
        attn_share,
        gain_one_sum,
        gain_two_sum,
        bias_sum,
        router_sum,
        in_share,
        out_share,
    )


BOTH = ("dp", "expert")


def flip(tensor, bit):
    if bit == "y":
        return lax.ppermute(tensor, "dp", [(0, 1), (1, 0)])
    count = lax.axis_size("expert")
    return lax.ppermute(tensor, "expert", [(i, i ^ bit) for i in range(count)])


def own_bit(bit):
    if bit == "y":
        return lax.axis_index("dp")
    return (lax.axis_index("expert") // bit) % 2


ORDERS = (("y", 2, 8, 4), (2, "y", 8, 4), (8, "y", 4, 2))
RS_ORDERS = ((8, 4, 2, "y"), ("y", 8, 4, 2), (2, "y", 8, 4))
PLACE = {"y": 0, 8: 1, 4: 2, 2: 3, 1: 4}


def gather_rows(shard, prepare, waiting, divide, last):
    rows, width = shard.shape
    pieces, begin = [], 0
    for size in (width // 3, width // 6, width // 2):
        piece = shard[:, begin : begin + size]
        pieces.append(piece.reshape(1, 1, 1, 1, rows, size))
        begin += size

    def grow(piece, bit):
        got = flip(piece, bit)
        low = own_bit(bit) == 0
        return jnp.concatenate(
            [jnp.where(low, piece, got), jnp.where(low, got, piece)], axis=PLACE[bit]
        )

    for step in range(4):
        if step == 2:
            pieces, waiting = lax.optimization_barrier((pieces, waiting))
            ready = prepare(*waiting)
        if step == 3:
            pieces, last = lax.optimization_barrier((pieces, last))
            last = divide(last, 0)
        pieces = [grow(piece, ORDERS[i][step]) for i, piece in enumerate(pieces)]
    pieces, ready, last = lax.optimization_barrier((pieces, ready, last))
    pieces = [piece.reshape(-1, rows, piece.shape[-1]) for piece in pieces]
    return pieces + [flip(piece, 1) for piece in pieces], ready, last


def reduce_step(total, bit):
    mine = own_bit(bit)
    axis = PLACE[bit]
    send = lax.dynamic_index_in_dim(total, 1 - mine, axis, keepdims=True).astype(jnp.bfloat16)
    keep = lax.dynamic_index_in_dim(total, mine, axis, keepdims=True)
    return keep + flip(send, bit).astype(jnp.float32)


def scatter_rows(leaves, stays, small, late):
    late = list(late)
    pieces = []
    for index, (leave, stay) in enumerate(zip(leaves, stays)):
        bit = RS_ORDERS[index][0]
        shape = [2, 2, 2, 2, 1] + list(stay.shape[1:])
        shape[PLACE[bit]] = 1
        pieces.append((stay + flip(leave, bit).astype(jnp.float32)).reshape(shape))
    for bit in (1, 2):
        small = small + flip(small, bit)
    for step in range(1, 4):
        pieces, late[step], small = lax.optimization_barrier((pieces, late[step], small))
        pieces = [reduce_step(piece, RS_ORDERS[i][step]) for i, piece in enumerate(pieces)]
        small = small + flip(small, ("y", 8, 4)[step - 1])
    whole = jnp.concatenate(pieces, axis=-1)
    return whole.reshape(whole.shape[-2], whole.shape[-1]), small, late


def dot(left, right, dims, **more):
    return lax.dot_general(
        left, right, (dims, ((), ())), preferred_element_type=jnp.float32, **more
    )


def call(kernel, mib, outs, scratch, *operands, plain_in=(), plain_out=(), free=()):
    def spec(shape):
        return pl.BlockSpec(
            shape, lambda i: (0,) * len(shape), pipeline_mode=pl.Buffered(1)
        )

    left = pl.BlockSpec(memory_space=pl.ANY)
    operands = operands[:1] + tuple(
        operand if i in free else pltpu.with_memory_space_constraint(operand, pltpu.HBM)
        for i, operand in enumerate(operands)
        if i
    )
    return pl.pallas_call(
        kernel,
        grid=(1,),
        out_shape=tuple(pltpu.HBM(*out) for out in outs),
        in_specs=[pl.BlockSpec(memory_space=pltpu.SMEM)]
        + [left if i in plain_in else spec(operand.shape) for i, operand in enumerate(operands) if i],
        out_specs=tuple(left if i in plain_out else spec(out[0]) for i, out in enumerate(outs)),
        scratch_shapes=scratch,
        compiler_params=pltpu.CompilerParams(vmem_limit_bytes=mib * 2**20),
    )(*operands)


def prepare_kernel(
    places, capacity, table_ref, buckets_ref, routes_ref, slots_ref,
    square_ref, tiled_ref, dispatch_ref, padded_ref,
):
    heads, count, _ = square_ref.shape
    turned = buckets_ref[...].astype(jnp.float32).T.astype(jnp.int32)
    wide = jnp.concatenate([turned, turned], axis=1)
    tiled_ref[...] = wide
    buckets = jnp.concatenate([wide, wide], axis=0)
    row = lax.broadcasted_iota(jnp.int32, (count, count), 0)
    column = lax.broadcasted_iota(jnp.int32, (count, count), 1)
    half = count // 2
    same = (row < half) == (column < half)
    for head in range(heads):
        total = jnp.where(same, 0.0, -jnp.inf)
        for bucket in range(table_ref.shape[0]):
            total = jnp.where(same & (buckets == bucket), table_ref[bucket, head], total)
        square_ref[head] = total
    routes = jnp.concatenate([routes_ref[0], routes_ref[1]], axis=1)
    slots = jnp.concatenate([slots_ref[0], slots_ref[1]], axis=1)
    second = lax.broadcasted_iota(jnp.int32, (1, count), 1) >= half
    at = slots + jnp.where(second, capacity, 0)
    chip = (routes & 1) * 8 + (routes >> 1)
    for ref, size in ((dispatch_ref, places), (padded_ref, 16)):
        flat = jnp.where(slots < capacity, chip * size + at, -1)
        rows = lax.broadcasted_iota(jnp.int32, ref.shape, 0)
        ref[...] = jnp.where(rows == flat, 1.0, 0.0).astype(jnp.bfloat16)


def attend_kernel(
    place_ref, x_ref, *rest,
):
    pieces, rest = rest[:6], rest[6:]
    (
        gain_one_ref, gain_two_ref, bias_ref, dispatch_ref, dy_ref,
        wt_qkv_ref, wt_o_ref, n1b_ref, qkv_ref, probs_ref, mixed_ref, resid_ref, n2b_ref, rows_ref,
        mixed_t, wt_ref, come, go_qkv, go_o,
    ) = rest
    core = place_ref[0]
    pairs = pieces[0].shape[0]
    for side, part in ((core, pieces[:3]), (1 - core, pieces[3:])):
        begin = 0
        for piece in part:
            size = piece.shape[2]
            pltpu.make_async_copy(
                piece, wt_ref.at[:, side, :, pl.ds(begin, size)], come
            ).start()
            begin += size
    heads = probs_ref.shape[0]
    width = x_ref.shape[1]
    size = width // heads
    x = x_ref[...].astype(jnp.float32)
    n1b_ref[...] = (x * rms_scale(x) * gain_one_ref[...]).astype(jnp.bfloat16)
    pltpu.make_async_copy(wt_ref, wt_ref, come).wait()
    most = pairs * 3 // 4
    leave_qkv = pltpu.make_async_copy(wt_ref.at[pl.ds(0, most)], wt_qkv_ref, go_qkv)
    leave_o = pltpu.make_async_copy(wt_ref.at[pl.ds(most, pairs - most)], wt_o_ref, go_o)
    leave_qkv.start()
    leave_o.start()
    qkv_ref[...] = dot(wt_ref[:most].reshape(3 * width, width), n1b_ref[...], ((1,), (1,))).astype(jnp.bfloat16)
    for head in range(heads):
        query = qkv_ref[head * size : (head + 1) * size]
        keys = qkv_ref[width + head * size : width + (head + 1) * size]
        values = qkv_ref[2 * width + head * size : 2 * width + (head + 1) * size]
        scores = dot(keys, query, ((0,), (0,))) + bias_ref[head]
        raised = jnp.exp(scores - jnp.max(scores, axis=0, keepdims=True))
        probs = raised / jnp.sum(raised, axis=0, keepdims=True)
        probs_ref[head] = probs
        mixed_t[head * size : (head + 1) * size] = dot(
            values, probs.astype(jnp.bfloat16), ((1,), (0,))
        )
    mixed_ref[...] = mixed_t[...].T.astype(jnp.bfloat16)
    resid = x + dot(
        mixed_ref[...], wt_ref[most:].reshape(width, width), ((1,), (1,))
    )
    resid_ref[...] = resid
    n2b_ref[...] = (resid * rms_scale(resid) * gain_two_ref[...]).astype(jnp.bfloat16)
    chips, places, _ = rows_ref.shape
    rows = dot(dispatch_ref[...], n2b_ref[...], ((1,), (0,))).reshape(chips, -1, width)
    rows_ref[:, :, :width] = rows[:, :places].astype(jnp.bfloat16)
    dy_rows = dot(dispatch_ref[...], dy_ref[...], ((1,), (0,))).reshape(chips, -1, width)
    rows_ref[:, :, width:] = dy_rows[:, :places].astype(jnp.bfloat16)
    leave_qkv.wait()
    leave_o.wait()


def attend_back_kernel(
    core_ref, dn2_ref, dispatch_ref, resid_ref, dy_ref, gain_two_ref, wt_ref, qkv_ref, probs_ref,
    n1b_ref, mixed_ref, dresid_ref, gain_ref, dqkv_ref, fold_ref, send_ref, keep_ref, columns,
):
    heads = probs_ref.shape[0]
    count, width = resid_ref.shape
    size = width // heads
    core = core_ref[0]
    resid = resid_ref[...]
    scale = rms_scale(resid)
    n2hat = resid * scale
    dn2 = dot(dispatch_ref[...], dn2_ref[:, :width], ((0,), (0,)))
    gain_ref[...] = jnp.sum(dn2 * n2hat, axis=0, keepdims=True)
    dhat = dn2 * gain_two_ref[...]
    dresid = dy_ref[...].astype(jnp.float32) + scale * (
        dhat - n2hat * jnp.mean(dhat * n2hat, axis=-1, keepdims=True)
    )
    dresid_ref[...] = dresid
    dattn = dresid.astype(jnp.bfloat16)
    dab = dot(dattn, wt_ref[...], ((1,), (0,)))
    dab_t = dab.T.astype(jnp.bfloat16)
    columns[3 * width :] = dresid.T.astype(jnp.bfloat16)
    for head in range(heads):
        at = slice(head * size, (head + 1) * size)
        query = qkv_ref[head * size : (head + 1) * size]
        keys = qkv_ref[width + head * size : width + (head + 1) * size]
        values = qkv_ref[2 * width + head * size : 2 * width + (head + 1) * size]
        dab_head = dab_t[at]
        probs = probs_ref[head]
        dvalue = dot(dab_head, probs.astype(jnp.bfloat16), ((1,), (1,)))
        dprobs = dot(values, dab_head, ((0,), (0,)))
        dscores = probs * (dprobs - jnp.sum(probs * dprobs, axis=0, keepdims=True))
        half = count // 2
        fold_ref[head] = dscores[:half] + dscores[half:]
        dscores_b = dscores.astype(jnp.bfloat16)
        dquery = dot(keys, dscores_b, ((1,), (0,)))
        dkey = dot(query, dscores_b, ((1,), (1,)))
        columns[head * size : (head + 1) * size] = dquery.astype(jnp.bfloat16)
        columns[width + head * size : width + (head + 1) * size] = dkey.astype(jnp.bfloat16)
        columns[2 * width + head * size : 2 * width + (head + 1) * size] = dvalue.astype(
            jnp.bfloat16
        )
    dqkv_ref[...] = columns[: 3 * width]
    block = width // 8
    sent = []
    for pair in range(16):
        theirs = pl.multiple_of((2 * pair + 1 - core) * block, block)
        mine = pl.multiple_of((2 * pair + core) * block, block)
        keep_ref[pair * block : (pair + 1) * block] = columns[pl.ds(mine, block), :]
        sent.append(columns[pl.ds(theirs, block), :])
    sent = jnp.concatenate(sent, axis=0)
    split = 12 * block
    send_ref[:split] = dot(sent[:split], n1b_ref[...], ((1,), (0,))).astype(jnp.bfloat16)
    send_ref[split:] = dot(sent[split:], mixed_ref[...], ((1,), (0,))).astype(jnp.bfloat16)


def token_back_kernel(
    bucket_count, _, x_ref, dqkv_ref, wt_ref, gain_one_ref, dresid_ref, fold_ref, buckets_ref, gain_part_ref,
    router_part_ref, grad_ref, small_ref,
):
    x = x_ref[...].astype(jnp.float32)
    scale = rms_scale(x)
    n1hat = x * scale
    width = x.shape[1]
    dn1 = dot(dqkv_ref[...], wt_ref[...], ((0,), (0,)))
    gain_part = jnp.sum(dn1 * n1hat, axis=0, keepdims=True)
    dhat = dn1 * gain_one_ref[...]
    grad_ref[...] = dresid_ref[...] + scale * (
        dhat - n1hat * jnp.mean(dhat * n1hat, axis=-1, keepdims=True)
    )
    experts = router_part_ref.shape[0]
    tiles = width // 128
    small_ref[...] = jnp.zeros(small_ref.shape, jnp.float32)
    for tile in range(tiles):
        at = slice(tile * 128, (tile + 1) * 128)
        small_ref[tile * experts : (tile + 1) * experts] = router_part_ref[:, at]
        base = tiles * experts + tile
        small_ref[base : base + 1] = gain_part[:, at]
        small_ref[base + 8 : base + 9] = gain_part_ref[:, at]
    heads = fold_ref.shape[0]
    lane = lax.broadcasted_iota(jnp.int32, (1, 128), 1)
    table = jnp.zeros((heads, 128), jnp.float32)
    buckets = buckets_ref[: fold_ref.shape[1]]
    fold = fold_ref[...]
    for bucket in range(bucket_count):
        column = jnp.sum(jnp.where((buckets == bucket)[None], fold, 0.0), axis=1)
        column = jnp.sum(column, axis=-1, keepdims=True)
        table = table + jnp.where(lane == bucket, column, 0.0)
    start = tiles * experts + 16
    small_ref[start : start + heads] = table


def split_kernel(
    place_ref, keep_ref, n1b_ref, mixed_ref, got_ref,
    send_a, send_b, send_c, keep_a, keep_b, keep_c, total,
):
    split = keep_ref.shape[0] * 3 // 4
    blocks, block, width = total.shape
    first = dot(keep_ref[:split], n1b_ref[...], ((1,), (0,)))
    first = first + got_ref[:split].astype(jnp.float32)
    total[: blocks * 3 // 4] = first.reshape(blocks * 3 // 4, block, width)
    last = dot(keep_ref[split:], mixed_ref[...], ((1,), (0,)))
    last = last + got_ref[split:].astype(jnp.float32)
    total[blocks * 3 // 4 :] = last.reshape(blocks // 4, block, width)
    begin = 0
    for index, (send, keep) in enumerate(((send_a, keep_a), (send_b, keep_b), (send_c, keep_c))):
        mine = place_ref[3 + index]
        stride = {2: 1, 4: 2, 8: 4, "y": 8}[RS_ORDERS[index][0]]
        columns = slice(begin, begin + send.shape[2])
        begin += send.shape[2]
        for j in range(blocks // 2):
            low = j // stride * 2 * stride + j % stride
            send[j] = total[low + (1 - mine) * stride, :, columns].astype(jnp.bfloat16)
            keep[j] = total[low + mine * stride, :, columns]


def expert_kernel(
    place_ref, own_ref, got_ref, router_ref,
    in_near_ref, in_arrived_ref, in_far_ref, out_near_ref, out_arrived_ref, out_far_ref,
    rows_ref, hidden_ref, du_ref, dmade_ref, mine_ref, theirs_ref, probs_ref, in_full, out_full,
    come_in, come_out,
):
    core, host = place_ref[0], place_ref[1]
    half, units = in_far_ref.shape
    own, width = got_ref.shape[0], got_ref.shape[1] // 2
    for side in range(2):

        at, other = pl.ds(side * half, half), pl.ds((1 - side) * half, half)

        @pl.when(core == side)
        def _():
            pltpu.make_async_copy(in_far_ref, in_full.at[other], come_in).start()
            pltpu.make_async_copy(out_far_ref, out_full.at[:, other], come_out).start()

        @pl.when((core == side) & (place_ref[2] == 1))
        def _():
            pltpu.make_async_copy(in_near_ref, in_full.at[at], come_in).start()
            pltpu.make_async_copy(out_near_ref, out_full.at[:, at], come_out).start()

        @pl.when((core == side) & (place_ref[2] == 0))
        def _():
            pltpu.make_async_copy(in_arrived_ref, in_full.at[at], come_in).start()
            pltpu.make_async_copy(out_arrived_ref, out_full.at[:, at], come_out).start()

    rows = jnp.concatenate([own_ref[:, :width], got_ref[:, :width]], axis=0)
    dy = jnp.concatenate([own_ref[:, width:], got_ref[:, width:]], axis=0)
    rows_ref[...] = rows
    logits = dot(rows, router_ref[...], ((1,), (1,)))
    raised = jnp.exp(logits - jnp.max(logits, axis=-1, keepdims=True))
    probs = raised / jnp.sum(raised, axis=-1, keepdims=True)
    probs_ref[...] = probs[:own]
    chosen = lax.broadcasted_iota(jnp.int32, probs.shape, 1) == host
    gate = jnp.sum(jnp.where(chosen, probs, 0.0), axis=-1, keepdims=True)
    dmade_ref[...] = (gate * dy.astype(jnp.float32)).astype(jnp.bfloat16)
    dmade = dmade_ref[...]
    pltpu.make_async_copy(in_full, in_full, come_in).wait()
    pltpu.make_async_copy(out_full, out_full, come_out).wait()
    made = jnp.zeros(rows.shape, jnp.float32)
    drows = jnp.zeros(rows.shape, jnp.float32)
    step = units // 3
    for begin in range(0, units, step):
        at = slice(begin, begin + step)
        upre = dot(rows, in_full[:, at], ((1,), (0,)))
        square = upre * upre
        bent = jnp.tanh(0.7978845608028654 * (upre + 0.044715 * upre * square))
        hidden = (0.5 * upre * (1.0 + bent)).astype(jnp.bfloat16)
        slope = 0.5 * (1.0 + bent) + 0.5 * upre * (1.0 - bent * bent) * (
            0.7978845608028654 * (1.0 + 3.0 * 0.044715 * square)
        )
        dhidden = dot(dmade, out_full[at, :], ((1,), (1,)))
        du = (dhidden * slope).astype(jnp.bfloat16)
        hidden_ref[:, at] = hidden
        du_ref[:, at] = du
        made = made + dot(hidden, out_full[at, :], ((1,), (0,)))
        drows = drows + dot(du, in_full[:, at], ((1,), (1,)))
    mine_ref[0] = made[:own]
    mine_ref[1] = drows[:own]
    theirs_ref[0] = made[own:]
    theirs_ref[1] = drows[own:]


def settle_kernel(
    place_ref, mine_ref, got_ref, own_ref, probs_ref, router_ref, back_ref, router_part_ref
):
    width = own_ref.shape[1] // 2
    chips, places, _ = back_ref.shape
    made = (mine_ref[0] + got_ref[0]).astype(jnp.bfloat16)
    row = lax.broadcasted_iota(jnp.int32, (chips * 16, made.shape[0]), 0)
    column = lax.broadcasted_iota(jnp.int32, row.shape, 1)
    inside = (row & 15) < places
    spread = jnp.where(inside & (column == (row >> 4) * places + (row & 15)), 1.0, 0.0)
    spread = spread.astype(jnp.bfloat16)

    def padded(values):
        wide = dot(spread, values, ((1,), (0,))).reshape(chips, 16, width)
        return wide[:, :places].astype(jnp.bfloat16)

    back_ref[:, :, width:] = padded(made)
    drows = (mine_ref[1] + got_ref[1]).astype(jnp.bfloat16).astype(jnp.float32)
    probs = probs_ref[...]
    chosen = (lax.broadcasted_iota(jnp.int32, probs.shape, 1) == place_ref[1]).astype(jnp.float32)
    gate = jnp.sum(probs * chosen, axis=-1, keepdims=True)
    dgate = jnp.sum(
        own_ref[:, width:].astype(jnp.float32) * made.astype(jnp.float32),
        axis=-1,
        keepdims=True,
    )
    dlogits = probs * dgate * (chosen - gate)
    router_part_ref[...] = dot(
        dlogits, own_ref[:, :width].astype(jnp.float32), ((0,), (0,)), precision=HIGH
    )
    dn2 = drows + dot(dlogits, router_ref[...].astype(jnp.float32), ((1,), (0,)), precision=HIGH)
    back_ref[:, :, :width] = padded(dn2.astype(jnp.bfloat16))


def paired_body(
    tokens,
    attn_weight,
    gain_attn,
    gain_expert,
    bias_table,
    router_weight,
    expert_in,
    expert_out,
    routes,
    slots,
    buckets,
    cotangent,
):
    f32, bf16 = jnp.float32, jnp.bfloat16
    micro, _, seq_len, width = tokens.shape
    count = micro * seq_len
    heads = bias_table.shape[1]
    head_size = width // heads
    bucket_count = bias_table.shape[0]
    experts = lax.axis_size("expert")
    capacity = (5 * seq_len + 4 * experts - 1) // (4 * experts)
    places = micro * capacity
    hidden_half = expert_in.shape[2] // 2
    width_half = width // 2
    dp_at, expert_at = lax.axis_index("dp"), lax.axis_index("expert")
    core = expert_at % 2
    home = core == dp_at
    host = expert_at - core + dp_at
    gain_one, gain_two = gain_attn.astype(f32), gain_expert.astype(f32)

    across, first = [], []
    for dp in range(2):
        for e in range(experts):
            here = dp * experts + e
            if e % 2 == dp:
                first.append((here, dp * experts + (e ^ 1), (1 - dp) * experts + e))
            else:
                across.append((here, (1 - dp) * experts + (e ^ 1)))
                first.append((here, (1 - dp) * experts + e, dp * experts + (e ^ 1)))
    outward = [(here, there) for here, there, _ in first]
    homeward = [(here, there) for here, _, there in first]

    groups = [
        [dp * experts + 2 * pair + side for dp in range(2) for pair in range(experts // 2)]
        for side in range(2)
    ]

    def to_chips(tensor):
        return lax.all_to_all(
            tensor, BOTH, split_axis=0, concat_axis=0, tiled=True, axis_index_groups=groups
        )

    row_count = experts * places
    upstream_b = cotangent.reshape(count, width)
    def parts_of(local, axis):
        near = lax.dynamic_slice_in_dim(local, dp_at * hidden_half, hidden_half, axis)
        far = lax.dynamic_slice_in_dim(local, (1 - dp_at) * hidden_half, hidden_half, axis)
        return near, far

    in_near, in_far = parts_of(expert_in[0], 1)
    def halves(tensor):
        return (
            lax.dynamic_slice_in_dim(tensor, core * width_half, width_half, 1),
            lax.dynamic_slice_in_dim(tensor, (1 - core) * width_half, width_half, 1),
        )

    def whole(keep, got, axis):
        low = core == 0
        return jnp.concatenate(
            [jnp.where(low, keep, got), jnp.where(low, got, keep)], axis=axis
        )

    moved = []

    def prepare(table, ids, route_ids, slot_ids, near, far):
        made = call(
            functools.partial(prepare_kernel, places, capacity),
            16,
            (
                ((heads, count, count), f32),
                ((seq_len, count), jnp.int32),
                ((row_count, count), bf16),
                ((experts * 16, count), bf16),
            ),
            [],
            table, ids, route_ids, slot_ids,
        )
        in_arrived = lax.ppermute(near, BOTH, across)
        moved.append(lax.ppermute(far, BOTH, outward))
        return tuple(made) + (in_arrived,)

    pieces, ready, (out_near, out_far) = gather_rows(
        attn_weight.T,
        prepare,
        (bias_table.astype(f32), buckets, routes, slots, in_near, in_far),
        parts_of,
        expert_out[0],
    )
    square, tiled, dispatch, padded, in_arrived = ready
    pieces, in_far = lax.optimization_barrier((pieces, moved[0]))
    out_arrived = lax.ppermute(out_near, BOTH, across)
    place = jnp.stack(
        [core, host, home.astype(jnp.int32)] + [own_bit(order[0]) for order in RS_ORDERS]
    ).astype(jnp.int32)
    gain_one, gain_two = gain_one[None], gain_two[None]
    local = tokens.reshape(count, width)
    wt_qkv, wt_o, n1b, qkv, probs, mixed_b, resid, n2b, outgoing = call(
        attend_kernel,
        26,
        (
            ((12, 2, width // 8, width), bf16),
            ((4, 2, width // 8, width), bf16),
            ((count, width), bf16),
            ((3 * width, count), bf16),
            ((heads, count, count), f32),
            ((count, width), bf16),
            ((count, width), f32),
            ((count, width), bf16),
            ((experts, places, 2 * width), bf16),
        ),
        [
            pltpu.VMEM((width, count), f32),
            pltpu.VMEM((16, 2, width // 8, width), bf16),
            pltpu.SemaphoreType.DMA,
            pltpu.SemaphoreType.DMA,
            pltpu.SemaphoreType.DMA,
        ],
        place, local, *pieces, gain_one, gain_two, square, padded, upstream_b,
        plain_in=range(2, 8),
        plain_out=(0, 1),
    )
    wt_qkv, wt_o = wt_qkv.reshape(3 * width, width), wt_o.reshape(width, width)
    outgoing, out_arrived, out_far = lax.optimization_barrier((outgoing, out_arrived, out_far))
    own_rows = to_chips(outgoing).reshape(row_count, 2 * width)
    in_parts = (in_near, in_arrived, in_far)
    out_parts = (out_near, out_arrived, lax.ppermute(out_far, BOTH, outward))
    rows, hidden, du, dmade, mine, theirs, row_probs = call(
        expert_kernel,
        34,
        (
            ((2 * row_count, width), bf16),
            ((2 * row_count, hidden_half), bf16),
            ((2 * row_count, hidden_half), bf16),
            ((2 * row_count, width), bf16),
            ((2, row_count, width), f32),
            ((2, row_count, width), f32),
            ((row_count, experts), f32),
        ),
        [
            pltpu.VMEM((width, hidden_half), bf16),
            pltpu.VMEM((hidden_half, width), bf16),
            pltpu.SemaphoreType.DMA,
            pltpu.SemaphoreType.DMA,
        ],
        place, own_rows, flip(own_rows, 1), router_weight.T, *in_parts, *out_parts,
        plain_in=range(4, 10),
        free=(2,),
    )
    back_rows, router_part = call(
        settle_kernel,
        10,
        (
            ((experts, places, 2 * width), bf16),
            ((experts, width), f32),
        ),
        [],
        place, mine, flip(theirs, 1), own_rows, row_probs, router_weight.T,
        free=(2,),
    )
    in_other = dot(halves(rows)[1], du, ((0,), (0,))).astype(bf16)
    back_rows, rows, hidden, du, dmade = lax.optimization_barrier(
        (back_rows, rows, hidden, du, dmade)
    )
    home_rows = to_chips(back_rows).reshape(row_count, 2 * width)
    rows_keep, _ = halves(rows)
    dmade_keep, dmade_got = halves(dmade)

    in_homely = lax.ppermute(in_other, BOTH, homeward)
    in_mine = dot(rows_keep, du, ((0,), (0,)))
    out_other = dot(hidden, dmade_got, ((0,), (0,))).astype(bf16)
    out_homely = lax.ppermute(out_other, BOTH, homeward)
    out_mine = dot(hidden, dmade_keep, ((0,), (0,)))
    home_rows, in_homely, out_homely, in_leave, out_leave = lax.optimization_barrier(
        (home_rows, in_homely, out_homely, in_mine.astype(bf16), out_mine.astype(bf16))
    )
    in_arrived = lax.ppermute(in_leave, BOTH, across)

    dresid, gain_two_part, dqkv, fold, send, keep = call(
        attend_back_kernel,
        26,
        (
            ((count, width), f32),
            ((1, width), f32),
            ((3 * width, count), bf16),
            ((heads, count // 2, count), f32),
            ((2 * width, width), bf16),
            ((2 * width, count), bf16),
        ),
        [pltpu.VMEM((4 * width, count), bf16)],
        place, home_rows, dispatch, resid, upstream_b, gain_two, wt_o, qkv, probs, n1b, mixed_b,
    )
    got = flip(send, 1)
    small_rows = (width // 128) * experts + 16 + (heads + 7) // 8 * 8
    token_grad, small = call(
        functools.partial(token_back_kernel, bucket_count),
        26,
        (
            ((count, width), f32),
            ((small_rows, 128), f32),
        ),
        [],
        place, local, dqkv, wt_qkv, gain_one, dresid, fold, tiled, gain_two_part,
        router_part,
    )
    block = width // 8
    pieces = (width // 6, width // 3, width // 2)
    cut = call(
        split_kernel,
        30,
        tuple(((8, block, piece), bf16) for piece in pieces)
        + tuple(((8, block, piece), f32) for piece in pieces),
        [pltpu.VMEM((16, block, width), f32)],
        place, keep, n1b, mixed_b, got,
        free=(4,),
    )
    cut, out_leave = lax.optimization_barrier((cut, out_leave))
    out_arrived = lax.ppermute(out_leave, BOTH, across)
    attn_share, small, late = scatter_rows(
        cut[:3],
        cut[3:],
        small,
        (
            (),
            (in_arrived, in_mine, in_homely),
            (out_arrived, out_mine, out_homely),
            (home_rows, routes),
        ),
    )
    _, in_late, out_late, (home_rows, routes) = late
    route_ids = routes[:, 0]
    in_arrived, in_mine, in_homely = in_late
    out_arrived, out_mine, out_homely = out_late
    in_back = (in_mine, in_homely, in_arrived)
    out_back = (out_mine, out_homely, out_arrived)

    def settled(parts, axis):
        near, homely, arrived = parts
        mine = jnp.where(home, near, homely.astype(f32))
        other = jnp.where(home, homely.astype(f32), arrived.astype(f32))
        return whole(mine, other, axis)

    in_share, out_share = settled(in_back, 1), settled(out_back, 0)
    router_probs = jax.nn.softmax(dot(n2b, router_weight, ((1,), (0,))), axis=-1)
    picked = (route_ids.reshape(count, 1) == jnp.arange(experts)).astype(f32)
    gate = jnp.sum(router_probs * picked, axis=-1, keepdims=True)
    returned = dot(dispatch, home_rows[:, width:], ((0,), (0,)))
    output = (resid + gate * returned).astype(bf16)

    attn_share = attn_share.T
    routed = (width // 128) * experts
    return (
        output.reshape(tokens.shape),
        token_grad.reshape(tokens.shape),
        attn_share,
        small[routed : routed + width // 128].reshape(width),
        small[routed + 8 : routed + 8 + width // 128].reshape(width),
        small[routed + 16 : routed + 16 + heads, :bucket_count].T,
        jnp.transpose(small[:routed].reshape(-1, experts, 128), (0, 2, 1)).reshape(width, experts),
        in_share[None],
        out_share[None],
    )


def solution(mesh):
    paired = mesh.shape["dp"] == 2 and mesh.shape["expert"] == 16
    chosen = paired_body if paired else body
    placed = (
        P(None, ("dp", "expert"), None, None),
        P(None, ("dp", "expert")),
        P(),
        P(),
        P(),
        P(),
        P("expert", "dp", None),
        P("expert", None, "dp"),
        P(None, ("dp", "expert"), None),
        P(None, ("dp", "expert"), None),
        P(),
        P(None, ("dp", "expert"), None, None),
    )
    return jax.shard_map(
        chosen,
        mesh=mesh,
        in_specs=placed,
        out_specs=(
            P(None, ("dp", "expert"), None, None),
            P(None, ("dp", "expert"), None, None),
            P(None, ("dp", "expert")),
            P(),
            P(),
            P(),
            P(),
            P("expert", "dp", None),
            P("expert", None, "dp"),
        ),
        check_vma=False,
    )
```
